256 devices in a mesh: seq: 32 (over z, x), head: 8 (over y, core).
Axes of the slice: x: 4, y: 4, z: 8, core: 2. Of those that a mesh axis runs over, the one named last changes fastest.
Arguments:
- queries: bfloat16 [2, 32, 14336], P(None, 'seq', 'head'), may hold values from -150 to 150
- new_keys: bfloat16 [2, 32, 14336], P(None, 'seq', 'head'), may hold values from -6 to 6
- new_values: bfloat16 [2, 32, 14336], P(None, 'seq', 'head'), may hold values from -6 to 6
- cache_keys: bfloat16 [32768, 14336], P('seq', 'head'), may hold values from -6 to 6
- cache_values: bfloat16 [32768, 14336], P('seq', 'head'), may hold values from -6 to 6
- slopes: float32 [112], P('head'), may hold values from 1.8310548e-05 to 0.025
- seg_blocks: int32 [32], replicated, may hold values from 1 to 128, 192 in all
- request_row: int32 [32], replicated, may hold values from 0 to 31, each once
- out_weight: bfloat16 [14336, 14336], P('head', 'seq'), may hold values from -0.046875 to 0.046875
- residual: bfloat16 [2, 32, 14336], P(None, 'head', 'seq'), may hold values from -6 to 6
Outputs:
- mixed: bfloat16 [2, 32, 14336], P(None, 'head', 'seq')
The draws below stay inside these ranges and needn't reach their ends.
Inputs may be any that keep to these rules, and one draw needn't show every extreme that they name: `seg_blocks`: the requests are packed in order from block 0; 192 blocks are used and the rest of the cache is unused. `request_row`: each query row belongs to exactly one request.
All inputs are finite; a program needn't handle non-finite values.
Results may differ from the reference program's by a relative error of at most 0.006.
Values may be sent and summed in bfloat16 or wider, within the bound.
No kernel may reach another device: no remote copies, remote signals or barrier semaphores. Data moves between devices by JAX's collectives and lax.ppermute only.
A program may use at most 64 MiB of HBM per device.

```python
import math
import jax
import jax.numpy as jnp
import numpy as np
from jax import lax

HEADS = 112
HDIM = 128
D = 14336
BLK = 128
NBLK = 256
NCACHE = 32768
REQ = 32
MOST = 128
LIVE = 192


def draw_cache_keys(key, part):
    noise = jnp.clip(jax.random.normal(jax.random.fold_in(key, 11), (NCACHE, HEADS * HDIM), jnp.float32), -6.0, 6.0)
    return noise.astype(jnp.bfloat16)


def draw_queries(key, part):
    noise = jnp.clip(jax.random.normal(jax.random.fold_in(key, 13), (2, REQ, HEADS * HDIM), jnp.float32), -6.0, 6.0)
    return noise.astype(jnp.bfloat16)


def steps_of(key, extent, split, least, largest):
    gain, own = 1.0, jax.random.fold_in(key, 6)
    for dim, parts in split:
        steps = jnp.exp(jax.random.uniform(jax.random.fold_in(own, dim), (parts,), jnp.float32, least / len(split), largest / len(split)))
        gain = gain * jnp.repeat(steps, extent[dim] // parts).reshape([-1 if axis == dim else 1 for axis in range(len(extent))])
    return gain


def split_up(count, total, reach, lean):
    loads = [(1 << 20) // math.isqrt(rank ** lean) + 1 for rank in range(2, count + 1)]
    spare, holding = total - reach - (count - 1), [1] * (count - 1)
    while spare > 0:
        free = [i for i in range(count - 1) if holding[i] < reach]
        mass, left = sum([loads[i] for i in free]), spare
        for i in free:
            more = min(reach - holding[i], max(1, left * loads[i] // mass), spare)
            holding[i] = holding[i] + more
            spare = spare - more
    return np.array([reach] + holding)


def ragged(own_key, count, total, bound, slope):
    if count == 2:
        one = jax.random.randint(own_key, (), max(1, total - bound), min(bound, total - 1) + 1)
        return jnp.stack([one, total - one])
    lengths = jnp.asarray(split_up(count, total, bound, slope), jnp.int32)
    twos = (count - 1) // 2
    giver, receiver = lengths[1:1 + 2 * twos:2], lengths[2:2 + 2 * twos:2]
    slack = jnp.minimum(giver - 1, bound - receiver)
    moved = jax.random.randint(jax.random.fold_in(own_key, 1), (twos,), 0, 1 << 20) % (slack + 1)
    lengths = lengths.at[1:1 + 2 * twos:2].set(giver - moved).at[2:2 + 2 * twos:2].set(receiver + moved)
    return lengths[jax.random.permutation(jax.random.fold_in(own_key, 2), count)]


def centred(stream_key, dims, scale, bound, cuts=(), kind=jnp.bfloat16):
    drawn = scale * jax.random.normal(stream_key, dims, jnp.float32)
    if cuts:
        drawn = drawn * steps_of(stream_key, dims, cuts, -0.22, 0.18)
    return jnp.clip(drawn, -bound, bound).astype(kind)


def setup_inputs(seed: int = 0) -> dict:
    streams_of = jax.random.split(jax.random.key(seed), 11)
    queries = draw_queries(jax.random.fold_in(streams_of[10], 71), 0)
    new_keys = centred(streams_of[1], (2, REQ, HEADS * HDIM), 1.0, 6.0, ((1, 32), (2, 8)))
    new_values = centred(streams_of[2], (2, REQ, HEADS * HDIM), 1.0, 6.0, ((1, 32), (2, 8)))
    cache_keys = draw_cache_keys(jax.random.fold_in(streams_of[10], 71), 0)
    cache_values = centred(streams_of[4], (NCACHE, HEADS * HDIM), 1.0, 6.0, ((0, 32), (1, 8)))
    slopes = jnp.clip(jnp.exp(math.log(0.025) - 7.219154 * jax.random.uniform(streams_of[5], (HEADS,), jnp.float32) ** steps_of(streams_of[5], (HEADS,), ((0, 8),), -0.2, 0.2)), 1.831054760259576e-05, 0.025)
    seg_blocks = ragged(streams_of[6], REQ, LIVE, MOST, 2).astype(jnp.int32)
    request_row = jax.random.permutation(streams_of[7], REQ).astype(jnp.int32)
    out_weight = centred(streams_of[8], (HEADS * HDIM, D), (HEADS * HDIM) ** -0.5, 0.046875, ((0, 8), (1, 32)))
    residual = centred(streams_of[9], (2, REQ, D), 1.0, 6.0, ((1, 8), (2, 32)))
    return dict(queries=queries, new_keys=new_keys, new_values=new_values, cache_keys=cache_keys, cache_values=cache_values, slopes=slopes, seg_blocks=seg_blocks, request_row=request_row, out_weight=out_weight, residual=residual)


NEG = -1e+30

def self_terms(q, k, v, slopes, scale):
    q = q.astype(jnp.float32)
    k = k.astype(jnp.float32)
    v = v.astype(jnp.float32)
    first = lax.optimization_barrier(jnp.sum(q[0] * k[0], axis=-1)) * scale
    cross = lax.optimization_barrier(jnp.sum(q[1] * k[0], axis=-1)) * scale - slopes
    second = lax.optimization_barrier(jnp.sum(q[1] * k[1], axis=-1)) * scale
    upper = jnp.maximum(cross, second)
    e_cross = jnp.exp(cross - upper)
    e_second = jnp.exp(second - upper)
    top = jnp.stack([first, upper])
    total = jnp.stack([jnp.ones_like(first), e_cross + e_second])
    acc = jnp.stack([v[0], e_cross[..., None] * v[0] + e_second[..., None] * v[1]])
    return (top, total, acc)

def reference(queries, new_keys, new_values, cache_keys, cache_values, slopes, seg_blocks, request_row, out_weight, residual):
    scale = 1.0 / math.sqrt(HDIM)
    starts = jnp.cumsum(seg_blocks) - seg_blocks
    index = jnp.arange(NBLK, dtype=jnp.int32)
    hit = (index[:, None] >= starts[None, :]) & (index[:, None] < (starts + seg_blocks)[None, :])
    live = jnp.any(hit, axis=1)
    block_row = lax.optimization_barrier(jnp.sum(jnp.where(hit, request_row[None, :], 0), axis=1)).astype(jnp.int32)
    first = lax.optimization_barrier(jnp.sum(jnp.where(hit, starts[None, :], 0), axis=1)).astype(jnp.int32)
    length = lax.optimization_barrier(jnp.sum(jnp.where(hit, seg_blocks[None, :], 0), axis=1)).astype(jnp.int32)
    base = (length * BLK - (index - first) * BLK).astype(jnp.int32)
    block_query = jnp.take(queries, block_row, axis=1).reshape(2, NBLK, HEADS, HDIM).transpose(1, 0, 2, 3)
    keys = cache_keys.reshape(NBLK, BLK, HEADS, HDIM)
    values = cache_values.reshape(NBLK, BLK, HEADS, HDIM)

    def block_term(args):
        keys_b, values_b, query_b, base_b, live_b = args
        scores = jnp.einsum('shd,thd->sht', query_b.astype(jnp.float32), keys_b.astype(jnp.float32)) * scale
        dist = (base_b + jnp.arange(2, dtype=jnp.int32)[:, None] - jnp.arange(BLK, dtype=jnp.int32)[None, :]).astype(jnp.float32)
        scores = scores - slopes[None, :, None] * dist[:, None, :]
        top = lax.optimization_barrier(jnp.max(scores, axis=-1))
        probs = jnp.exp(scores - top[..., None])
        total = lax.optimization_barrier(jnp.sum(probs, axis=-1))
        weights = probs.astype(jnp.bfloat16)
        acc = jnp.einsum('sht,thd->shd', weights.astype(jnp.float32), values_b.astype(jnp.float32))
        top = jnp.where(live_b, top, NEG)
        total = jnp.where(live_b, total, 0.0)
        acc = jnp.where(live_b, acc, 0.0)
        return (top, total, acc)
    tops, totals, accs = lax.map(block_term, (keys, values, block_query, base, live))
    rowhot = (block_row[:, None] == jnp.arange(REQ, dtype=jnp.int32)[None, :]) & live[:, None]
    tab_top = lax.optimization_barrier(jnp.max(jnp.where(rowhot[:, :, None, None], tops[:, None], NEG), axis=0))
    ratio = jnp.exp(tops - jnp.take(tab_top, block_row, axis=0))
    tab_sum = jax.ops.segment_sum(ratio * totals, block_row, num_segments=REQ)
    tab_acc = jax.ops.segment_sum(ratio[..., None] * accs, block_row, num_segments=REQ)
    tab_top = tab_top.transpose(1, 0, 2)
    tab_sum = tab_sum.transpose(1, 0, 2)
    tab_acc = tab_acc.transpose(1, 0, 2, 3)
    own_top, own_sum, own_acc = self_terms(queries.reshape(2, REQ, HEADS, HDIM), new_keys.reshape(2, REQ, HEADS, HDIM), new_values.reshape(2, REQ, HEADS, HDIM), slopes, scale)
    top = jnp.maximum(tab_top, own_top)
    wa = jnp.exp(tab_top - top)
    wb = jnp.exp(own_top - top)
    total = tab_sum * wa + own_sum * wb
    acc = tab_acc * wa[..., None] + own_acc * wb[..., None]
    attended = (acc / total[..., None]).astype(jnp.bfloat16).reshape(2 * REQ, HEADS * HDIM)
    projected = jnp.dot(attended, out_weight, preferred_element_type=jnp.float32).reshape(2, REQ, D)
    return (residual.astype(jnp.float32) + projected).astype(jnp.bfloat16)
```

```python
import functools
import math

import jax
import jax.numpy as jnp
from jax import lax
from jax.experimental import pallas as pl
from jax.experimental.pallas import tpu as pltpu
from jax.sharding import PartitionSpec as P

BLK = 128
NEG = -1e30
STEPS = 2
GROUP = 16
STATS = 128
VMEM_LIMIT = 48 * 1024 * 1024


def iota(shape, dim):
    return lax.broadcasted_iota(jnp.int32, shape, dim)


def head_mask(width, hdim):
    return iota((GROUP, width), 1) // hdim == iota((GROUP, width), 0)


def by_step(x, mask):
    rows = [
        jnp.sum(jnp.where(mask, x[s * GROUP : (s + 1) * GROUP], 0.0), axis=0, keepdims=True)
        for s in range(STEPS)
    ]
    return jnp.concatenate(rows, axis=0)


def in_bf16_parts(x, parts):
    out = []
    for _ in range(parts):
        part = x.astype(jnp.bfloat16).astype(jnp.float32)
        out.append(part)
        x = x - part
    return out


def attend_kernel(blocks, hdim, meta, slopes, query, keys, values, out, kbuf, vbuf, ksem, vsem):
    width = kbuf.shape[1]
    scale = 1.0 / math.sqrt(hdim)
    kcopy, vcopy = [], []
    for b in range(blocks):
        rows = pl.ds(b * BLK, BLK)
        kcopy.append(pltpu.make_async_copy(keys.at[rows], kbuf.at[rows], ksem.at[b]))
        vcopy.append(pltpu.make_async_copy(values.at[rows], vbuf.at[rows], vsem.at[b]))
    for copy in kcopy:
        copy.start()
    for copy in vcopy:
        copy.start()

    mask = head_mask(width, hdim)
    lane = iota((STEPS, STATS), 1)
    empty = jnp.concatenate(
        [jnp.zeros((STEPS, width), jnp.float32), jnp.where(lane < GROUP, NEG, 0.0)], axis=1
    ).astype(out.dtype)
    for r in range(out.shape[0]):
        out[r] = empty

    shape = (STEPS * GROUP, BLK)
    when = iota(shape, 0) // GROUP - iota(shape, 1)
    slope = slopes[...]
    scores = []
    for b in range(blocks):
        q = query[meta[0, b]].astype(jnp.float32)
        spread = jnp.concatenate(
            [jnp.where(mask, q[s : s + 1], 0.0) for s in range(STEPS)], axis=0
        ).astype(jnp.bfloat16)
        kcopy[b].wait()
        raw = lax.dot_general(
            spread,
            kbuf[b * BLK : (b + 1) * BLK],
            (((1,), (1,)), ((), ())),
            preferred_element_type=jnp.float32,
        )
        dist = (when + meta[1, b]).astype(jnp.float32)
        scores.append(raw * scale - slope * dist)

    joined = [meta[3, b] == 1 for b in range(blocks)]
    tops = [jnp.max(x, axis=1, keepdims=True) for x in scores]
    for b in range(1, blocks):
        tops[b] = jnp.where(joined[b], jnp.maximum(tops[b], tops[b - 1]), tops[b])
    for b in range(blocks - 2, -1, -1):
        tops[b] = jnp.where(joined[b + 1], tops[b + 1], tops[b])
    probs = [jnp.exp(x - top) for x, top in zip(scores, tops)]
    totals = [jnp.sum(p, axis=1, keepdims=True) for p in probs]
    for b in range(1, blocks):
        totals[b] = totals[b] + jnp.where(joined[b], totals[b - 1], 0.0)

    offset = iota((STEPS * GROUP, STATS), 1) - iota((STEPS * GROUP, STATS), 0) % GROUP
    every = jnp.full((GROUP, STATS), True)
    acc = None
    for b in range(blocks):
        vcopy[b].wait()
        full = jnp.dot(
            probs[b].astype(jnp.bfloat16),
            vbuf[b * BLK : (b + 1) * BLK],
            preferred_element_type=jnp.float32,
        )
        mine = by_step(full, mask)
        acc = mine if acc is None else mine + jnp.where(joined[b], acc, 0.0)
        stats = jnp.zeros((STEPS * GROUP, STATS), jnp.float32)
        for k, part in enumerate(in_bf16_parts(tops[b], 3) + in_bf16_parts(totals[b], 2)):
            stats = jnp.where(offset == k * GROUP, part, stats)
        row = jnp.concatenate([acc, by_step(stats, every)], axis=1).astype(out.dtype)

        @pl.when(meta[2, b] == 1)
        def _():
            out[meta[0, b]] = row


def own_kernel(heads, hdim, query, key, value, slopes, stats, acc):
    scale = 1.0 / math.sqrt(hdim)
    q = query[...].astype(jnp.float32)
    k = key[...].astype(jnp.float32)
    v = value[...].astype(jnp.float32)
    q0, q1 = q[0:1], q[1:2]
    k0, k1 = k[0:1], k[1:2]
    v0, v1 = v[0:1], v[1:2]
    lane = iota((1, STATS), 1)
    tops = [jnp.zeros((1, STATS), jnp.float32) for _ in range(STEPS)]
    sums = [jnp.zeros((1, STATS), jnp.float32) for _ in range(STEPS)]
    rows = [[], []]
    products = jnp.concatenate([q0 * k0, q1 * k0, q1 * k1], axis=0)
    for h in range(heads):
        at = slice(h * hdim, (h + 1) * hdim)
        dots = jnp.sum(products[:, at], axis=1, keepdims=True) * scale
        first = dots[0:1]
        cross = dots[1:2] - slopes[h : h + 1]
        second = dots[2:3]
        upper = jnp.maximum(cross, second)
        e_cross = jnp.exp(cross - upper)
        e_second = jnp.exp(second - upper)
        tops[0] = jnp.where(lane == h, first, tops[0])
        tops[1] = jnp.where(lane == h, upper, tops[1])
        sums[0] = jnp.where(lane == h + GROUP, 1.0, sums[0])
        sums[1] = jnp.where(lane == h + GROUP, e_cross + e_second, sums[1])
        rows[0].append(v0[:, at])
        rows[1].append(e_cross * v0[:, at] + e_second * v1[:, at])
    stats[...] = jnp.concatenate([tops[0] + sums[0], tops[1] + sums[1]], axis=0)
    acc[...] = jnp.concatenate([jnp.concatenate(r, axis=1) for r in rows], axis=0)


def left(x, lanes):
    return pltpu.roll(x, x.shape[1] - lanes, 1) if lanes else x


def join_kernel(heads, hdim, parts, own_stats, own_acc, out):
    width = heads * hdim
    count = parts.shape[0]
    stats = parts[:, width : width + STATS].astype(jnp.float32)
    top = (stats + left(stats, GROUP)) + left(stats, 2 * GROUP)
    total = left(stats, 3 * GROUP) + left(stats, 4 * GROUP)
    step = iota((count, STATS), 0) % STEPS
    lane = iota((count, STATS), 1)
    real = lane < heads
    top = jnp.where(real, top, NEG)
    total = jnp.where(real, total, 0.0)
    own = own_stats[...]
    own_real = iota(own.shape, 1) < heads
    own_top = jnp.where(own_real, own, 0.0)
    own_total = jnp.where(own_real, left(own, GROUP), 1.0)
    highest = [
        jnp.maximum(
            jnp.max(jnp.where(step == s, top, NEG), axis=0, keepdims=True), own_top[s : s + 1]
        )
        for s in range(STEPS)
    ]
    weight = jnp.exp(top - jnp.where(step == 0, highest[0], highest[1]))
    weight = jnp.where(real, weight, 0.0)
    own_weight = jnp.exp(own_top - jnp.concatenate(highest, axis=0))
    weighted = weight * total
    sums = [
        jnp.sum(jnp.where(step == s, weighted, 0.0), axis=0, keepdims=True) for s in range(STEPS)
    ]
    inverse = 1.0 / (jnp.concatenate(sums, axis=0) + own_weight * own_total)
    own_weight = own_weight * inverse
    weight = weight * jnp.where(step == 0, inverse[0:1], inverse[1:2])
    placed = jnp.where(step == 0, weight, 0.0) + pltpu.roll(
        jnp.where(step == 1, weight, 0.0), GROUP, 1
    )
    high, low = in_bf16_parts(placed, 2)
    both = high + pltpu.roll(low, STEPS * GROUP, 1)
    both = both.T[: 2 * STEPS * GROUP].astype(jnp.bfloat16)
    full = jnp.dot(both, parts[:, :width], preferred_element_type=jnp.float32)
    full = full[: STEPS * GROUP] + full[STEPS * GROUP :]
    acc = by_step(full, head_mask(width, hdim))
    mine = own_acc[...]
    mine = jnp.concatenate(
        [mine[:, h * hdim : (h + 1) * hdim] * own_weight[:, h : h + 1] for h in range(heads)],
        axis=1,
    )
    attended = (acc + mine).astype(out.dtype)
    for r in range(out.shape[0]):
        out[r] = attended


def copies_kernel(x, out):
    for r in range(out.shape[0]):
        out[r] = x[...]


def on_device(kernel, out_shape, in_spaces, **more):
    return pl.pallas_call(
        kernel,
        out_shape=out_shape,
        in_specs=[pl.BlockSpec(memory_space=m) for m in in_spaces],
        compiler_params=pltpu.CompilerParams(vmem_limit_bytes=VMEM_LIMIT),
        **more,
    )


def block_table(seg_blocks, request_row, blocks):
    requests = seg_blocks.shape[0]
    order = jnp.arange(requests, dtype=jnp.int32)
    starts = jnp.sum(jnp.where(order[None, :] < order[:, None], seg_blocks[None, :], 0), axis=1)
    index = lax.axis_index("seq") * blocks + jnp.arange(blocks, dtype=jnp.int32)
    ends = starts + seg_blocks
    hit = (index[:, None] >= starts[None, :]) & (index[:, None] < ends[None, :])
    pick = lambda x: jnp.sum(jnp.where(hit, x[None, :], 0), axis=1)
    row = pick(request_row)
    base = pick(ends) * BLK - index * BLK
    live = jnp.any(hit, axis=1)
    before = hit & (index[:, None] > starts[None, :]) & (jnp.arange(blocks)[:, None] > 0)
    joined = jnp.any(before, axis=1)
    return jnp.stack([row, base, live.astype(jnp.int32), joined.astype(jnp.int32)])


def body(
    queries,
    new_keys,
    new_values,
    cache_keys,
    cache_values,
    slopes,
    seg_blocks,
    request_row,
    out_weight,
    residual,
):
    heads = slopes.shape[0]
    width = queries.shape[2]
    hdim = width // heads
    peers = lax.axis_size("seq")
    groups = lax.axis_size("head")
    blocks = cache_keys.shape[0] // BLK
    vmem, smem, anywhere = pltpu.VMEM, pltpu.SMEM, pl.ANY
    own_query = queries.reshape(STEPS, width)

    copies = on_device(
        copies_kernel, jax.ShapeDtypeStruct((peers, STEPS, width), jnp.bfloat16), [vmem]
    )(own_query)
    everyone = lax.all_to_all(copies, "seq", 0, 0, tiled=True)

    table = block_table(seg_blocks, request_row, blocks)
    column = jnp.tile(jnp.pad(slopes, (0, GROUP - heads)), STEPS)[:, None]
    own_stats, own_acc = on_device(
        functools.partial(own_kernel, heads, hdim),
        (
            jax.ShapeDtypeStruct((STEPS, STATS), jnp.float32),
            jax.ShapeDtypeStruct((STEPS, width), jnp.float32),
        ),
        [vmem] * 4,
    )(own_query, new_keys.reshape(STEPS, width), new_values.reshape(STEPS, width), column)

    partials = on_device(
        functools.partial(attend_kernel, blocks, hdim),
        jax.ShapeDtypeStruct((peers, STEPS, width + STATS), jnp.bfloat16),
        [smem, vmem, vmem, anywhere, anywhere],
        scratch_shapes=[
            pltpu.VMEM(cache_keys.shape, jnp.bfloat16),
            pltpu.VMEM(cache_values.shape, jnp.bfloat16),
            pltpu.SemaphoreType.DMA((blocks,)),
            pltpu.SemaphoreType.DMA((blocks,)),
        ],
    )(table, column, everyone, cache_keys, cache_values)
    arrived = lax.all_to_all(partials, "seq", 0, 0, tiled=True)

    attended = on_device(
        functools.partial(join_kernel, heads, hdim),
        jax.ShapeDtypeStruct((peers, STEPS, width), jnp.bfloat16),
        [vmem] * 3,
    )(arrived.reshape(peers * STEPS, width + STATS), own_stats, own_acc)
    rows = lax.all_to_all(attended, "seq", 0, 0, tiled=True).reshape(peers * STEPS, width)

    projected = jnp.dot(rows, out_weight, preferred_element_type=jnp.float32)
    projected = projected.astype(jnp.bfloat16).reshape(groups, -1, out_weight.shape[1])
    shares = lax.all_to_all(projected, "head", 0, 0, tiled=True)
    summed = jnp.sum(shares.astype(jnp.float32), axis=0)
    summed = summed.reshape(-1, STEPS, out_weight.shape[1]).transpose(1, 0, 2)
    return (residual.astype(jnp.float32) + summed).astype(jnp.bfloat16)


def solution(mesh):
    in_specs = (
        P(None, "seq", "head"),
        P(None, "seq", "head"),
        P(None, "seq", "head"),
        P("seq", "head"),
        P("seq", "head"),
        P("head"),
        P(),
        P(),
        P("head", "seq"),
        P(None, "head", "seq"),
    )
    out_specs = P(None, "head", "seq")
    return jax.shard_map(body, mesh=mesh, in_specs=in_specs, out_specs=out_specs, check_vma=False)
```

```python
import functools
import math

import jax
import jax.numpy as jnp
from jax import lax
from jax.experimental import pallas as pl
from jax.experimental.pallas import tpu as pltpu
from jax.sharding import PartitionSpec as P

BLK = 128
NEG = -1e30
STEPS = 2
GROUP = 16
STATS = 128
MIB = 1024 * 1024


def iota(shape, dim):
    return lax.broadcasted_iota(jnp.int32, shape, dim)


def head_mask(width, hdim):
    return iota((GROUP, width), 1) // hdim == iota((GROUP, width), 0)


def by_step(x, mask):
    rows = [
        jnp.sum(jnp.where(mask, x[s * GROUP : (s + 1) * GROUP], 0.0), axis=0, keepdims=True)
        for s in range(STEPS)
    ]
    return jnp.concatenate(rows, axis=0)


def in_bf16_parts(x, parts):
    out = []
    for _ in range(parts):
        part = x.astype(jnp.bfloat16).astype(jnp.float32)
        out.append(part)
        x = x - part
    return out


def left(x, lanes):
    return pltpu.roll(x, x.shape[1] - lanes, 1) if lanes else x


def attend_kernel(
    blocks, hdim, meta, slopes, query, own_stats, keys, values, out, kbuf, vbuf, sems
):
    width = keys.shape[1]
    per = STEPS * GROUP
    packs = BLK // per
    scale = 1.0 / math.sqrt(hdim)
    copies = []
    for i, (src, dst) in enumerate(((keys, kbuf), (values, vbuf))):
        for b in range(blocks):
            rows = pl.ds(b * BLK, BLK)
            copies.append(pltpu.make_async_copy(src.at[rows], dst.at[rows], sems.at[i, b]))
    for copy in copies:
        copy.start()
    mask = head_mask(width, hdim)
    lane = iota((STEPS, STATS), 1)
    empty = jnp.concatenate(
        [jnp.zeros((STEPS, width), jnp.float32), jnp.where(lane < GROUP, NEG, 0.0)], axis=1
    ).astype(out.dtype)
    for r in range(out.shape[0]):
        out[r] = empty

    raw = []
    for g in range(blocks // packs):
        spread = []
        for b in range(g * packs, (g + 1) * packs):
            q = query[meta[0, b]].astype(jnp.float32)
            for s in range(STEPS):
                spread.append(jnp.where(mask, q[s : s + 1], 0.0).astype(jnp.bfloat16))
        for b in range(g * packs, (g + 1) * packs):
            copies[b].wait()
        raw.append(
            lax.dot_general(
                kbuf[g * packs * BLK : (g + 1) * packs * BLK],
                jnp.concatenate(spread, axis=0),
                (((1,), (1,)), ((), ())),
                preferred_element_type=jnp.float32,
            )
        )

    pack = iota((BLK, BLK), 1) // per
    when = (iota((BLK, BLK), 1) % per) // GROUP - iota((BLK, BLK), 0)
    slope = slopes[...]
    joined = [meta[3, b] == 1 for b in range(blocks)]
    scores = []
    tops = []
    for g in range(blocks // packs):
        for k in range(packs):
            b = g * packs + k
            tile = raw[g][k * BLK : (k + 1) * BLK]
            base = meta[1, b]
            x = tile if k == 0 else jnp.where(pack == k, tile, x)
            dist = when + base if k == 0 else jnp.where(pack == k, when + base, dist)
        x = x * scale - slope * dist.astype(jnp.float32)
        scores.append(x)
        top = jnp.max(x, axis=0, keepdims=True)
        tops += [left(top, k * per) for k in range(packs)]
    for b in range(1, blocks):
        tops[b] = jnp.where(joined[b], jnp.maximum(tops[b], tops[b - 1]), tops[b])
    for b in range(blocks - 2, -1, -1):
        tops[b] = jnp.where(joined[b + 1], tops[b + 1], tops[b])

    place = iota((1, BLK), 1) // per
    totals = []
    weights = []
    for g in range(blocks // packs):
        top = tops[g * packs]
        for k in range(1, packs):
            top = jnp.where(place == k, pltpu.roll(tops[g * packs + k], k * per, 1), top)
        probs = jnp.exp(scores[g] - top)
        total = jnp.sum(probs, axis=0, keepdims=True)
        totals += [left(total, k * per) for k in range(packs)]
        weights.append(probs.T.astype(jnp.bfloat16))
    for b in range(1, blocks):
        totals[b] = totals[b] + jnp.where(joined[b], totals[b - 1], 0.0)

    parts = in_bf16_parts(jnp.concatenate(tops, axis=0), 3)
    parts += in_bf16_parts(jnp.concatenate(totals, axis=0), 2)
    field = iota((blocks, STATS), 1) // GROUP
    stats = []
    for s in range(STEPS):
        row = jnp.zeros((blocks, STATS), jnp.float32)
        for k, part in enumerate(parts):
            row = jnp.where(field == k, left(part, (s - k) * GROUP % STATS), row)
        stats.append(row)

    rows = []
    acc = None
    for b in range(blocks):
        k = b % packs
        copies[blocks + b].wait()
        full = jnp.dot(
            weights[b // packs][k * per : (k + 1) * per],
            vbuf[b * BLK : (b + 1) * BLK],
            preferred_element_type=jnp.float32,
        )
        mine = by_step(full, mask)
        acc = mine if acc is None else mine + jnp.where(joined[b], acc, 0.0)
        tail = jnp.concatenate([x[b : b + 1] for x in stats], axis=0)
        row = jnp.concatenate([acc, tail], axis=1).astype(out.dtype)
        rows.append(jnp.where(meta[2, b] == 1, row, empty))
    for b in range(blocks):
        out[meta[0, b]] = rows[b]


def own_kernel(heads, hdim, query, key, value, slopes, stats, acc):
    scale = 1.0 / math.sqrt(hdim)
    q = query[...].astype(jnp.float32)
    k = key[...].astype(jnp.float32)
    v = value[...].astype(jnp.float32)
    q0, q1 = q[0:1], q[1:2]
    k0, k1 = k[0:1], k[1:2]
    v0, v1 = v[0:1], v[1:2]
    lane = iota((1, STATS), 1)
    tops = [jnp.zeros((1, STATS), jnp.float32) for _ in range(STEPS)]
    sums = [jnp.zeros((1, STATS), jnp.float32) for _ in range(STEPS)]
    rows = [[], []]
    products = jnp.concatenate([q0 * k0, q1 * k0, q1 * k1], axis=0)
    for h in range(heads):
        at = slice(h * hdim, (h + 1) * hdim)
        dots = jnp.sum(products[:, at], axis=1, keepdims=True) * scale
        first = dots[0:1]
        cross = dots[1:2] - slopes[:, h : h + 1]
        second = dots[2:3]
        upper = jnp.maximum(cross, second)
        e_cross = jnp.exp(cross - upper)
        e_second = jnp.exp(second - upper)
        tops[0] = jnp.where(lane == h, first, tops[0])
        tops[1] = jnp.where(lane == h, upper, tops[1])
        sums[0] = jnp.where(lane == h + GROUP, 1.0, sums[0])
        sums[1] = jnp.where(lane == h + GROUP, e_cross + e_second, sums[1])
        rows[0].append(v0[:, at])
        rows[1].append(e_cross * v0[:, at] + e_second * v1[:, at])
    stats[...] = jnp.concatenate([tops[0] + sums[0], tops[1] + sums[1]], axis=0)
    acc[...] = jnp.concatenate([jnp.concatenate(r, axis=1) for r in rows], axis=0)


def join_kernel(heads, hdim, parts, own_stats, own_acc, out):
    width = heads * hdim
    count = parts.shape[0]
    stats = parts[:, width : width + STATS].astype(jnp.float32)
    top = (stats + left(stats, GROUP)) + left(stats, 2 * GROUP)
    total = left(stats, 3 * GROUP) + left(stats, 4 * GROUP)
    step = iota((count, STATS), 0) % STEPS
    lane = iota((count, STATS), 1)
    real = lane < heads
    top = jnp.where(real, top, NEG)
    total = jnp.where(real, total, 0.0)
    own = own_stats[...]
    own_real = iota(own.shape, 1) < heads
    own_top = jnp.where(own_real, own, 0.0)
    own_total = jnp.where(own_real, left(own, GROUP), 1.0)
    highest = [
        jnp.maximum(
            jnp.max(jnp.where(step == s, top, NEG), axis=0, keepdims=True), own_top[s : s + 1]
        )
        for s in range(STEPS)
    ]
    weight = jnp.exp(top - jnp.where(step == 0, highest[0], highest[1]))
    weight = jnp.where(real, weight, 0.0)
    own_weight = jnp.exp(own_top - jnp.concatenate(highest, axis=0))
    weighted = weight * total
    sums = [
        jnp.sum(jnp.where(step == s, weighted, 0.0), axis=0, keepdims=True) for s in range(STEPS)
    ]
    inverse = 1.0 / (jnp.concatenate(sums, axis=0) + own_weight * own_total)
    own_weight = own_weight * inverse
    weight = weight * jnp.where(step == 0, inverse[0:1], inverse[1:2])
    placed = jnp.where(step == 0, weight, 0.0) + pltpu.roll(
        jnp.where(step == 1, weight, 0.0), GROUP, 1
    )
    high, low = in_bf16_parts(placed, 2)
    both = high + pltpu.roll(low, STEPS * GROUP, 1)
    both = both.T[: 2 * STEPS * GROUP].astype(jnp.bfloat16)
    full = jnp.dot(both, parts[:, :width], preferred_element_type=jnp.float32)
    full = full[: STEPS * GROUP] + full[STEPS * GROUP :]
    acc = by_step(full, head_mask(width, hdim))
    mine = own_acc[...]
    mine = jnp.concatenate(
        [mine[:, h * hdim : (h + 1) * hdim] * own_weight[:, h : h + 1] for h in range(heads)],
        axis=1,
    )
    attended = (acc + mine).astype(out.dtype)
    for r in range(out.shape[0]):
        out[r] = attended


def project_kernel(rows, weight, mine, theirs):
    full = lax.dot_general(
        rows[...], weight[...], (((1,), (1,)), ((), ())), preferred_element_type=jnp.float32
    )
    first = lax.axis_index("head") % 2 == 0
    chips, size = mine.shape[0], mine.shape[1]
    for c in range(chips):
        a = full[2 * c * size : (2 * c + 1) * size]
        b = full[(2 * c + 1) * size : (2 * c + 2) * size]
        mine[c] = jnp.where(first, a, b)
        theirs[c] = jnp.where(first, b, a).astype(theirs.dtype)


def pair_kernel(mine, got, total, *rest):
    shares, both = rest[:-1], rest[-1]
    chips = mine.shape[0]
    chip = lax.axis_index("head") // 2
    for c in range(chips):
        both[c] = mine[c] + got[c].astype(jnp.float32)
    total[...] = both[chip]
    for hop, share in enumerate(shares, 1):
        share[...] = both[lax.rem(chip + hop, chips)].astype(share.dtype)


def finish_kernel(total, *rest):
    shares, residual, out = rest[:-2], rest[-2], rest[-1]
    x = total[...]
    for share in shares:
        x = x + share[...].astype(jnp.float32)
    for s in range(STEPS):
        rows = [x[r : r + 1] for r in range(s, x.shape[0], STEPS)]
        y = residual[s].astype(jnp.float32) + jnp.concatenate(rows, axis=0)
        out[s] = y.astype(out.dtype)


def copies_kernel(x, out):
    for r in range(out.shape[0]):
        out[r] = x[...]


def on_device(kernel, out_shape, in_spaces, limit, **more):
    return pl.pallas_call(
        kernel,
        out_shape=out_shape,
        in_specs=[pl.BlockSpec(memory_space=m) for m in in_spaces],
        compiler_params=pltpu.CompilerParams(vmem_limit_bytes=limit * MIB),
        **more,
    )


def block_table(seg_blocks, request_row, blocks):
    requests = seg_blocks.shape[0]
    order = jnp.arange(requests, dtype=jnp.int32)
    starts = jnp.sum(jnp.where(order[None, :] < order[:, None], seg_blocks[None, :], 0), axis=1)
    index = lax.axis_index("seq") * blocks + jnp.arange(blocks, dtype=jnp.int32)
    ends = starts + seg_blocks
    hit = (index[:, None] >= starts[None, :]) & (index[:, None] < ends[None, :])
    pick = lambda x: jnp.sum(jnp.where(hit, x[None, :], 0), axis=1)
    row = pick(request_row)
    base = pick(ends) * BLK - index * BLK
    live = jnp.any(hit, axis=1)
    before = hit & (index[:, None] > starts[None, :]) & (jnp.arange(blocks)[:, None] > 0)
    joined = jnp.any(before, axis=1)
    return jnp.stack([row, base, live.astype(jnp.int32), joined.astype(jnp.int32)])


def project_and_sum(rows, out_weight, residual, groups):
    chips = groups // 2
    size, columns = rows.shape[0] // groups, out_weight.shape[1]
    each = (chips, size, columns)
    mine, theirs = on_device(
        project_kernel,
        (jax.ShapeDtypeStruct(each, jnp.float32), jax.ShapeDtypeStruct(each, jnp.bfloat16)),
        [pltpu.VMEM] * 2,
        16,
    )(rows, out_weight.T)
    got = lax.ppermute(theirs, "head", [(i, i ^ 1) for i in range(groups)])
    share = jax.ShapeDtypeStruct((size, columns), jnp.bfloat16)
    total, *shares = on_device(
        pair_kernel,
        (jax.ShapeDtypeStruct((size, columns), jnp.float32), *[share] * (chips - 1)),
        [pltpu.VMEM] * 2,
        16,
        scratch_shapes=[pltpu.VMEM(each, jnp.float32)],
    )(mine, got)
    arrived = [
        lax.ppermute(x, "head", [(i, (i + 2 * hop) % groups) for i in range(groups)])
        for hop, x in enumerate(shares, 1)
    ]
    return on_device(
        finish_kernel,
        jax.ShapeDtypeStruct(residual.shape, residual.dtype),
        [pltpu.VMEM] * (chips + 1),
        16,
    )(total, *arrived, residual)


def body(
    queries,
    new_keys,
    new_values,
    cache_keys,
    cache_values,
    slopes,
    seg_blocks,
    request_row,
    out_weight,
    residual,
):
    heads = slopes.shape[0]
    width = queries.shape[2]
    hdim = width // heads
    peers = lax.axis_size("seq")
    groups = lax.axis_size("head")
    blocks = cache_keys.shape[0] // BLK
    vmem, smem, anywhere = pltpu.VMEM, pltpu.SMEM, pl.ANY
    own_query = queries.reshape(STEPS, width)

    copies = on_device(
        copies_kernel, jax.ShapeDtypeStruct((peers, STEPS, width), jnp.bfloat16), [vmem], 4
    )(own_query)
    everyone = lax.all_to_all(copies, "seq", 0, 0, tiled=True)

    table = block_table(seg_blocks, request_row, blocks)
    lanes = jnp.tile(jnp.pad(slopes, (0, GROUP - heads)), BLK // GROUP)[None]
    own_stats, own_acc = on_device(
        functools.partial(own_kernel, heads, hdim),
        (
            jax.ShapeDtypeStruct((STEPS, STATS), jnp.float32),
            jax.ShapeDtypeStruct((STEPS, width), jnp.float32),
        ),
        [vmem] * 4,
        4,
    )(own_query, new_keys.reshape(STEPS, width), new_values.reshape(STEPS, width), lanes)

    partials = on_device(
        functools.partial(attend_kernel, blocks, hdim),
        jax.ShapeDtypeStruct((peers, STEPS, width + STATS), jnp.bfloat16),
        [smem, vmem, vmem, pl.ANY, pltpu.HBM, pltpu.HBM],
        32,
        scratch_shapes=[
            pltpu.VMEM(cache_keys.shape, jnp.bfloat16),
            pltpu.VMEM(cache_values.shape, jnp.bfloat16),
            pltpu.SemaphoreType.DMA((2, blocks)),
        ],
    )(
        table,
        lanes,
        everyone,
        own_stats,
        pltpu.with_memory_space_constraint(cache_keys, pltpu.HBM),
        pltpu.with_memory_space_constraint(cache_values, pltpu.HBM),
    )
    arrived = lax.all_to_all(partials, "seq", 0, 0, tiled=True)

    attended = on_device(
        functools.partial(join_kernel, heads, hdim),
        jax.ShapeDtypeStruct((peers, STEPS, width), jnp.bfloat16),
        [vmem] * 3,
        16,
    )(arrived.reshape(peers * STEPS, width + STATS), own_stats, own_acc)
    rows = lax.all_to_all(attended, "seq", 0, 0, tiled=True).reshape(peers * STEPS, width)

    return project_and_sum(rows, out_weight, residual, groups)


def solution(mesh):
    in_specs = (
        P(None, "seq", "head"),
        P(None, "seq", "head"),
        P(None, "seq", "head"),
        P("seq", "head"),
        P("seq", "head"),
        P("head"),
        P(),
        P(),
        P("head", "seq"),
        P(None, "head", "seq"),
    )
    out_specs = P(None, "head", "seq")
    return jax.shard_map(body, mesh=mesh, in_specs=in_specs, out_specs=out_specs, check_vma=False)
```

```python
import functools
import math

import jax
import jax.numpy as jnp
from jax import lax
from jax.experimental import pallas as pl
from jax.experimental.pallas import tpu as pltpu
from jax.sharding import PartitionSpec as P

BLK = 128
NEG = -1e30
STEPS = 2
GROUP = 16
STATS = 128
MIB = 1024 * 1024


def iota(shape, dim):
    return lax.broadcasted_iota(jnp.int32, shape, dim)


def head_mask(width, hdim):
    return iota((GROUP, width), 1) // hdim == iota((GROUP, width), 0)


def by_step(x, mask):
    rows = [
        jnp.sum(jnp.where(mask, x[s * GROUP : (s + 1) * GROUP], 0.0), axis=0, keepdims=True)
        for s in range(STEPS)
    ]
    return jnp.concatenate(rows, axis=0)


def in_bf16_parts(x, parts):
    out = []
    for _ in range(parts):
        part = x.astype(jnp.bfloat16).astype(jnp.float32)
        out.append(part)
        x = x - part
    return out


def left(x, lanes):
    return pltpu.roll(x, x.shape[1] - lanes, 1) if lanes else x


def attend_kernel(
    blocks,
    heads,
    seg_blocks,
    request_row,
    slopes,
    query,
    own_query,
    new_key,
    new_value,
    keys,
    values,
    out,
    own_stats,
    own_acc,
    kbuf,
    vbuf,
    sems,
):
    width = keys.shape[1]
    hdim = width // heads
    per = STEPS * GROUP
    packs = BLK // per
    scale = 1.0 / math.sqrt(hdim)
    copies = []
    for i, (src, dst) in enumerate(((keys, kbuf), (values, vbuf))):
        for b in range(blocks):
            rows = pl.ds(b * BLK, BLK)
            copies.append(pltpu.make_async_copy(src.at[rows], dst.at[rows], sems.at[i, b]))
    for copy in copies:
        copy.start()
    table = block_table(blocks, seg_blocks, request_row)
    mask = head_mask(width, hdim)
    lane = iota((STEPS, STATS), 1)
    empty = jnp.concatenate(
        [jnp.zeros((STEPS, width), jnp.float32), jnp.where(lane < GROUP, NEG, 0.0)], axis=1
    ).astype(out.dtype)
    for r in range(out.shape[0]):
        out[r] = empty

    own_stats[...], own_acc[...] = own_terms(heads, hdim, own_query, new_key, new_value, slopes)

    raw = []
    for g in range(blocks // packs):
        spread = []
        for b in range(g * packs, (g + 1) * packs):
            q = query[table[b][0]].astype(jnp.float32)
            for s in range(STEPS):
                spread.append(jnp.where(mask, q[s : s + 1], 0.0).astype(jnp.bfloat16))
        for b in range(g * packs, (g + 1) * packs):
            copies[b].wait()
        raw.append(
            lax.dot_general(
                kbuf[g * packs * BLK : (g + 1) * packs * BLK],
                jnp.concatenate(spread, axis=0),
                (((1,), (1,)), ((), ())),
                preferred_element_type=jnp.float32,
            )
        )

    pack = iota((BLK, BLK), 1) // per
    when = (iota((BLK, BLK), 1) % per) // GROUP - iota((BLK, BLK), 0)
    slope = jnp.zeros((1, BLK), jnp.float32)
    for h in range(heads):
        slope = jnp.where(iota((1, BLK), 1) % GROUP == h, slopes[h], slope)
    joined = [table[b][3] for b in range(blocks)]
    scores = []
    tops = []
    for g in range(blocks // packs):
        for k in range(packs):
            b = g * packs + k
            tile = raw[g][k * BLK : (k + 1) * BLK]
            base = table[b][1]
            x = tile if k == 0 else jnp.where(pack == k, tile, x)
            dist = when + base if k == 0 else jnp.where(pack == k, when + base, dist)
        x = x * scale - slope * dist.astype(jnp.float32)
        scores.append(x)
        top = jnp.max(x, axis=0, keepdims=True)
        tops += [left(top, k * per) for k in range(packs)]
    for b in range(1, blocks):
        tops[b] = jnp.where(joined[b], jnp.maximum(tops[b], tops[b - 1]), tops[b])
    for b in range(blocks - 2, -1, -1):
        tops[b] = jnp.where(joined[b + 1], tops[b + 1], tops[b])

    place = iota((1, BLK), 1) // per
    totals = []
    weights = []
    for g in range(blocks // packs):
        top = tops[g * packs]
        for k in range(1, packs):
            top = jnp.where(place == k, pltpu.roll(tops[g * packs + k], k * per, 1), top)
        probs = jnp.exp(scores[g] - top)
        total = jnp.sum(probs, axis=0, keepdims=True)
        totals += [left(total, k * per) for k in range(packs)]
        weights.append(probs.T.astype(jnp.bfloat16))
    for b in range(1, blocks):
        totals[b] = totals[b] + jnp.where(joined[b], totals[b - 1], 0.0)

    parts = in_bf16_parts(jnp.concatenate(tops, axis=0), 3)
    parts += in_bf16_parts(jnp.concatenate(totals, axis=0), 2)
    field = iota((blocks, STATS), 1) // GROUP
    stats = []
    for s in range(STEPS):
        row = jnp.zeros((blocks, STATS), jnp.float32)
        for k, part in enumerate(parts):
            row = jnp.where(field == k, left(part, (s - k) * GROUP % STATS), row)
        stats.append(row)

    rows = []
    acc = None
    for b in range(blocks):
        k = b % packs
        copies[blocks + b].wait()
        full = jnp.dot(
            weights[b // packs][k * per : (k + 1) * per],
            vbuf[b * BLK : (b + 1) * BLK],
            preferred_element_type=jnp.float32,
        )
        mine = by_step(full, mask)
        acc = mine if acc is None else mine + jnp.where(joined[b], acc, 0.0)
        tail = jnp.concatenate([x[b : b + 1] for x in stats], axis=0)
        row = jnp.concatenate([acc, tail], axis=1).astype(out.dtype)
        rows.append(jnp.where(table[b][2], row, empty))
    for b in range(blocks):
        out[table[b][0]] = rows[b]


def own_terms(heads, hdim, query, key, value, slopes):
    scale = 1.0 / math.sqrt(hdim)
    q = query[...].astype(jnp.float32)
    k = key[...].astype(jnp.float32)
    v = value[...].astype(jnp.float32)
    q0, q1 = q[0:1], q[1:2]
    k0, k1 = k[0:1], k[1:2]
    v0, v1 = v[0:1], v[1:2]
    lane = iota((1, STATS), 1)
    tops = [jnp.zeros((1, STATS), jnp.float32) for _ in range(STEPS)]
    sums = [jnp.zeros((1, STATS), jnp.float32) for _ in range(STEPS)]
    rows = [[], []]
    products = jnp.concatenate([q0 * k0, q1 * k0, q1 * k1], axis=0)
    for h in range(heads):
        at = slice(h * hdim, (h + 1) * hdim)
        dots = jnp.sum(products[:, at], axis=1, keepdims=True) * scale
        first = dots[0:1]
        cross = dots[1:2] - slopes[h]
        second = dots[2:3]
        upper = jnp.maximum(cross, second)
        e_cross = jnp.exp(cross - upper)
        e_second = jnp.exp(second - upper)
        tops[0] = jnp.where(lane == h, first, tops[0])
        tops[1] = jnp.where(lane == h, upper, tops[1])
        sums[0] = jnp.where(lane == h + GROUP, 1.0, sums[0])
        sums[1] = jnp.where(lane == h + GROUP, e_cross + e_second, sums[1])
        rows[0].append(v0[:, at])
        rows[1].append(e_cross * v0[:, at] + e_second * v1[:, at])
    stats = jnp.concatenate([tops[0] + sums[0], tops[1] + sums[1]], axis=0)
    return stats, jnp.concatenate([jnp.concatenate(r, axis=1) for r in rows], axis=0)


def block_table(blocks, seg_blocks, request_row):
    requests = seg_blocks.shape[0]
    index = lax.axis_index("seq") * blocks

    def skip(i, carry):
        request, end, total = carry
        total = total + seg_blocks[i]
        passed = total <= index
        return request + passed.astype(jnp.int32), jnp.where(passed, total, end), total

    zero = jnp.int32(0)
    request, end, _ = lax.fori_loop(0, requests, skip, (zero, zero, zero))
    last = requests - 1
    end = end + seg_blocks[jnp.minimum(request, last)]
    table = []
    for b in range(blocks):
        joined = jnp.bool_(False)
        if b:
            joined = index + b < end
            request = jnp.where(joined, request, request + 1)
            end = jnp.where(joined, end, end + seg_blocks[jnp.minimum(request, last)])
        live = request <= last
        row = request_row[jnp.minimum(request, last)]
        table.append((row, (end - index - b) * BLK, live, joined & live))
    return table


def join_kernel(heads, hdim, parts, own_stats, own_acc, out):
    width = heads * hdim
    count = parts.shape[0]
    stats = parts[:, width : width + STATS].astype(jnp.float32)
    top = (stats + left(stats, GROUP)) + left(stats, 2 * GROUP)
    total = left(stats, 3 * GROUP) + left(stats, 4 * GROUP)
    step = iota((count, STATS), 0) % STEPS
    lane = iota((count, STATS), 1)
    real = lane < heads
    top = jnp.where(real, top, NEG)
    total = jnp.where(real, total, 0.0)
    own = own_stats[...]
    own_real = iota(own.shape, 1) < heads
    own_top = jnp.where(own_real, own, 0.0)
    own_total = jnp.where(own_real, left(own, GROUP), 1.0)
    highest = [
        jnp.maximum(
            jnp.max(jnp.where(step == s, top, NEG), axis=0, keepdims=True), own_top[s : s + 1]
        )
        for s in range(STEPS)
    ]
    weight = jnp.exp(top - jnp.where(step == 0, highest[0], highest[1]))
    weight = jnp.where(real, weight, 0.0)
    own_weight = jnp.exp(own_top - jnp.concatenate(highest, axis=0))
    weighted = weight * total
    sums = [
        jnp.sum(jnp.where(step == s, weighted, 0.0), axis=0, keepdims=True) for s in range(STEPS)
    ]
    inverse = 1.0 / (jnp.concatenate(sums, axis=0) + own_weight * own_total)
    own_weight = own_weight * inverse
    weight = weight * jnp.where(step == 0, inverse[0:1], inverse[1:2])
    placed = jnp.where(step == 0, weight, 0.0) + pltpu.roll(
        jnp.where(step == 1, weight, 0.0), GROUP, 1
    )
    high, low = in_bf16_parts(placed, 2)
    both = high + pltpu.roll(low, STEPS * GROUP, 1)
    both = both.T[: 2 * STEPS * GROUP].astype(jnp.bfloat16)
    full = jnp.dot(both, parts[:, :width], preferred_element_type=jnp.float32)
    full = full[: STEPS * GROUP] + full[STEPS * GROUP :]
    acc = by_step(full, head_mask(width, hdim))
    mine = own_acc[...]
    mine = jnp.concatenate(
        [mine[:, h * hdim : (h + 1) * hdim] * own_weight[:, h : h + 1] for h in range(heads)],
        axis=1,
    )
    attended = (acc + mine).astype(out.dtype)
    for r in range(out.shape[0]):
        out[r] = attended


def project_kernel(rows, weight, mine, theirs):
    full = lax.dot_general(
        rows[...], weight[...], (((1,), (1,)), ((), ())), preferred_element_type=jnp.float32
    )
    first = lax.axis_index("head") % 2 == 0
    chips, size = mine.shape[0], mine.shape[1]
    for c in range(chips):
        a = full[2 * c * size : (2 * c + 1) * size]
        b = full[(2 * c + 1) * size : (2 * c + 2) * size]
        mine[c] = jnp.where(first, a, b)
        theirs[c] = jnp.where(first, b, a).astype(theirs.dtype)


def pair_kernel(mine, got, total, *rest):
    shares, both = rest[:-1], rest[-1]
    chips = mine.shape[0]
    chip = lax.axis_index("head") // 2
    for c in range(chips):
        both[c] = mine[c] + got[c].astype(jnp.float32)
    total[...] = both[chip]
    for hop, share in enumerate(shares, 1):
        share[...] = both[lax.rem(chip + hop, chips)].astype(share.dtype)


def finish_kernel(total, *rest):
    shares, residual, out = rest[:-2], rest[-2], rest[-1]
    x = total[...]
    for share in shares:
        x = x + share[...].astype(jnp.float32)
    for s in range(STEPS):
        rows = [x[r : r + 1] for r in range(s, x.shape[0], STEPS)]
        y = residual[s].astype(jnp.float32) + jnp.concatenate(rows, axis=0)
        out[s] = y.astype(out.dtype)


def copies_kernel(x, out, sems):
    copies = [pltpu.make_async_copy(x, out.at[r], sems.at[r]) for r in range(out.shape[0])]
    for copy in copies:
        copy.start()
    for copy in copies:
        copy.wait()


def in_hbm(x):
    return pltpu.with_memory_space_constraint(x, pltpu.HBM)


def on_device(kernel, out_shape, in_spaces, limit, **more):
    return pl.pallas_call(
        kernel,
        out_shape=out_shape,
        in_specs=[pl.BlockSpec(memory_space=m) for m in in_spaces],
        compiler_params=pltpu.CompilerParams(vmem_limit_bytes=limit * MIB),
        **more,
    )


def project_and_sum(rows, out_weight, residual, groups):
    chips = groups // 2
    size, columns = rows.shape[0] // groups, out_weight.shape[1]
    each = (chips, size, columns)
    mine, theirs = on_device(
        project_kernel,
        (jax.ShapeDtypeStruct(each, jnp.float32), jax.ShapeDtypeStruct(each, jnp.bfloat16)),
        [pltpu.VMEM] * 2,
        16,
    )(rows, out_weight.T)
    got = lax.ppermute(theirs, "head", [(i, i ^ 1) for i in range(groups)])
    share = jax.ShapeDtypeStruct((size, columns), jnp.bfloat16)
    total, *shares = on_device(
        pair_kernel,
        (jax.ShapeDtypeStruct((size, columns), jnp.float32), *[share] * (chips - 1)),
        [pltpu.VMEM] * 2,
        16,
        scratch_shapes=[pltpu.VMEM(each, jnp.float32)],
    )(mine, got)
    arrived = [
        lax.ppermute(x, "head", [(i, (i + 2 * hop) % groups) for i in range(groups)])
        for hop, x in enumerate(shares, 1)
    ]
    return on_device(
        finish_kernel,
        jax.ShapeDtypeStruct(residual.shape, residual.dtype),
        [pltpu.VMEM] * (chips + 1),
        16,
    )(total, *arrived, residual)


def body(
    queries,
    new_keys,
    new_values,
    cache_keys,
    cache_values,
    slopes,
    seg_blocks,
    request_row,
    out_weight,
    residual,
):
    heads = slopes.shape[0]
    width = queries.shape[2]
    hdim = width // heads
    peers = lax.axis_size("seq")
    groups = lax.axis_size("head")
    blocks = cache_keys.shape[0] // BLK
    vmem, smem = pltpu.VMEM, pltpu.SMEM
    own_query = queries.reshape(STEPS, width)

    copies = on_device(
        copies_kernel,
        jax.ShapeDtypeStruct((peers, STEPS, width), jnp.bfloat16),
        [pltpu.HBM],
        4,
        scratch_shapes=[pltpu.SemaphoreType.DMA((peers,))],
    )(in_hbm(own_query))
    everyone = lax.all_to_all(copies, "seq", 0, 0, tiled=True)

    partials, own_stats, own_acc = on_device(
        functools.partial(attend_kernel, blocks, heads),
        (
            jax.ShapeDtypeStruct((peers, STEPS, width + STATS), jnp.bfloat16),
            jax.ShapeDtypeStruct((STEPS, STATS), jnp.float32),
            jax.ShapeDtypeStruct((STEPS, width), jnp.float32),
        ),
        [smem] * 3 + [vmem] * 4 + [pltpu.HBM] * 2,
        32,
        scratch_shapes=[
            pltpu.VMEM(cache_keys.shape, jnp.bfloat16),
            pltpu.VMEM(cache_values.shape, jnp.bfloat16),
            pltpu.SemaphoreType.DMA((2, blocks)),
        ],
    )(
        in_hbm(seg_blocks),
        in_hbm(request_row),
        in_hbm(slopes),
        everyone,
        in_hbm(own_query),
        in_hbm(new_keys.reshape(STEPS, width)),
        in_hbm(new_values.reshape(STEPS, width)),
        in_hbm(cache_keys),
        in_hbm(cache_values),
    )
    arrived = lax.all_to_all(partials, "seq", 0, 0, tiled=True)

    attended = on_device(
        functools.partial(join_kernel, heads, hdim),
        jax.ShapeDtypeStruct((peers, STEPS, width), jnp.bfloat16),
        [vmem] * 3,
        16,
    )(arrived.reshape(peers * STEPS, width + STATS), own_stats, own_acc)
    rows = lax.all_to_all(attended, "seq", 0, 0, tiled=True).reshape(peers * STEPS, width)

    return project_and_sum(rows, out_weight, residual, groups)


def solution(mesh):
    in_specs = (
        P(None, "seq", "head"),
        P(None, "seq", "head"),
        P(None, "seq", "head"),
        P("seq", "head"),
        P("seq", "head"),
        P("head"),
        P(),
        P(),
        P("head", "seq"),
        P(None, "head", "seq"),
    )
    out_specs = P(None, "head", "seq")
    return jax.shard_map(body, mesh=mesh, in_specs=in_specs, out_specs=out_specs, check_vma=False)
```

```python
import functools
import math

import jax
import jax.numpy as jnp
from jax import lax
from jax.experimental import pallas as pl
from jax.experimental.pallas import tpu as pltpu
from jax.sharding import PartitionSpec as P

BLK = 128
NEG = -1e30
STEPS = 2
GROUP = 16
STATS = 128
MIB = 1024 * 1024


def iota(shape, dim):
    return lax.broadcasted_iota(jnp.int32, shape, dim)


def head_mask(width, hdim):
    return iota((GROUP, width), 1) // hdim == iota((GROUP, width), 0)


def by_step(x, mask):
    rows = [
        jnp.sum(jnp.where(mask, x[s * GROUP : (s + 1) * GROUP], 0.0), axis=0, keepdims=True)
        for s in range(STEPS)
    ]
    return jnp.concatenate(rows, axis=0)


def in_bf16_parts(x, parts):
    out = []
    for _ in range(parts):
        part = x.astype(jnp.bfloat16).astype(jnp.float32)
        out.append(part)
        x = x - part
    return out


def left(x, lanes):
    return pltpu.roll(x, x.shape[1] - lanes, 1) if lanes else x


def stage_kernel(keys, out, sems):
    copies = []
    for b in range(sems.shape[0]):
        rows = pl.ds(b * BLK, BLK)
        copies.append(pltpu.make_async_copy(keys.at[rows], out.at[rows], sems.at[b]))
    for copy in copies:
        copy.start()
    for copy in copies:
        copy.wait()


def attend_kernel(
    blocks, hdim, meta, slopes, query, own_stats, staged, keys, values, out, kbuf, vbuf, sems
):
    width = keys.shape[1]
    per = STEPS * GROUP
    packs = BLK // per
    scale = 1.0 / math.sqrt(hdim)
    ready = staged.shape[0] // BLK
    key_copies = {}
    for b in range(ready, blocks):
        rows = pl.ds((b - ready) * BLK, BLK)
        copy = pltpu.make_async_copy(keys.at[pl.ds(b * BLK, BLK)], kbuf.at[rows], sems.at[0, b])
        key_copies[b] = copy
    value_copies = []
    for b in range(blocks):
        rows = pl.ds(b * BLK, BLK)
        value_copies.append(pltpu.make_async_copy(values.at[rows], vbuf.at[rows], sems.at[1, b]))
    for copy in (*key_copies.values(), *value_copies):
        copy.start()
    mask = head_mask(width, hdim)
    lane = iota((STEPS, STATS), 1)
    empty = jnp.concatenate(
        [jnp.zeros((STEPS, width), jnp.float32), jnp.where(lane < GROUP, NEG, 0.0)], axis=1
    ).astype(out.dtype)
    for r in range(out.shape[0]):
        out[r] = empty

    raw = []
    for g in range(blocks // packs):
        spread = []
        for b in range(g * packs, (g + 1) * packs):
            q = query[meta[0, b]].astype(jnp.float32)
            for s in range(STEPS):
                spread.append(jnp.where(mask, q[s : s + 1], 0.0).astype(jnp.bfloat16))
        spread = jnp.concatenate(spread, axis=0)
        first, last = g * packs, (g + 1) * packs
        split = min(max(first, ready), last)
        pieces = []
        if split > first:
            pieces.append(staged[first * BLK : split * BLK])
        if last > split:
            for b in range(split, last):
                key_copies[b].wait()
            pieces.append(kbuf[(split - ready) * BLK : (last - ready) * BLK])
        tiles = [
            lax.dot_general(
                piece, spread, (((1,), (1,)), ((), ())), preferred_element_type=jnp.float32
            )
            for piece in pieces
        ]
        raw.append(tiles[0] if len(tiles) == 1 else jnp.concatenate(tiles, axis=0))

    pack = iota((BLK, BLK), 1) // per
    when = (iota((BLK, BLK), 1) % per) // GROUP - iota((BLK, BLK), 0)
    slope = slopes[...]
    joined = [meta[3, b] == 1 for b in range(blocks)]
    scores = []
    tops = []
    for g in range(blocks // packs):
        for k in range(packs):
            b = g * packs + k
            tile = raw[g][k * BLK : (k + 1) * BLK]
            base = meta[1, b]
            x = tile if k == 0 else jnp.where(pack == k, tile, x)
            dist = when + base if k == 0 else jnp.where(pack == k, when + base, dist)
        x = x * scale - slope * dist.astype(jnp.float32)
        scores.append(x)
        top = jnp.max(x, axis=0, keepdims=True)
        tops += [left(top, k * per) for k in range(packs)]
    for b in range(1, blocks):
        tops[b] = jnp.where(joined[b], jnp.maximum(tops[b], tops[b - 1]), tops[b])
    for b in range(blocks - 2, -1, -1):
        tops[b] = jnp.where(joined[b + 1], tops[b + 1], tops[b])

    place = iota((1, BLK), 1) // per
    totals = []
    weights = []
    for g in range(blocks // packs):
        top = tops[g * packs]
        for k in range(1, packs):
            top = jnp.where(place == k, pltpu.roll(tops[g * packs + k], k * per, 1), top)
        probs = jnp.exp(scores[g] - top)
        total = jnp.sum(probs, axis=0, keepdims=True)
        totals += [left(total, k * per) for k in range(packs)]
        weights.append(probs.T.astype(jnp.bfloat16))
    for b in range(1, blocks):
        totals[b] = totals[b] + jnp.where(joined[b], totals[b - 1], 0.0)

    parts = in_bf16_parts(jnp.concatenate(tops, axis=0), 3)
    parts += in_bf16_parts(jnp.concatenate(totals, axis=0), 2)
    field = iota((blocks, STATS), 1) // GROUP
    stats = []
    for s in range(STEPS):
        row = jnp.zeros((blocks, STATS), jnp.float32)
        for k, part in enumerate(parts):
            row = jnp.where(field == k, left(part, (s - k) * GROUP % STATS), row)
        stats.append(row)

    rows = []
    acc = None
    for b in range(blocks):
        k = b % packs
        value_copies[b].wait()
        full = jnp.dot(
            weights[b // packs][k * per : (k + 1) * per],
            vbuf[b * BLK : (b + 1) * BLK],
            preferred_element_type=jnp.float32,
        )
        mine = by_step(full, mask)
        acc = mine if acc is None else mine + jnp.where(joined[b], acc, 0.0)
        tail = jnp.concatenate([x[b : b + 1] for x in stats], axis=0)
        row = jnp.concatenate([acc, tail], axis=1).astype(out.dtype)
        rows.append(jnp.where(meta[2, b] == 1, row, empty))
    for b in range(blocks):
        out[meta[0, b]] = rows[b]


def own_kernel(heads, hdim, query, key, value, slopes, stats, acc):
    scale = 1.0 / math.sqrt(hdim)
    q = query[...].astype(jnp.float32)
    k = key[...].astype(jnp.float32)
    v = value[...].astype(jnp.float32)
    q0, q1 = q[0:1], q[1:2]
    k0, k1 = k[0:1], k[1:2]
    v0, v1 = v[0:1], v[1:2]
    lane = iota((1, STATS), 1)
    tops = [jnp.zeros((1, STATS), jnp.float32) for _ in range(STEPS)]
    sums = [jnp.zeros((1, STATS), jnp.float32) for _ in range(STEPS)]
    rows = [[], []]
    products = jnp.concatenate([q0 * k0, q1 * k0, q1 * k1], axis=0)
    for h in range(heads):
        at = slice(h * hdim, (h + 1) * hdim)
        dots = jnp.sum(products[:, at], axis=1, keepdims=True) * scale
        first = dots[0:1]
        cross = dots[1:2] - slopes[:, h : h + 1]
        second = dots[2:3]
        upper = jnp.maximum(cross, second)
        e_cross = jnp.exp(cross - upper)
        e_second = jnp.exp(second - upper)
        tops[0] = jnp.where(lane == h, first, tops[0])
        tops[1] = jnp.where(lane == h, upper, tops[1])
        sums[0] = jnp.where(lane == h + GROUP, 1.0, sums[0])
        sums[1] = jnp.where(lane == h + GROUP, e_cross + e_second, sums[1])
        rows[0].append(v0[:, at])
        rows[1].append(e_cross * v0[:, at] + e_second * v1[:, at])
    stats[...] = jnp.concatenate([tops[0] + sums[0], tops[1] + sums[1]], axis=0)
    acc[...] = jnp.concatenate([jnp.concatenate(r, axis=1) for r in rows], axis=0)


def join_kernel(heads, hdim, parts, own_stats, own_acc, out):
    width = heads * hdim
    count = parts.shape[0]
    stats = parts[:, width : width + STATS].astype(jnp.float32)
    top = (stats + left(stats, GROUP)) + left(stats, 2 * GROUP)
    total = left(stats, 3 * GROUP) + left(stats, 4 * GROUP)
    step = iota((count, STATS), 0) % STEPS
    lane = iota((count, STATS), 1)
    real = lane < heads
    top = jnp.where(real, top, NEG)
    total = jnp.where(real, total, 0.0)
    own = own_stats[...]
    own_real = iota(own.shape, 1) < heads
    own_top = jnp.where(own_real, own, 0.0)
    own_total = jnp.where(own_real, left(own, GROUP), 1.0)
    highest = [
        jnp.maximum(
            jnp.max(jnp.where(step == s, top, NEG), axis=0, keepdims=True), own_top[s : s + 1]
        )
        for s in range(STEPS)
    ]
    weight = jnp.exp(top - jnp.where(step == 0, highest[0], highest[1]))
    weight = jnp.where(real, weight, 0.0)
    own_weight = jnp.exp(own_top - jnp.concatenate(highest, axis=0))
    weighted = weight * total
    sums = [
        jnp.sum(jnp.where(step == s, weighted, 0.0), axis=0, keepdims=True) for s in range(STEPS)
    ]
    inverse = 1.0 / (jnp.concatenate(sums, axis=0) + own_weight * own_total)
    own_weight = own_weight * inverse
    weight = weight * jnp.where(step == 0, inverse[0:1], inverse[1:2])
    placed = jnp.where(step == 0, weight, 0.0) + pltpu.roll(
        jnp.where(step == 1, weight, 0.0), GROUP, 1
    )
    high, low = in_bf16_parts(placed, 2)
    both = high + pltpu.roll(low, STEPS * GROUP, 1)
    both = both.T[: 2 * STEPS * GROUP].astype(jnp.bfloat16)
    full = jnp.dot(both, parts[:, :width], preferred_element_type=jnp.float32)
    full = full[: STEPS * GROUP] + full[STEPS * GROUP :]
    acc = by_step(full, head_mask(width, hdim))
    mine = own_acc[...]
    mine = jnp.concatenate(
        [mine[:, h * hdim : (h + 1) * hdim] * own_weight[:, h : h + 1] for h in range(heads)],
        axis=1,
    )
    attended = (acc + mine).astype(out.dtype)
    for r in range(out.shape[0]):
        out[r] = attended


def project_kernel(rows, weight, mine, theirs):
    full = lax.dot_general(
        rows[...], weight[...], (((1,), (1,)), ((), ())), preferred_element_type=jnp.float32
    )
    first = lax.axis_index("head") % 2 == 0
    chips, size = mine.shape[0], mine.shape[1]
    for c in range(chips):
        a = full[2 * c * size : (2 * c + 1) * size]
        b = full[(2 * c + 1) * size : (2 * c + 2) * size]
        mine[c] = jnp.where(first, a, b)
        theirs[c] = jnp.where(first, b, a).astype(theirs.dtype)


def pair_kernel(mine, got, total, *rest):
    shares, both = rest[:-1], rest[-1]
    chips = mine.shape[0]
    chip = lax.axis_index("head") // 2
    for c in range(chips):
        both[c] = mine[c] + got[c].astype(jnp.float32)
    total[...] = both[chip]
    for hop, share in enumerate(shares, 1):
        share[...] = both[lax.rem(chip + hop, chips)].astype(share.dtype)


def finish_kernel(total, *rest):
    shares, residual, out = rest[:-2], rest[-2], rest[-1]
    x = total[...]
    for share in shares:
        x = x + share[...].astype(jnp.float32)
    for s in range(STEPS):
        rows = [x[r : r + 1] for r in range(s, x.shape[0], STEPS)]
        y = residual[s].astype(jnp.float32) + jnp.concatenate(rows, axis=0)
        out[s] = y.astype(out.dtype)


def copies_kernel(x, out):
    for r in range(out.shape[0]):
        out[r] = x[...]


def in_hbm(x):
    return pltpu.with_memory_space_constraint(x, pltpu.HBM)


def on_device(kernel, out_shape, in_spaces, limit, **more):
    return pl.pallas_call(
        kernel,
        out_shape=out_shape,
        in_specs=[pl.BlockSpec(memory_space=m) for m in in_spaces],
        compiler_params=pltpu.CompilerParams(vmem_limit_bytes=limit * MIB),
        **more,
    )


def block_table(seg_blocks, request_row, blocks):
    requests = seg_blocks.shape[0]
    order = jnp.arange(requests, dtype=jnp.int32)
    starts = jnp.sum(jnp.where(order[None, :] < order[:, None], seg_blocks[None, :], 0), axis=1)
    index = lax.axis_index("seq") * blocks + jnp.arange(blocks, dtype=jnp.int32)
    ends = starts + seg_blocks
    hit = (index[:, None] >= starts[None, :]) & (index[:, None] < ends[None, :])
    pick = lambda x: jnp.sum(jnp.where(hit, x[None, :], 0), axis=1)
    row = pick(request_row)
    base = pick(ends) * BLK - index * BLK
    live = jnp.any(hit, axis=1)
    before = hit & (index[:, None] > starts[None, :]) & (jnp.arange(blocks)[:, None] > 0)
    joined = jnp.any(before, axis=1)
    return jnp.stack([row, base, live.astype(jnp.int32), joined.astype(jnp.int32)])


def project_and_sum(rows, out_weight, residual, groups):
    chips = groups // 2
    size, columns = rows.shape[0] // groups, out_weight.shape[1]
    each = (chips, size, columns)
    mine, theirs = on_device(
        project_kernel,
        (jax.ShapeDtypeStruct(each, jnp.float32), jax.ShapeDtypeStruct(each, jnp.bfloat16)),
        [pltpu.VMEM] * 2,
        16,
    )(rows, out_weight.T)
    got = lax.ppermute(theirs, "head", [(i, i ^ 1) for i in range(groups)])
    share = jax.ShapeDtypeStruct((size, columns), jnp.bfloat16)
    total, *shares = on_device(
        pair_kernel,
        (jax.ShapeDtypeStruct((size, columns), jnp.float32), *[share] * (chips - 1)),
        [pltpu.VMEM] * 2,
        16,
        scratch_shapes=[pltpu.VMEM(each, jnp.float32)],
    )(mine, got)
    arrived = [
        lax.ppermute(x, "head", [(i, (i + 2 * hop) % groups) for i in range(groups)])
        for hop, x in enumerate(shares, 1)
    ]
    return on_device(
        finish_kernel,
        jax.ShapeDtypeStruct(residual.shape, residual.dtype),
        [pltpu.VMEM] * (chips + 1),
        16,
    )(total, *arrived, residual)


def body(
    queries,
    new_keys,
    new_values,
    cache_keys,
    cache_values,
    slopes,
    seg_blocks,
    request_row,
    out_weight,
    residual,
):
    heads = slopes.shape[0]
    width = queries.shape[2]
    hdim = width // heads
    peers = lax.axis_size("seq")
    groups = lax.axis_size("head")
    blocks = cache_keys.shape[0] // BLK
    vmem, smem, anywhere = pltpu.VMEM, pltpu.SMEM, pl.ANY
    own_query = queries.reshape(STEPS, width)

    copies = on_device(
        copies_kernel, jax.ShapeDtypeStruct((peers, STEPS, width), jnp.bfloat16), [vmem], 4
    )(own_query)
    everyone = lax.all_to_all(copies, "seq", 0, 0, tiled=True)

    table = block_table(seg_blocks, request_row, blocks)
    lanes = jnp.tile(jnp.pad(slopes, (0, GROUP - heads)), BLK // GROUP)[None]
    own_stats, own_acc = on_device(
        functools.partial(own_kernel, heads, hdim),
        (
            jax.ShapeDtypeStruct((STEPS, STATS), jnp.float32),
            jax.ShapeDtypeStruct((STEPS, width), jnp.float32),
        ),
        [vmem] * 4,
        4,
    )(own_query, new_keys.reshape(STEPS, width), new_values.reshape(STEPS, width), lanes)

    ready = blocks - 1
    staged = on_device(
        stage_kernel,
        pltpu.VMEM((ready * BLK, width), jnp.bfloat16),
        [pltpu.HBM],
        2,
        out_specs=pl.BlockSpec(memory_space=pl.ANY),
        scratch_shapes=[pltpu.SemaphoreType.DMA((ready,))],
        cost_estimate=pl.CostEstimate(
            flops=0, bytes_accessed=4 * ready * BLK * width, transcendentals=0
        ),
    )(in_hbm(cache_keys))
    partials = on_device(
        functools.partial(attend_kernel, blocks, hdim),
        jax.ShapeDtypeStruct((peers, STEPS, width + STATS), jnp.bfloat16),
        [smem, vmem, vmem, pl.ANY, vmem, pltpu.HBM, pltpu.HBM],
        32,
        scratch_shapes=[
            pltpu.VMEM(((blocks - ready) * BLK, width), jnp.bfloat16),
            pltpu.VMEM(cache_values.shape, jnp.bfloat16),
            pltpu.SemaphoreType.DMA((2, blocks)),
        ],
    )(table, lanes, everyone, own_stats, staged, in_hbm(cache_keys), in_hbm(cache_values))
    arrived = lax.all_to_all(partials, "seq", 0, 0, tiled=True)

    attended = on_device(
        functools.partial(join_kernel, heads, hdim),
        jax.ShapeDtypeStruct((peers, STEPS, width), jnp.bfloat16),
        [vmem] * 3,
        16,
    )(arrived.reshape(peers * STEPS, width + STATS), own_stats, own_acc)
    rows = lax.all_to_all(attended, "seq", 0, 0, tiled=True).reshape(peers * STEPS, width)

    return project_and_sum(rows, out_weight, residual, groups)


def solution(mesh):
    in_specs = (
        P(None, "seq", "head"),
        P(None, "seq", "head"),
        P(None, "seq", "head"),
        P("seq", "head"),
        P("seq", "head"),
        P("head"),
        P(),
        P(),
        P("head", "seq"),
        P(None, "head", "seq"),
    )
    out_specs = P(None, "head", "seq")
    return jax.shard_map(body, mesh=mesh, in_specs=in_specs, out_specs=out_specs, check_vma=False)
```

```python
import functools
import math

import jax
import jax.numpy as jnp
from jax import lax
from jax.experimental import pallas as pl
from jax.experimental.pallas import tpu as pltpu
from jax.sharding import PartitionSpec as P

BLK = 128
NEG = -1e30
STEPS = 2
GROUP = 16
STATS = 128
MIB = 1024 * 1024


def iota(shape, dim):
    return lax.broadcasted_iota(jnp.int32, shape, dim)


def head_mask(width, hdim):
    return iota((GROUP, width), 1) // hdim == iota((GROUP, width), 0)


def by_step(x, mask):
    rows = [
        jnp.sum(jnp.where(mask, x[s * GROUP : (s + 1) * GROUP], 0.0), axis=0, keepdims=True)
        for s in range(STEPS)
    ]
    return jnp.concatenate(rows, axis=0)


def in_bf16_parts(x, parts):
    out = []
    for _ in range(parts):
        part = x.astype(jnp.bfloat16).astype(jnp.float32)
        out.append(part)
        x = x - part
    return out


def left(x, lanes):
    return pltpu.roll(x, x.shape[1] - lanes, 1) if lanes else x


def stage_kernel(keys, out, sems):
    copies = []
    for b in range(sems.shape[0]):
        rows = pl.ds(b * BLK, BLK)
        copies.append(pltpu.make_async_copy(keys.at[rows], out.at[rows], sems.at[b]))
    for copy in copies:
        copy.start()
    for copy in copies:
        copy.wait()


def attend_kernel(
    blocks,
    hdim,
    meta,
    slopes,
    query,
    own_stats,
    staged,
    keys,
    values,
    weight,
    out,
    weight_out,
    kbuf,
    vbuf,
    sems,
    weight_sem,
):
    width = keys.shape[1]
    per = STEPS * GROUP
    packs = BLK // per
    scale = 1.0 / math.sqrt(hdim)
    ready = staged.shape[0] // BLK
    key_copies = {}
    for b in range(ready, blocks):
        rows = pl.ds((b - ready) * BLK, BLK)
        copy = pltpu.make_async_copy(keys.at[pl.ds(b * BLK, BLK)], kbuf.at[rows], sems.at[0, b])
        key_copies[b] = copy
    value_copies = []
    for b in range(blocks):
        rows = pl.ds(b * BLK, BLK)
        value_copies.append(pltpu.make_async_copy(values.at[rows], vbuf.at[rows], sems.at[1, b]))
    weight_copy = pltpu.make_async_copy(weight, weight_out, weight_sem)
    for copy in (*key_copies.values(), *value_copies, weight_copy):
        copy.start()
    mask = head_mask(width, hdim)
    lane = iota((STEPS, STATS), 1)
    empty = jnp.concatenate(
        [jnp.zeros((STEPS, width), jnp.float32), jnp.where(lane < GROUP, NEG, 0.0)], axis=1
    ).astype(out.dtype)
    for r in range(out.shape[0]):
        out[r] = empty

    raw = []
    for g in range(blocks // packs):
        spread = []
        for b in range(g * packs, (g + 1) * packs):
            q = query[meta[0, b]].astype(jnp.float32)
            for s in range(STEPS):
                spread.append(jnp.where(mask, q[s : s + 1], 0.0).astype(jnp.bfloat16))
        spread = jnp.concatenate(spread, axis=0)
        first, last = g * packs, (g + 1) * packs
        split = min(max(first, ready), last)
        pieces = []
        if split > first:
            pieces.append(staged[first * BLK : split * BLK])
        if last > split:
            for b in range(split, last):
                key_copies[b].wait()
            pieces.append(kbuf[(split - ready) * BLK : (last - ready) * BLK])
        tiles = [
            lax.dot_general(
                piece, spread, (((1,), (1,)), ((), ())), preferred_element_type=jnp.float32
            )
            for piece in pieces
        ]
        raw.append(tiles[0] if len(tiles) == 1 else jnp.concatenate(tiles, axis=0))

    pack = iota((BLK, BLK), 1) // per
    when = (iota((BLK, BLK), 1) % per) // GROUP - iota((BLK, BLK), 0)
    slope = slopes[...]
    joined = [meta[3, b] == 1 for b in range(blocks)]
    scores = []
    tops = []
    for g in range(blocks // packs):
        for k in range(packs):
            b = g * packs + k
            tile = raw[g][k * BLK : (k + 1) * BLK]
            base = meta[1, b]
            x = tile if k == 0 else jnp.where(pack == k, tile, x)
            dist = when + base if k == 0 else jnp.where(pack == k, when + base, dist)
        x = x * scale - slope * dist.astype(jnp.float32)
        scores.append(x)
        top = jnp.max(x, axis=0, keepdims=True)
        tops += [left(top, k * per) for k in range(packs)]
    for b in range(1, blocks):
        tops[b] = jnp.where(joined[b], jnp.maximum(tops[b], tops[b - 1]), tops[b])
    for b in range(blocks - 2, -1, -1):
        tops[b] = jnp.where(joined[b + 1], tops[b + 1], tops[b])

    place = iota((1, BLK), 1) // per
    totals = []
    weights = []
    for g in range(blocks // packs):
        top = tops[g * packs]
        for k in range(1, packs):
            top = jnp.where(place == k, pltpu.roll(tops[g * packs + k], k * per, 1), top)
        probs = jnp.exp(scores[g] - top)
        total = jnp.sum(probs, axis=0, keepdims=True)
        totals += [left(total, k * per) for k in range(packs)]
        weights.append(probs.T.astype(jnp.bfloat16))
    for b in range(1, blocks):
        totals[b] = totals[b] + jnp.where(joined[b], totals[b - 1], 0.0)

    parts = in_bf16_parts(jnp.concatenate(tops, axis=0), 3)
    parts += in_bf16_parts(jnp.concatenate(totals, axis=0), 2)
    field = iota((blocks, STATS), 1) // GROUP
    stats = []
    for s in range(STEPS):
        row = jnp.zeros((blocks, STATS), jnp.float32)
        for k, part in enumerate(parts):
            row = jnp.where(field == k, left(part, (s - k) * GROUP % STATS), row)
        stats.append(row)

    rows = []
    acc = None
    for b in range(blocks):
        k = b % packs
        value_copies[b].wait()
        full = jnp.dot(
            weights[b // packs][k * per : (k + 1) * per],
            vbuf[b * BLK : (b + 1) * BLK],
            preferred_element_type=jnp.float32,
        )
        mine = by_step(full, mask)
        acc = mine if acc is None else mine + jnp.where(joined[b], acc, 0.0)
        tail = jnp.concatenate([x[b : b + 1] for x in stats], axis=0)
        row = jnp.concatenate([acc, tail], axis=1).astype(out.dtype)
        rows.append(jnp.where(meta[2, b] == 1, row, empty))
    for b in range(blocks):
        out[meta[0, b]] = rows[b]
    weight_copy.wait()


def own_kernel(heads, hdim, query, key, value, slopes, stats, acc):
    scale = 1.0 / math.sqrt(hdim)
    q = query[...].astype(jnp.float32)
    k = key[...].astype(jnp.float32)
    v = value[...].astype(jnp.float32)
    q0, q1 = q[0:1], q[1:2]
    k0, k1 = k[0:1], k[1:2]
    v0, v1 = v[0:1], v[1:2]
    lane = iota((1, STATS), 1)
    tops = [jnp.zeros((1, STATS), jnp.float32) for _ in range(STEPS)]
    sums = [jnp.zeros((1, STATS), jnp.float32) for _ in range(STEPS)]
    rows = [[], []]
    products = jnp.concatenate([q0 * k0, q1 * k0, q1 * k1], axis=0)
    for h in range(heads):
        at = slice(h * hdim, (h + 1) * hdim)
        dots = jnp.sum(products[:, at], axis=1, keepdims=True) * scale
        first = dots[0:1]
        cross = dots[1:2] - slopes[:, h : h + 1]
        second = dots[2:3]
        upper = jnp.maximum(cross, second)
        e_cross = jnp.exp(cross - upper)
        e_second = jnp.exp(second - upper)
        tops[0] = jnp.where(lane == h, first, tops[0])
        tops[1] = jnp.where(lane == h, upper, tops[1])
        sums[0] = jnp.where(lane == h + GROUP, 1.0, sums[0])
        sums[1] = jnp.where(lane == h + GROUP, e_cross + e_second, sums[1])
        rows[0].append(v0[:, at])
        rows[1].append(e_cross * v0[:, at] + e_second * v1[:, at])
    stats[...] = jnp.concatenate([tops[0] + sums[0], tops[1] + sums[1]], axis=0)
    acc[...] = jnp.concatenate([jnp.concatenate(r, axis=1) for r in rows], axis=0)


def join_kernel(heads, hdim, parts, own_stats, own_acc, out):
    width = heads * hdim
    count = parts.shape[0]
    stats = parts[:, width : width + STATS].astype(jnp.float32)
    top = (stats + left(stats, GROUP)) + left(stats, 2 * GROUP)
    total = left(stats, 3 * GROUP) + left(stats, 4 * GROUP)
    step = iota((count, STATS), 0) % STEPS
    lane = iota((count, STATS), 1)
    real = lane < heads
    top = jnp.where(real, top, NEG)
    total = jnp.where(real, total, 0.0)
    own = own_stats[...]
    own_real = iota(own.shape, 1) < heads
    own_top = jnp.where(own_real, own, 0.0)
    own_total = jnp.where(own_real, left(own, GROUP), 1.0)
    highest = [
        jnp.maximum(
            jnp.max(jnp.where(step == s, top, NEG), axis=0, keepdims=True), own_top[s : s + 1]
        )
        for s in range(STEPS)
    ]
    weight = jnp.exp(top - jnp.where(step == 0, highest[0], highest[1]))
    weight = jnp.where(real, weight, 0.0)
    own_weight = jnp.exp(own_top - jnp.concatenate(highest, axis=0))
    weighted = weight * total
    sums = [
        jnp.sum(jnp.where(step == s, weighted, 0.0), axis=0, keepdims=True) for s in range(STEPS)
    ]
    inverse = 1.0 / (jnp.concatenate(sums, axis=0) + own_weight * own_total)
    own_weight = own_weight * inverse
    weight = weight * jnp.where(step == 0, inverse[0:1], inverse[1:2])
    placed = jnp.where(step == 0, weight, 0.0) + pltpu.roll(
        jnp.where(step == 1, weight, 0.0), GROUP, 1
    )
    high, low = in_bf16_parts(placed, 2)
    both = high + pltpu.roll(low, STEPS * GROUP, 1)
    both = both.T[: 2 * STEPS * GROUP].astype(jnp.bfloat16)
    full = jnp.dot(both, parts[:, :width], preferred_element_type=jnp.float32)
    full = full[: STEPS * GROUP] + full[STEPS * GROUP :]
    acc = by_step(full, head_mask(width, hdim))
    mine = own_acc[...]
    mine = jnp.concatenate(
        [mine[:, h * hdim : (h + 1) * hdim] * own_weight[:, h : h + 1] for h in range(heads)],
        axis=1,
    )
    attended = (acc + mine).astype(out.dtype)
    for r in range(out.shape[0]):
        out[r] = attended


def project_kernel(rows, weight, mine, theirs):
    full = lax.dot_general(
        rows[...], weight[...], (((1,), (1,)), ((), ())), preferred_element_type=jnp.float32
    )
    first = lax.axis_index("head") % 2 == 0
    chips, size = mine.shape[0], mine.shape[1]
    for c in range(chips):
        a = full[2 * c * size : (2 * c + 1) * size]
        b = full[(2 * c + 1) * size : (2 * c + 2) * size]
        mine[c] = jnp.where(first, a, b)
        theirs[c] = jnp.where(first, b, a).astype(theirs.dtype)


def pair_kernel(mine, got, total, *rest):
    shares, both = rest[:-1], rest[-1]
    chips = mine.shape[0]
    chip = lax.axis_index("head") // 2
    for c in range(chips):
        both[c] = mine[c] + got[c].astype(jnp.float32)
    total[...] = both[chip]
    for hop, share in enumerate(shares, 1):
        share[...] = both[lax.rem(chip + hop, chips)].astype(share.dtype)


def finish_kernel(total, *rest):
    shares, residual, out = rest[:-2], rest[-2], rest[-1]
    x = total[...]
    for share in shares:
        x = x + share[...].astype(jnp.float32)
    for s in range(STEPS):
        rows = [x[r : r + 1] for r in range(s, x.shape[0], STEPS)]
        y = residual[s].astype(jnp.float32) + jnp.concatenate(rows, axis=0)
        out[s] = y.astype(out.dtype)


def copies_kernel(x, out):
    for r in range(out.shape[0]):
        out[r] = x[...]


def in_hbm(x):
    return pltpu.with_memory_space_constraint(x, pltpu.HBM)


def on_device(kernel, out_shape, in_spaces, limit, **more):
    return pl.pallas_call(
        kernel,
        out_shape=out_shape,
        in_specs=[pl.BlockSpec(memory_space=m) for m in in_spaces],
        compiler_params=pltpu.CompilerParams(vmem_limit_bytes=limit * MIB),
        **more,
    )


def block_table(seg_blocks, request_row, blocks):
    requests = seg_blocks.shape[0]
    order = jnp.arange(requests, dtype=jnp.int32)
    starts = jnp.sum(jnp.where(order[None, :] < order[:, None], seg_blocks[None, :], 0), axis=1)
    index = lax.axis_index("seq") * blocks + jnp.arange(blocks, dtype=jnp.int32)
    ends = starts + seg_blocks
    hit = (index[:, None] >= starts[None, :]) & (index[:, None] < ends[None, :])
    pick = lambda x: jnp.sum(jnp.where(hit, x[None, :], 0), axis=1)
    row = pick(request_row)
    base = pick(ends) * BLK - index * BLK
    live = jnp.any(hit, axis=1)
    before = hit & (index[:, None] > starts[None, :]) & (jnp.arange(blocks)[:, None] > 0)
    joined = jnp.any(before, axis=1)
    return jnp.stack([row, base, live.astype(jnp.int32), joined.astype(jnp.int32)])


def project_and_sum(rows, weight, residual, groups):
    chips = groups // 2
    size, columns = rows.shape[0] // groups, weight.shape[0]
    each = (chips, size, columns)
    mine, theirs = on_device(
        project_kernel,
        (jax.ShapeDtypeStruct(each, jnp.float32), jax.ShapeDtypeStruct(each, jnp.bfloat16)),
        [pltpu.VMEM] * 2,
        16,
    )(rows, weight)
    got = lax.ppermute(theirs, "head", [(i, i ^ 1) for i in range(groups)])
    share = jax.ShapeDtypeStruct((size, columns), jnp.bfloat16)
    total, *shares = on_device(
        pair_kernel,
        (jax.ShapeDtypeStruct((size, columns), jnp.float32), *[share] * (chips - 1)),
        [pltpu.VMEM] * 2,
        16,
        scratch_shapes=[pltpu.VMEM(each, jnp.float32)],
    )(mine, got)
    arrived = [
        lax.ppermute(x, "head", [(i, (i + 2 * hop) % groups) for i in range(groups)])
        for hop, x in enumerate(shares, 1)
    ]
    return on_device(
        finish_kernel,
        jax.ShapeDtypeStruct(residual.shape, residual.dtype),
        [pltpu.VMEM] * (chips + 1),
        16,
    )(total, *arrived, residual)


def body(
    queries,
    new_keys,
    new_values,
    cache_keys,
    cache_values,
    slopes,
    seg_blocks,
    request_row,
    out_weight,
    residual,
):
    heads = slopes.shape[0]
    width = queries.shape[2]
    hdim = width // heads
    peers = lax.axis_size("seq")
    groups = lax.axis_size("head")
    blocks = cache_keys.shape[0] // BLK
    vmem, smem, anywhere = pltpu.VMEM, pltpu.SMEM, pl.ANY
    own_query = queries.reshape(STEPS, width)

    copies = on_device(
        copies_kernel, jax.ShapeDtypeStruct((peers, STEPS, width), jnp.bfloat16), [vmem], 4
    )(own_query)
    everyone = lax.all_to_all(copies, "seq", 0, 0, tiled=True)

    table = block_table(seg_blocks, request_row, blocks)
    lanes = jnp.tile(jnp.pad(slopes, (0, GROUP - heads)), BLK // GROUP)[None]
    own_stats, own_acc = on_device(
        functools.partial(own_kernel, heads, hdim),
        (
            jax.ShapeDtypeStruct((STEPS, STATS), jnp.float32),
            jax.ShapeDtypeStruct((STEPS, width), jnp.float32),
        ),
        [vmem] * 4,
        4,
    )(own_query, new_keys.reshape(STEPS, width), new_values.reshape(STEPS, width), lanes)

    ready = blocks - 1
    staged = on_device(
        stage_kernel,
        pltpu.VMEM((ready * BLK, width), jnp.bfloat16),
        [pltpu.HBM],
        2,
        out_specs=pl.BlockSpec(memory_space=pl.ANY),
        scratch_shapes=[pltpu.SemaphoreType.DMA((ready,))],
        cost_estimate=pl.CostEstimate(
            flops=0, bytes_accessed=4 * ready * BLK * width, transcendentals=0
        ),
    )(in_hbm(cache_keys))
    partials, weight = on_device(
        functools.partial(attend_kernel, blocks, hdim),
        (
            jax.ShapeDtypeStruct((peers, STEPS, width + STATS), jnp.bfloat16),
            pltpu.HBM(out_weight.shape[::-1], jnp.bfloat16),
        ),
        [smem, vmem, vmem, pl.ANY, vmem] + [pltpu.HBM] * 3,
        32,
        out_specs=(pl.BlockSpec(memory_space=vmem), pl.BlockSpec(memory_space=pl.ANY)),
        scratch_shapes=[
            pltpu.VMEM(((blocks - ready) * BLK, width), jnp.bfloat16),
            pltpu.VMEM(cache_values.shape, jnp.bfloat16),
            pltpu.SemaphoreType.DMA((2, blocks)),
            pltpu.SemaphoreType.DMA,
        ],
    )(
        table,
        lanes,
        everyone,
        own_stats,
        staged,
        in_hbm(cache_keys),
        in_hbm(cache_values),
        in_hbm(out_weight.T),
    )
    arrived = lax.all_to_all(partials, "seq", 0, 0, tiled=True)

    attended = on_device(
        functools.partial(join_kernel, heads, hdim),
        jax.ShapeDtypeStruct((peers, STEPS, width), jnp.bfloat16),
        [vmem] * 3,
        16,
    )(arrived.reshape(peers * STEPS, width + STATS), own_stats, own_acc)
    rows = lax.all_to_all(attended, "seq", 0, 0, tiled=True).reshape(peers * STEPS, width)

    return project_and_sum(rows, weight, residual, groups)


def solution(mesh):
    in_specs = (
        P(None, "seq", "head"),
        P(None, "seq", "head"),
        P(None, "seq", "head"),
        P("seq", "head"),
        P("seq", "head"),
        P("head"),
        P(),
        P(),
        P("head", "seq"),
        P(None, "head", "seq"),
    )
    out_specs = P(None, "head", "seq")
    return jax.shard_map(body, mesh=mesh, in_specs=in_specs, out_specs=out_specs, check_vma=False)
```

```python
import functools
import math

import jax
import jax.numpy as jnp
from jax import lax
from jax.experimental import pallas as pl
from jax.experimental.pallas import tpu as pltpu
from jax.sharding import PartitionSpec as P

BLK = 128
NEG = -1e30
STEPS = 2
GROUP = 16
STATS = 128
MIB = 1024 * 1024


def iota(shape, dim):
    return lax.broadcasted_iota(jnp.int32, shape, dim)


def head_mask(width, hdim):
    return iota((GROUP, width), 1) // hdim == iota((GROUP, width), 0)


def by_step(x, mask):
    rows = [
        jnp.sum(jnp.where(mask, x[s * GROUP : (s + 1) * GROUP], 0.0), axis=0, keepdims=True)
        for s in range(STEPS)
    ]
    return jnp.concatenate(rows, axis=0)


def in_bf16_parts(x, parts):
    out = []
    for _ in range(parts):
        part = x.astype(jnp.bfloat16).astype(jnp.float32)
        out.append(part)
        x = x - part
    return out


def left(x, lanes):
    return pltpu.roll(x, x.shape[1] - lanes, 1) if lanes else x


def stage_kernel(keys, out, sems):
    copies = []
    for b in range(sems.shape[0]):
        rows = pl.ds(b * BLK, BLK)
        copies.append(pltpu.make_async_copy(keys.at[rows], out.at[rows], sems.at[b]))
    for copy in copies:
        copy.start()
    for copy in copies:
        copy.wait()


def attend_kernel(
    blocks,
    hdim,
    meta,
    slopes,
    query,
    own_stats,
    staged,
    keys,
    values,
    weight,
    out,
    weight_out,
    kbuf,
    vbuf,
    wbuf,
    sems,
    weight_sems,
):
    width = keys.shape[1]
    per = STEPS * GROUP
    packs = BLK // per
    scale = 1.0 / math.sqrt(hdim)
    ready = staged.shape[0] // BLK
    key_copies = {}
    for b in range(ready, blocks):
        rows = pl.ds((b - ready) * BLK, BLK)
        copy = pltpu.make_async_copy(keys.at[pl.ds(b * BLK, BLK)], kbuf.at[rows], sems.at[0, b])
        key_copies[b] = copy
    value_copies = []
    for b in range(blocks):
        rows = pl.ds(b * BLK, BLK)
        value_copies.append(pltpu.make_async_copy(values.at[rows], vbuf.at[rows], sems.at[1, b]))
    weight_in = pltpu.make_async_copy(weight, wbuf, weight_sems.at[0])
    weight_back = pltpu.make_async_copy(wbuf, weight_out, weight_sems.at[1])
    for copy in (*key_copies.values(), *value_copies, weight_in):
        copy.start()
    mask = head_mask(width, hdim)
    lane = iota((STEPS, STATS), 1)
    empty = jnp.concatenate(
        [jnp.zeros((STEPS, width), jnp.float32), jnp.where(lane < GROUP, NEG, 0.0)], axis=1
    ).astype(out.dtype)
    for r in range(out.shape[0]):
        out[r] = empty

    raw = []
    for g in range(blocks // packs):
        spread = []
        for b in range(g * packs, (g + 1) * packs):
            q = query[meta[0, b]].astype(jnp.float32)
            for s in range(STEPS):
                spread.append(jnp.where(mask, q[s : s + 1], 0.0).astype(jnp.bfloat16))
        spread = jnp.concatenate(spread, axis=0)
        first, last = g * packs, (g + 1) * packs
        split = min(max(first, ready), last)
        pieces = []
        if split > first:
            pieces.append(staged[first * BLK : split * BLK])
        if last > split:
            for b in range(split, last):
                key_copies[b].wait()
            pieces.append(kbuf[(split - ready) * BLK : (last - ready) * BLK])
        tiles = [
            lax.dot_general(
                piece, spread, (((1,), (1,)), ((), ())), preferred_element_type=jnp.float32
            )
            for piece in pieces
        ]
        raw.append(tiles[0] if len(tiles) == 1 else jnp.concatenate(tiles, axis=0))

    pack = iota((BLK, BLK), 1) // per
    when = (iota((BLK, BLK), 1) % per) // GROUP - iota((BLK, BLK), 0)
    slope = slopes[...]
    joined = [meta[3, b] == 1 for b in range(blocks)]
    scores = []
    tops = []
    for g in range(blocks // packs):
        for k in range(packs):
            b = g * packs + k
            tile = raw[g][k * BLK : (k + 1) * BLK]
            base = meta[1, b]
            x = tile if k == 0 else jnp.where(pack == k, tile, x)
            dist = when + base if k == 0 else jnp.where(pack == k, when + base, dist)
        x = x * scale - slope * dist.astype(jnp.float32)
        scores.append(x)
        top = jnp.max(x, axis=0, keepdims=True)
        tops += [left(top, k * per) for k in range(packs)]
    for b in range(1, blocks):
        tops[b] = jnp.where(joined[b], jnp.maximum(tops[b], tops[b - 1]), tops[b])
    for b in range(blocks - 2, -1, -1):
        tops[b] = jnp.where(joined[b + 1], tops[b + 1], tops[b])

    place = iota((1, BLK), 1) // per
    totals = []
    weights = []
    for g in range(blocks // packs):
        top = tops[g * packs]
        for k in range(1, packs):
            top = jnp.where(place == k, pltpu.roll(tops[g * packs + k], k * per, 1), top)
        probs = jnp.exp(scores[g] - top)
        total = jnp.sum(probs, axis=0, keepdims=True)
        totals += [left(total, k * per) for k in range(packs)]
        weights.append(probs.T.astype(jnp.bfloat16))
    for b in range(1, blocks):
        totals[b] = totals[b] + jnp.where(joined[b], totals[b - 1], 0.0)

    parts = in_bf16_parts(jnp.concatenate(tops, axis=0), 3)
    parts += in_bf16_parts(jnp.concatenate(totals, axis=0), 2)
    field = iota((blocks, STATS), 1) // GROUP
    stats = []
    for s in range(STEPS):
        row = jnp.zeros((blocks, STATS), jnp.float32)
        for k, part in enumerate(parts):
            row = jnp.where(field == k, left(part, (s - k) * GROUP % STATS), row)
        stats.append(row)

    rows = []
    acc = None
    for b in range(blocks):
        k = b % packs
        value_copies[b].wait()
        full = jnp.dot(
            weights[b // packs][k * per : (k + 1) * per],
            vbuf[b * BLK : (b + 1) * BLK],
            preferred_element_type=jnp.float32,
        )
        mine = by_step(full, mask)
        acc = mine if acc is None else mine + jnp.where(joined[b], acc, 0.0)
        tail = jnp.concatenate([x[b : b + 1] for x in stats], axis=0)
        row = jnp.concatenate([acc, tail], axis=1).astype(out.dtype)
        rows.append(jnp.where(meta[2, b] == 1, row, empty))
        if b == blocks // 2:
            weight_in.wait()
            weight_back.start()
    for b in range(blocks):
        out[meta[0, b]] = rows[b]
    weight_back.wait()


def own_kernel(heads, hdim, query, key, value, slopes, stats, acc):
    scale = 1.0 / math.sqrt(hdim)
    q = query[...].astype(jnp.float32)
    k = key[...].astype(jnp.float32)
    v = value[...].astype(jnp.float32)
    q0, q1 = q[0:1], q[1:2]
    k0, k1 = k[0:1], k[1:2]
    v0, v1 = v[0:1], v[1:2]
    lane = iota((1, STATS), 1)
    tops = [jnp.zeros((1, STATS), jnp.float32) for _ in range(STEPS)]
    sums = [jnp.zeros((1, STATS), jnp.float32) for _ in range(STEPS)]
    rows = [[], []]
    products = jnp.concatenate([q0 * k0, q1 * k0, q1 * k1], axis=0)
    for h in range(heads):
        at = slice(h * hdim, (h + 1) * hdim)
        dots = jnp.sum(products[:, at], axis=1, keepdims=True) * scale
        first = dots[0:1]
        cross = dots[1:2] - slopes[:, h : h + 1]
        second = dots[2:3]
        upper = jnp.maximum(cross, second)
        e_cross = jnp.exp(cross - upper)
        e_second = jnp.exp(second - upper)
        tops[0] = jnp.where(lane == h, first, tops[0])
        tops[1] = jnp.where(lane == h, upper, tops[1])
        sums[0] = jnp.where(lane == h + GROUP, 1.0, sums[0])
        sums[1] = jnp.where(lane == h + GROUP, e_cross + e_second, sums[1])
        rows[0].append(v0[:, at])
        rows[1].append(e_cross * v0[:, at] + e_second * v1[:, at])
    stats[...] = jnp.concatenate([tops[0] + sums[0], tops[1] + sums[1]], axis=0)
    acc[...] = jnp.concatenate([jnp.concatenate(r, axis=1) for r in rows], axis=0)


def join_kernel(heads, hdim, parts, own_stats, own_acc, out):
    width = heads * hdim
    count = parts.shape[0]
    stats = parts[:, width : width + STATS].astype(jnp.float32)
    top = (stats + left(stats, GROUP)) + left(stats, 2 * GROUP)
    total = left(stats, 3 * GROUP) + left(stats, 4 * GROUP)
    step = iota((count, STATS), 0) % STEPS
    lane = iota((count, STATS), 1)
    real = lane < heads
    top = jnp.where(real, top, NEG)
    total = jnp.where(real, total, 0.0)
    own = own_stats[...]
    own_real = iota(own.shape, 1) < heads
    own_top = jnp.where(own_real, own, 0.0)
    own_total = jnp.where(own_real, left(own, GROUP), 1.0)
    highest = [
        jnp.maximum(
            jnp.max(jnp.where(step == s, top, NEG), axis=0, keepdims=True), own_top[s : s + 1]
        )
        for s in range(STEPS)
    ]
    weight = jnp.exp(top - jnp.where(step == 0, highest[0], highest[1]))
    weight = jnp.where(real, weight, 0.0)
    own_weight = jnp.exp(own_top - jnp.concatenate(highest, axis=0))
    weighted = weight * total
    sums = [
        jnp.sum(jnp.where(step == s, weighted, 0.0), axis=0, keepdims=True) for s in range(STEPS)
    ]
    inverse = 1.0 / (jnp.concatenate(sums, axis=0) + own_weight * own_total)
    own_weight = own_weight * inverse
    weight = weight * jnp.where(step == 0, inverse[0:1], inverse[1:2])
    placed = jnp.where(step == 0, weight, 0.0) + pltpu.roll(
        jnp.where(step == 1, weight, 0.0), GROUP, 1
    )
    high, low = in_bf16_parts(placed, 2)
    both = high + pltpu.roll(low, STEPS * GROUP, 1)
    both = both.T[: 2 * STEPS * GROUP].astype(jnp.bfloat16)
    full = jnp.dot(both, parts[:, :width], preferred_element_type=jnp.float32)
    full = full[: STEPS * GROUP] + full[STEPS * GROUP :]
    acc = by_step(full, head_mask(width, hdim))
    mine = own_acc[...]
    mine = jnp.concatenate(
        [mine[:, h * hdim : (h + 1) * hdim] * own_weight[:, h : h + 1] for h in range(heads)],
        axis=1,
    )
    attended = (acc + mine).astype(out.dtype)
    for r in range(out.shape[0]):
        out[r] = attended


def project_kernel(rows, weight, mine, theirs):
    full = lax.dot_general(
        rows[...], weight[...], (((1,), (1,)), ((), ())), preferred_element_type=jnp.float32
    )
    first = lax.axis_index("head") % 2 == 0
    chips, size = mine.shape[0], mine.shape[1]
    for c in range(chips):
        a = full[2 * c * size : (2 * c + 1) * size]
        b = full[(2 * c + 1) * size : (2 * c + 2) * size]
        mine[c] = jnp.where(first, a, b)
        theirs[c] = jnp.where(first, b, a).astype(theirs.dtype)


def pair_kernel(mine, got, total, *rest):
    shares, both = rest[:-1], rest[-1]
    chips = mine.shape[0]
    chip = lax.axis_index("head") // 2
    for c in range(chips):
        both[c] = mine[c] + got[c].astype(jnp.float32)
    total[...] = both[chip]
    for hop, share in enumerate(shares, 1):
        share[...] = both[lax.rem(chip + hop, chips)].astype(share.dtype)


def finish_kernel(total, *rest):
    shares, residual, out = rest[:-2], rest[-2], rest[-1]
    x = total[...]
    for share in shares:
        x = x + share[...].astype(jnp.float32)
    for s in range(STEPS):
        rows = [x[r : r + 1] for r in range(s, x.shape[0], STEPS)]
        y = residual[s].astype(jnp.float32) + jnp.concatenate(rows, axis=0)
        out[s] = y.astype(out.dtype)


def copies_kernel(x, out):
    for r in range(out.shape[0]):
        out[r] = x[...]


def in_hbm(x):
    return pltpu.with_memory_space_constraint(x, pltpu.HBM)


def on_device(kernel, out_shape, in_spaces, limit, **more):
    return pl.pallas_call(
        kernel,
        out_shape=out_shape,
        in_specs=[pl.BlockSpec(memory_space=m) for m in in_spaces],
        compiler_params=pltpu.CompilerParams(vmem_limit_bytes=limit * MIB),
        **more,
    )


def block_table(seg_blocks, request_row, blocks):
    requests = seg_blocks.shape[0]
    order = jnp.arange(requests, dtype=jnp.int32)
    starts = jnp.sum(jnp.where(order[None, :] < order[:, None], seg_blocks[None, :], 0), axis=1)
    index = lax.axis_index("seq") * blocks + jnp.arange(blocks, dtype=jnp.int32)
    ends = starts + seg_blocks
    hit = (index[:, None] >= starts[None, :]) & (index[:, None] < ends[None, :])
    pick = lambda x: jnp.sum(jnp.where(hit, x[None, :], 0), axis=1)
    row = pick(request_row)
    base = pick(ends) * BLK - index * BLK
    live = jnp.any(hit, axis=1)
    before = hit & (index[:, None] > starts[None, :]) & (jnp.arange(blocks)[:, None] > 0)
    joined = jnp.any(before, axis=1)
    return jnp.stack([row, base, live.astype(jnp.int32), joined.astype(jnp.int32)])


def project_and_sum(rows, weight, residual, groups):
    chips = groups // 2
    size, columns = rows.shape[0] // groups, weight.shape[0]
    each = (chips, size, columns)
    mine, theirs = on_device(
        project_kernel,
        (jax.ShapeDtypeStruct(each, jnp.float32), jax.ShapeDtypeStruct(each, jnp.bfloat16)),
        [pltpu.VMEM] * 2,
        16,
    )(rows, weight)
    got = lax.ppermute(theirs, "head", [(i, i ^ 1) for i in range(groups)])
    share = jax.ShapeDtypeStruct((size, columns), jnp.bfloat16)
    total, *shares = on_device(
        pair_kernel,
        (jax.ShapeDtypeStruct((size, columns), jnp.float32), *[share] * (chips - 1)),
        [pltpu.VMEM] * 2,
        16,
        scratch_shapes=[pltpu.VMEM(each, jnp.float32)],
    )(mine, got)
    arrived = [
        lax.ppermute(x, "head", [(i, (i + 2 * hop) % groups) for i in range(groups)])
        for hop, x in enumerate(shares, 1)
    ]
    return on_device(
        finish_kernel,
        jax.ShapeDtypeStruct(residual.shape, residual.dtype),
        [pltpu.VMEM] * (chips + 1),
        16,
    )(total, *arrived, residual)


def body(
    queries,
    new_keys,
    new_values,
    cache_keys,
    cache_values,
    slopes,
    seg_blocks,
    request_row,
    out_weight,
    residual,
):
    heads = slopes.shape[0]
    width = queries.shape[2]
    hdim = width // heads
    peers = lax.axis_size("seq")
    groups = lax.axis_size("head")
    blocks = cache_keys.shape[0] // BLK
    vmem, smem, anywhere = pltpu.VMEM, pltpu.SMEM, pl.ANY
    own_query = queries.reshape(STEPS, width)

    copies = on_device(
        copies_kernel, jax.ShapeDtypeStruct((peers, STEPS, width), jnp.bfloat16), [vmem], 4
    )(own_query)
    everyone = lax.all_to_all(copies, "seq", 0, 0, tiled=True)

    table = block_table(seg_blocks, request_row, blocks)
    lanes = jnp.tile(jnp.pad(slopes, (0, GROUP - heads)), BLK // GROUP)[None]
    own_stats, own_acc = on_device(
        functools.partial(own_kernel, heads, hdim),
        (
            jax.ShapeDtypeStruct((STEPS, STATS), jnp.float32),
            jax.ShapeDtypeStruct((STEPS, width), jnp.float32),
        ),
        [vmem] * 4,
        4,
    )(own_query, new_keys.reshape(STEPS, width), new_values.reshape(STEPS, width), lanes)

    ready = blocks - 1
    staged = on_device(
        stage_kernel,
        pltpu.VMEM((ready * BLK, width), jnp.bfloat16),
        [pltpu.HBM],
        2,
        out_specs=pl.BlockSpec(memory_space=pl.ANY),
        scratch_shapes=[pltpu.SemaphoreType.DMA((ready,))],
        cost_estimate=pl.CostEstimate(
            flops=0, bytes_accessed=4 * ready * BLK * width, transcendentals=0
        ),
    )(in_hbm(cache_keys))
    partials, weight = on_device(
        functools.partial(attend_kernel, blocks, hdim),
        (
            jax.ShapeDtypeStruct((peers, STEPS, width + STATS), jnp.bfloat16),
            pltpu.HBM(out_weight.shape[::-1], jnp.bfloat16),
        ),
        [smem, vmem, vmem, pl.ANY, vmem] + [pltpu.HBM] * 3,
        32,
        out_specs=(pl.BlockSpec(memory_space=vmem), pl.BlockSpec(memory_space=pl.ANY)),
        scratch_shapes=[
            pltpu.VMEM(((blocks - ready) * BLK, width), jnp.bfloat16),
            pltpu.VMEM(cache_values.shape, jnp.bfloat16),
            pltpu.VMEM(out_weight.shape[::-1], jnp.bfloat16),
            pltpu.SemaphoreType.DMA((2, blocks)),
            pltpu.SemaphoreType.DMA((2,)),
        ],
    )(
        table,
        lanes,
        everyone,
        own_stats,
        staged,
        in_hbm(cache_keys),
        in_hbm(cache_values),
        in_hbm(out_weight.T),
    )
    arrived = lax.all_to_all(partials, "seq", 0, 0, tiled=True)

    attended = on_device(
        functools.partial(join_kernel, heads, hdim),
        jax.ShapeDtypeStruct((peers, STEPS, width), jnp.bfloat16),
        [vmem] * 3,
        16,
    )(arrived.reshape(peers * STEPS, width + STATS), own_stats, own_acc)
    rows = lax.all_to_all(attended, "seq", 0, 0, tiled=True).reshape(peers * STEPS, width)

    return project_and_sum(rows, weight, residual, groups)


def solution(mesh):
    in_specs = (
        P(None, "seq", "head"),
        P(None, "seq", "head"),
        P(None, "seq", "head"),
        P("seq", "head"),
        P("seq", "head"),
        P("head"),
        P(),
        P(),
        P("head", "seq"),
        P(None, "head", "seq"),
    )
    out_specs = P(None, "head", "seq")
    return jax.shard_map(body, mesh=mesh, in_specs=in_specs, out_specs=out_specs, check_vma=False)
```

```python
import functools
import math

import jax
import jax.numpy as jnp
from jax import lax
from jax.experimental import pallas as pl
from jax.experimental.pallas import tpu as pltpu
from jax.sharding import PartitionSpec as P

BLK = 128
NEG = -1e30
STEPS = 2
GROUP = 16
STATS = 128
MIB = 1024 * 1024


def iota(shape, dim):
    return lax.broadcasted_iota(jnp.int32, shape, dim)


def head_mask(width, hdim):
    return iota((GROUP, width), 1) // hdim == iota((GROUP, width), 0)


def by_step(x, mask):
    rows = [
        jnp.sum(jnp.where(mask, x[s * GROUP : (s + 1) * GROUP], 0.0), axis=0, keepdims=True)
        for s in range(STEPS)
    ]
    return jnp.concatenate(rows, axis=0)


def in_bf16_parts(x, parts):
    out = []
    for _ in range(parts):
        part = x.astype(jnp.bfloat16).astype(jnp.float32)
        out.append(part)
        x = x - part
    return out


def left(x, lanes):
    return pltpu.roll(x, x.shape[1] - lanes, 1) if lanes else x


def stage_kernel(keys, out, sems):
    copies = []
    for b in range(sems.shape[0]):
        rows = pl.ds(b * BLK, BLK)
        copies.append(pltpu.make_async_copy(keys.at[rows], out.at[rows], sems.at[b]))
    for copy in copies:
        copy.start()
    for copy in copies:
        copy.wait()


def attend_kernel(
    blocks,
    hdim,
    meta,
    slopes,
    query,
    own_stats,
    staged,
    keys,
    values,
    weight,
    out,
    weight_out,
    kbuf,
    vbuf,
    wbuf,
    sems,
    weight_sems,
):
    width = keys.shape[1]
    per = STEPS * GROUP
    packs = BLK // per
    scale = 1.0 / math.sqrt(hdim)
    ready = staged.shape[0] // BLK
    key_copies = {}
    for b in range(ready, blocks):
        rows = pl.ds((b - ready) * BLK, BLK)
        copy = pltpu.make_async_copy(keys.at[pl.ds(b * BLK, BLK)], kbuf.at[rows], sems.at[0, b])
        key_copies[b] = copy
    value_copies = []
    for b in range(blocks):
        rows = pl.ds(b * BLK, BLK)
        value_copies.append(pltpu.make_async_copy(values.at[rows], vbuf.at[rows], sems.at[1, b]))
    weight_in = pltpu.make_async_copy(weight, wbuf, weight_sems.at[0])
    weight_back = pltpu.make_async_copy(wbuf, weight_out, weight_sems.at[1])
    for copy in (*key_copies.values(), *value_copies, weight_in):
        copy.start()
    mask = head_mask(width, hdim)
    lane = iota((STEPS, STATS), 1)
    empty = jnp.concatenate(
        [jnp.zeros((STEPS, width), jnp.float32), jnp.where(lane < GROUP, NEG, 0.0)], axis=1
    ).astype(out.dtype)
    for r in range(out.shape[0]):
        out[r] = empty

    raw = []
    for g in range(blocks // packs):
        spread = []
        for b in range(g * packs, (g + 1) * packs):
            q = query[meta[0, b]].astype(jnp.float32)
            for s in range(STEPS):
                spread.append(jnp.where(mask, q[s : s + 1], 0.0).astype(jnp.bfloat16))
        spread = jnp.concatenate(spread, axis=0)
        first, last = g * packs, (g + 1) * packs
        split = min(max(first, ready), last)
        pieces = []
        if split > first:
            pieces.append(staged[first * BLK : split * BLK])
        if last > split:
            for b in range(split, last):
                key_copies[b].wait()
            pieces.append(kbuf[(split - ready) * BLK : (last - ready) * BLK])
        tiles = [
            lax.dot_general(
                piece, spread, (((1,), (1,)), ((), ())), preferred_element_type=jnp.float32
            )
            for piece in pieces
        ]
        raw.append(tiles[0] if len(tiles) == 1 else jnp.concatenate(tiles, axis=0))

    pack = iota((BLK, BLK), 1) // per
    when = (iota((BLK, BLK), 1) % per) // GROUP - iota((BLK, BLK), 0)
    slope = slopes[...]
    joined = [meta[3, b] == 1 for b in range(blocks)]
    scores = []
    tops = []
    for g in range(blocks // packs):
        for k in range(packs):
            b = g * packs + k
            tile = raw[g][k * BLK : (k + 1) * BLK]
            base = meta[1, b]
            x = tile if k == 0 else jnp.where(pack == k, tile, x)
            dist = when + base if k == 0 else jnp.where(pack == k, when + base, dist)
        x = x * scale - slope * dist.astype(jnp.float32)
        scores.append(x)
        top = jnp.max(x, axis=0, keepdims=True)
        tops += [left(top, k * per) for k in range(packs)]
    for b in range(1, blocks):
        tops[b] = jnp.where(joined[b], jnp.maximum(tops[b], tops[b - 1]), tops[b])
    for b in range(blocks - 2, -1, -1):
        tops[b] = jnp.where(joined[b + 1], tops[b + 1], tops[b])

    place = iota((1, BLK), 1) // per
    totals = []
    weights = []
    for g in range(blocks // packs):
        top = tops[g * packs]
        for k in range(1, packs):
            top = jnp.where(place == k, pltpu.roll(tops[g * packs + k], k * per, 1), top)
        probs = jnp.exp(scores[g] - top)
        total = jnp.sum(probs, axis=0, keepdims=True)
        totals += [left(total, k * per) for k in range(packs)]
        weights.append(probs.T.astype(jnp.bfloat16))
    for b in range(1, blocks):
        totals[b] = totals[b] + jnp.where(joined[b], totals[b - 1], 0.0)

    parts = in_bf16_parts(jnp.concatenate(tops, axis=0), 3)
    parts += in_bf16_parts(jnp.concatenate(totals, axis=0), 2)
    field = iota((blocks, STATS), 1) // GROUP
    stats = []
    for s in range(STEPS):
        row = jnp.zeros((blocks, STATS), jnp.float32)
        for k, part in enumerate(parts):
            row = jnp.where(field == k, left(part, (s - k) * GROUP % STATS), row)
        stats.append(row)

    rows = []
    acc = None
    for b in range(blocks):
        k = b % packs
        value_copies[b].wait()
        full = jnp.dot(
            weights[b // packs][k * per : (k + 1) * per],
            vbuf[b * BLK : (b + 1) * BLK],
            preferred_element_type=jnp.float32,
        )
        mine = by_step(full, mask)
        acc = mine if acc is None else mine + jnp.where(joined[b], acc, 0.0)
        tail = jnp.concatenate([x[b : b + 1] for x in stats], axis=0)
        row = jnp.concatenate([acc, tail], axis=1).astype(out.dtype)
        rows.append(jnp.where(meta[2, b] == 1, row, empty))
        if b == blocks // 2:
            weight_in.wait()
            weight_back.start()
    for b in range(blocks):
        out[meta[0, b]] = rows[b]
    weight_back.wait()


def own_kernel(heads, hdim, query, key, value, slopes, stats, acc):
    scale = 1.0 / math.sqrt(hdim)
    q = query[...].astype(jnp.float32)
    k = key[...].astype(jnp.float32)
    v = value[...].astype(jnp.float32)
    q0, q1 = q[0:1], q[1:2]
    k0, k1 = k[0:1], k[1:2]
    v0, v1 = v[0:1], v[1:2]
    lane = iota((1, STATS), 1)
    tops = [jnp.zeros((1, STATS), jnp.float32) for _ in range(STEPS)]
    sums = [jnp.zeros((1, STATS), jnp.float32) for _ in range(STEPS)]
    rows = [[], []]
    products = jnp.concatenate([q0 * k0, q1 * k0, q1 * k1], axis=0)
    for h in range(heads):
        at = slice(h * hdim, (h + 1) * hdim)
        dots = jnp.sum(products[:, at], axis=1, keepdims=True) * scale
        first = dots[0:1]
        cross = dots[1:2] - slopes[:, h : h + 1]
        second = dots[2:3]
        upper = jnp.maximum(cross, second)
        e_cross = jnp.exp(cross - upper)
        e_second = jnp.exp(second - upper)
        tops[0] = jnp.where(lane == h, first, tops[0])
        tops[1] = jnp.where(lane == h, upper, tops[1])
        sums[0] = jnp.where(lane == h + GROUP, 1.0, sums[0])
        sums[1] = jnp.where(lane == h + GROUP, e_cross + e_second, sums[1])
        rows[0].append(v0[:, at])
        rows[1].append(e_cross * v0[:, at] + e_second * v1[:, at])
    stats[...] = jnp.concatenate([tops[0] + sums[0], tops[1] + sums[1]], axis=0)
    acc[...] = jnp.concatenate([jnp.concatenate(r, axis=1) for r in rows], axis=0)


def join_kernel(heads, hdim, parts, own_stats, own_acc, out):
    width = heads * hdim
    count = parts.shape[0]
    stats = parts[:, width : width + STATS].astype(jnp.float32)
    top = (stats + left(stats, GROUP)) + left(stats, 2 * GROUP)
    total = left(stats, 3 * GROUP) + left(stats, 4 * GROUP)
    step = iota((count, STATS), 0) % STEPS
    lane = iota((count, STATS), 1)
    real = lane < heads
    top = jnp.where(real, top, NEG)
    total = jnp.where(real, total, 0.0)
    own = own_stats[...]
    own_real = iota(own.shape, 1) < heads
    own_top = jnp.where(own_real, own, 0.0)
    own_total = jnp.where(own_real, left(own, GROUP), 1.0)
    highest = [
        jnp.maximum(
            jnp.max(jnp.where(step == s, top, NEG), axis=0, keepdims=True), own_top[s : s + 1]
        )
        for s in range(STEPS)
    ]
    weight = jnp.exp(top - jnp.where(step == 0, highest[0], highest[1]))
    weight = jnp.where(real, weight, 0.0)
    own_weight = jnp.exp(own_top - jnp.concatenate(highest, axis=0))
    weighted = weight * total
    sums = [
        jnp.sum(jnp.where(step == s, weighted, 0.0), axis=0, keepdims=True) for s in range(STEPS)
    ]
    inverse = 1.0 / (jnp.concatenate(sums, axis=0) + own_weight * own_total)
    own_weight = own_weight * inverse
    weight = weight * jnp.where(step == 0, inverse[0:1], inverse[1:2])
    placed = jnp.where(step == 0, weight, 0.0) + pltpu.roll(
        jnp.where(step == 1, weight, 0.0), GROUP, 1
    )
    high, low = in_bf16_parts(placed, 2)
    both = high + pltpu.roll(low, STEPS * GROUP, 1)
    both = both.T[: 2 * STEPS * GROUP].astype(jnp.bfloat16)
    full = jnp.dot(both, parts[:, :width], preferred_element_type=jnp.float32)
    full = full[: STEPS * GROUP] + full[STEPS * GROUP :]
    acc = by_step(full, head_mask(width, hdim))
    mine = own_acc[...]
    mine = jnp.concatenate(
        [mine[:, h * hdim : (h + 1) * hdim] * own_weight[:, h : h + 1] for h in range(heads)],
        axis=1,
    )
    attended = (acc + mine).astype(out.dtype)
    for r in range(out.shape[0]):
        out[r] = attended


def project_kernel(rows, weight, out):
    full = lax.dot_general(
        rows[...], weight[...], (((1,), (1,)), ((), ())), preferred_element_type=jnp.float32
    )
    size = out.shape[1]
    for i in range(out.shape[0]):
        out[i] = full[i * size : (i + 1) * size].astype(out.dtype)


def finish_kernel(shares, residual, out):
    x = jnp.sum(shares[...].astype(jnp.float32), axis=0)
    for s in range(STEPS):
        rows = [x[r : r + 1] for r in range(s, x.shape[0], STEPS)]
        y = residual[s].astype(jnp.float32) + jnp.concatenate(rows, axis=0)
        out[s] = y.astype(out.dtype)


def copies_kernel(x, out):
    for r in range(out.shape[0]):
        out[r] = x[...]


def in_hbm(x):
    return pltpu.with_memory_space_constraint(x, pltpu.HBM)


def on_device(kernel, out_shape, in_spaces, limit, **more):
    return pl.pallas_call(
        kernel,
        out_shape=out_shape,
        in_specs=[pl.BlockSpec(memory_space=m) for m in in_spaces],
        compiler_params=pltpu.CompilerParams(vmem_limit_bytes=limit * MIB),
        **more,
    )


def block_table(seg_blocks, request_row, blocks):
    requests = seg_blocks.shape[0]
    order = jnp.arange(requests, dtype=jnp.int32)
    starts = jnp.sum(jnp.where(order[None, :] < order[:, None], seg_blocks[None, :], 0), axis=1)
    index = lax.axis_index("seq") * blocks + jnp.arange(blocks, dtype=jnp.int32)
    ends = starts + seg_blocks
    hit = (index[:, None] >= starts[None, :]) & (index[:, None] < ends[None, :])
    pick = lambda x: jnp.sum(jnp.where(hit, x[None, :], 0), axis=1)
    row = pick(request_row)
    base = pick(ends) * BLK - index * BLK
    live = jnp.any(hit, axis=1)
    before = hit & (index[:, None] > starts[None, :]) & (jnp.arange(blocks)[:, None] > 0)
    joined = jnp.any(before, axis=1)
    return jnp.stack([row, base, live.astype(jnp.int32), joined.astype(jnp.int32)])


def project_and_sum(rows, weight, residual, groups):
    each = (groups, rows.shape[0] // groups, weight.shape[0])
    projected = on_device(
        project_kernel, jax.ShapeDtypeStruct(each, jnp.bfloat16), [pltpu.VMEM] * 2, 16
    )(rows, weight)
    shares = lax.all_to_all(projected, "head", 0, 0, tiled=True)
    return on_device(
        finish_kernel,
        jax.ShapeDtypeStruct(residual.shape, residual.dtype),
        [pltpu.VMEM] * 2,
        16,
    )(shares, residual)


def body(
    queries,
    new_keys,
    new_values,
    cache_keys,
    cache_values,
    slopes,
    seg_blocks,
    request_row,
    out_weight,
    residual,
):
    heads = slopes.shape[0]
    width = queries.shape[2]
    hdim = width // heads
    peers = lax.axis_size("seq")
    groups = lax.axis_size("head")
    blocks = cache_keys.shape[0] // BLK
    vmem, smem, anywhere = pltpu.VMEM, pltpu.SMEM, pl.ANY
    own_query = queries.reshape(STEPS, width)

    copies = on_device(
        copies_kernel, jax.ShapeDtypeStruct((peers, STEPS, width), jnp.bfloat16), [vmem], 4
    )(in_hbm(own_query))
    everyone = lax.all_to_all(copies, "seq", 0, 0, tiled=True)

    table = block_table(seg_blocks, request_row, blocks)
    lanes = jnp.tile(jnp.pad(slopes, (0, GROUP - heads)), BLK // GROUP)[None]
    own_stats, own_acc = on_device(
        functools.partial(own_kernel, heads, hdim),
        (
            jax.ShapeDtypeStruct((STEPS, STATS), jnp.float32),
            jax.ShapeDtypeStruct((STEPS, width), jnp.float32),
        ),
        [vmem] * 4,
        4,
    )(own_query, new_keys.reshape(STEPS, width), new_values.reshape(STEPS, width), lanes)

    ready = blocks - 1
    staged = on_device(
        stage_kernel,
        pltpu.VMEM((ready * BLK, width), jnp.bfloat16),
        [pltpu.HBM],
        2,
        out_specs=pl.BlockSpec(memory_space=pl.ANY),
        scratch_shapes=[pltpu.SemaphoreType.DMA((ready,))],
        cost_estimate=pl.CostEstimate(
            flops=0, bytes_accessed=4 * ready * BLK * width, transcendentals=0
        ),
    )(in_hbm(cache_keys))
    partials, weight = on_device(
        functools.partial(attend_kernel, blocks, hdim),
        (
            jax.ShapeDtypeStruct((peers, STEPS, width + STATS), jnp.bfloat16),
            pltpu.HBM(out_weight.shape[::-1], jnp.bfloat16),
        ),
        [smem, vmem, vmem, pl.ANY, vmem] + [pltpu.HBM] * 3,
        32,
        out_specs=(pl.BlockSpec(memory_space=vmem), pl.BlockSpec(memory_space=pl.ANY)),
        scratch_shapes=[
            pltpu.VMEM(((blocks - ready) * BLK, width), jnp.bfloat16),
            pltpu.VMEM(cache_values.shape, jnp.bfloat16),
            pltpu.VMEM(out_weight.shape[::-1], jnp.bfloat16),
            pltpu.SemaphoreType.DMA((2, blocks)),
            pltpu.SemaphoreType.DMA((2,)),
        ],
    )(
        table,
        lanes,
        everyone,
        own_stats,
        staged,
        in_hbm(cache_keys),
        in_hbm(cache_values),
        in_hbm(out_weight.T),
    )
    arrived = lax.all_to_all(partials, "seq", 0, 0, tiled=True)

    attended = on_device(
        functools.partial(join_kernel, heads, hdim),
        jax.ShapeDtypeStruct((peers, STEPS, width), jnp.bfloat16),
        [vmem] * 3,
        16,
    )(arrived.reshape(peers * STEPS, width + STATS), own_stats, own_acc)
    rows = lax.all_to_all(attended, "seq", 0, 0, tiled=True).reshape(peers * STEPS, width)

    return project_and_sum(rows, weight, residual, groups)


def solution(mesh):
    in_specs = (
        P(None, "seq", "head"),
        P(None, "seq", "head"),
        P(None, "seq", "head"),
        P("seq", "head"),
        P("seq", "head"),
        P("head"),
        P(),
        P(),
        P("head", "seq"),
        P(None, "head", "seq"),
    )
    out_specs = P(None, "head", "seq")
    return jax.shard_map(body, mesh=mesh, in_specs=in_specs, out_specs=out_specs, check_vma=False)
```

```python
import functools
import math

import jax
import jax.numpy as jnp
from jax import lax
from jax.experimental import pallas as pl
from jax.experimental.pallas import tpu as pltpu
from jax.sharding import PartitionSpec as P

BLK = 128
NEG = -1e30
STEPS = 2
GROUP = 16
ROWS = 8
STATS = 128
MIB = 1024 * 1024


def iota(shape, dim):
    return lax.broadcasted_iota(jnp.int32, shape, dim)


def head_mask(width, hdim):
    return iota((GROUP, width), 1) // hdim == iota((GROUP, width), 0)


def by_step(x, mask):
    rows = [
        jnp.sum(jnp.where(mask, x[s * GROUP : (s + 1) * GROUP], 0.0), axis=0, keepdims=True)
        for s in range(STEPS)
    ]
    return jnp.concatenate(rows, axis=0)


def in_bf16_parts(x, parts):
    out = []
    for _ in range(parts):
        part = x.astype(jnp.bfloat16).astype(jnp.float32)
        out.append(part)
        x = x - part
    return out


def left(x, lanes):
    return pltpu.roll(x, x.shape[1] - lanes, 1) if lanes else x


def stage_kernel(keys, weight, out, weight_out, wbuf, sems, weight_sems):
    weight_in = pltpu.make_async_copy(weight, wbuf, weight_sems.at[0])
    weight_back = pltpu.make_async_copy(wbuf, weight_out, weight_sems.at[1])
    weight_in.start()
    copies = []
    for b in range(sems.shape[0]):
        rows = pl.ds(b * BLK, BLK)
        copies.append(pltpu.make_async_copy(keys.at[rows], out.at[rows], sems.at[b]))
    for copy in copies:
        copy.start()
    weight_in.wait()
    weight_back.start()
    for copy in (*copies, weight_back):
        copy.wait()


def attend_kernel(
    blocks,
    hdim,
    meta,
    slopes,
    query,
    own_stats,
    staged,
    keys,
    values,
    weight,
    out,
    weight_out,
    kbuf,
    vbuf,
    sems,
):
    width = keys.shape[1]
    per = STEPS * GROUP
    packs = BLK // per
    scale = 1.0 / math.sqrt(hdim)
    ready = staged.shape[0] // BLK
    key_copies = {}
    for b in range(ready, blocks):
        rows = pl.ds((b - ready) * BLK, BLK)
        copy = pltpu.make_async_copy(keys.at[pl.ds(b * BLK, BLK)], kbuf.at[rows], sems.at[0, b])
        key_copies[b] = copy
    value_copies = []
    for b in range(blocks):
        rows = pl.ds(b * BLK, BLK)
        value_copies.append(pltpu.make_async_copy(values.at[rows], vbuf.at[rows], sems.at[1, b]))
    for copy in (*key_copies.values(), *value_copies):
        copy.start()
    mask = head_mask(width, hdim)
    lane = iota((STEPS, STATS), 1)
    empty = jnp.concatenate(
        [jnp.zeros((STEPS, width), jnp.float32), jnp.where(lane < GROUP, NEG, 0.0)], axis=1
    ).astype(out.dtype)
    for r in range(out.shape[0]):
        out[r] = empty

    raw = []
    for g in range(blocks // packs):
        spread = []
        for b in range(g * packs, (g + 1) * packs):
            q = query[meta[0, b]].astype(jnp.float32)
            for s in range(STEPS):
                spread.append(jnp.where(mask, q[s : s + 1], 0.0).astype(jnp.bfloat16))
        spread = jnp.concatenate(spread, axis=0)
        first, last = g * packs, (g + 1) * packs
        split = min(max(first, ready), last)
        pieces = []
        if split > first:
            pieces.append(staged[first * BLK : split * BLK])
        if last > split:
            for b in range(split, last):
                key_copies[b].wait()
            pieces.append(kbuf[(split - ready) * BLK : (last - ready) * BLK])
        tiles = [
            lax.dot_general(
                piece, spread, (((1,), (1,)), ((), ())), preferred_element_type=jnp.float32
            )
            for piece in pieces
        ]
        raw.append(tiles[0] if len(tiles) == 1 else jnp.concatenate(tiles, axis=0))

    pack = iota((BLK, BLK), 1) // per
    when = (iota((BLK, BLK), 1) % per) // GROUP - iota((BLK, BLK), 0)
    slope = slopes[...]
    joined = [meta[3, b] == 1 for b in range(blocks)]
    scores = []
    tops = []
    for g in range(blocks // packs):
        for k in range(packs):
            b = g * packs + k
            tile = raw[g][k * BLK : (k + 1) * BLK]
            base = meta[1, b]
            x = tile if k == 0 else jnp.where(pack == k, tile, x)
            dist = when + base if k == 0 else jnp.where(pack == k, when + base, dist)
        x = x * scale - slope * dist.astype(jnp.float32)
        scores.append(x)
        top = jnp.max(x, axis=0, keepdims=True)
        tops += [left(top, k * per) for k in range(packs)]
    for b in range(1, blocks):
        tops[b] = jnp.where(joined[b], jnp.maximum(tops[b], tops[b - 1]), tops[b])
    for b in range(blocks - 2, -1, -1):
        tops[b] = jnp.where(joined[b + 1], tops[b + 1], tops[b])

    row = iota((BLK, BLK), 0)
    source = row // per * per + row % STEPS * GROUP + row % per // STEPS
    swap = (source == iota((BLK, BLK), 1)).astype(jnp.bfloat16)
    place = iota((1, BLK), 1) // per
    totals = []
    weights = []
    for g in range(blocks // packs):
        top = tops[g * packs]
        for k in range(1, packs):
            top = jnp.where(place == k, pltpu.roll(tops[g * packs + k], k * per, 1), top)
        probs = jnp.exp(scores[g] - top)
        total = jnp.sum(probs, axis=0, keepdims=True)
        totals += [left(total, k * per) for k in range(packs)]
        weights.append(
            lax.dot_general(
                swap,
                probs.astype(jnp.bfloat16),
                (((1,), (1,)), ((), ())),
                preferred_element_type=jnp.float32,
            )
        )
    for b in range(1, blocks):
        totals[b] = totals[b] + jnp.where(joined[b], totals[b - 1], 0.0)

    parts = in_bf16_parts(jnp.concatenate(tops, axis=0), 3)
    parts += in_bf16_parts(jnp.concatenate(totals, axis=0), 2)
    field = iota((blocks, STATS), 1) // GROUP
    stats = []
    for s in range(STEPS):
        row = jnp.zeros((blocks, STATS), jnp.float32)
        for k, part in enumerate(parts):
            row = jnp.where(field == k, left(part, (s - k) * GROUP % STATS), row)
        stats.append(row)

    rows = []
    acc = None
    for b in range(blocks):
        k = b % packs
        value_copies[b].wait()
        mine = []
        for h in range(0, width // hdim, ROWS // STEPS):
            lanes = slice(h * hdim, min(h + ROWS // STEPS, width // hdim) * hdim)
            some = jnp.dot(
                weights[b // packs][k * per + STEPS * h :][:ROWS].astype(jnp.bfloat16),
                vbuf[b * BLK : (b + 1) * BLK, lanes],
                preferred_element_type=jnp.float32,
            )
            for i in range(some.shape[1] // hdim):
                mine.append(some[STEPS * i : STEPS * (i + 1), i * hdim : (i + 1) * hdim])
        mine = jnp.concatenate(mine, axis=1)
        acc = mine if acc is None else mine + jnp.where(joined[b], acc, 0.0)
        tail = jnp.concatenate([x[b : b + 1] for x in stats], axis=0)
        row = jnp.concatenate([acc, tail], axis=1).astype(out.dtype)
        rows.append(jnp.where(meta[2, b] == 1, row, empty))
    for b in range(blocks):
        out[meta[0, b]] = rows[b]


def own_kernel(heads, hdim, query, key, value, slopes, stats, acc):
    scale = 1.0 / math.sqrt(hdim)
    q = query[...].astype(jnp.float32)
    k = key[...].astype(jnp.float32)
    v = value[...].astype(jnp.float32)
    q0, q1 = q[0:1], q[1:2]
    k0, k1 = k[0:1], k[1:2]
    v0, v1 = v[0:1], v[1:2]
    lane = iota((1, STATS), 1)
    tops = [jnp.zeros((1, STATS), jnp.float32) for _ in range(STEPS)]
    sums = [jnp.zeros((1, STATS), jnp.float32) for _ in range(STEPS)]
    rows = [[], []]
    products = jnp.concatenate([q0 * k0, q1 * k0, q1 * k1], axis=0)
    for h in range(heads):
        at = slice(h * hdim, (h + 1) * hdim)
        dots = jnp.sum(products[:, at], axis=1, keepdims=True) * scale
        first = dots[0:1]
        cross = dots[1:2] - slopes[:, h : h + 1]
        second = dots[2:3]
        upper = jnp.maximum(cross, second)
        e_cross = jnp.exp(cross - upper)
        e_second = jnp.exp(second - upper)
        tops[0] = jnp.where(lane == h, first, tops[0])
        tops[1] = jnp.where(lane == h, upper, tops[1])
        sums[0] = jnp.where(lane == h + GROUP, 1.0, sums[0])
        sums[1] = jnp.where(lane == h + GROUP, e_cross + e_second, sums[1])
        rows[0].append(v0[:, at])
        rows[1].append(e_cross * v0[:, at] + e_second * v1[:, at])
    stats[...] = jnp.concatenate([tops[0] + sums[0], tops[1] + sums[1]], axis=0)
    acc[...] = jnp.concatenate([jnp.concatenate(r, axis=1) for r in rows], axis=0)


def join_kernel(heads, hdim, parts, own_stats, own_acc, out):
    width = heads * hdim
    count = parts.shape[0]
    stats = parts[:, width : width + STATS].astype(jnp.float32)
    top = (stats + left(stats, GROUP)) + left(stats, 2 * GROUP)
    total = left(stats, 3 * GROUP) + left(stats, 4 * GROUP)
    step = iota((count, STATS), 0) % STEPS
    lane = iota((count, STATS), 1)
    real = lane < heads
    top = jnp.where(real, top, NEG)
    total = jnp.where(real, total, 0.0)
    own = own_stats[...]
    own_real = iota(own.shape, 1) < heads
    own_top = jnp.where(own_real, own, 0.0)
    own_total = jnp.where(own_real, left(own, GROUP), 1.0)
    highest = [
        jnp.maximum(
            jnp.max(jnp.where(step == s, top, NEG), axis=0, keepdims=True), own_top[s : s + 1]
        )
        for s in range(STEPS)
    ]
    weight = jnp.exp(top - jnp.where(step == 0, highest[0], highest[1]))
    weight = jnp.where(real, weight, 0.0)
    own_weight = jnp.exp(own_top - jnp.concatenate(highest, axis=0))
    weighted = weight * total
    sums = [
        jnp.sum(jnp.where(step == s, weighted, 0.0), axis=0, keepdims=True) for s in range(STEPS)
    ]
    inverse = 1.0 / (jnp.concatenate(sums, axis=0) + own_weight * own_total)
    own_weight = own_weight * inverse
    weight = weight * jnp.where(step == 0, inverse[0:1], inverse[1:2])
    placed = jnp.where(step == 0, weight, 0.0) + pltpu.roll(
        jnp.where(step == 1, weight, 0.0), GROUP, 1
    )
    high, low = in_bf16_parts(placed, 2)
    both = high + pltpu.roll(low, STEPS * GROUP, 1)
    both = both.T[: 2 * STEPS * GROUP].astype(jnp.bfloat16)
    full = jnp.dot(both, parts[:, :width], preferred_element_type=jnp.float32)
    full = full[: STEPS * GROUP] + full[STEPS * GROUP :]
    acc = by_step(full, head_mask(width, hdim))
    mine = own_acc[...]
    mine = jnp.concatenate(
        [mine[:, h * hdim : (h + 1) * hdim] * own_weight[:, h : h + 1] for h in range(heads)],
        axis=1,
    )
    attended = (acc + mine).astype(out.dtype)
    for r in range(out.shape[0]):
        out[r] = attended


def project_kernel(rows, weight, mine, theirs):
    full = lax.dot_general(
        rows[...], weight[...], (((1,), (1,)), ((), ())), preferred_element_type=jnp.float32
    )
    first = lax.axis_index("head") % 2 == 0
    chips, size = mine.shape[0], mine.shape[1]
    for c in range(chips):
        a = full[2 * c * size : (2 * c + 1) * size]
        b = full[(2 * c + 1) * size : (2 * c + 2) * size]
        mine[c] = jnp.where(first, a, b)
        theirs[c] = jnp.where(first, b, a).astype(theirs.dtype)


def pair_kernel(mine, got, total, *rest):
    shares, both = rest[:-1], rest[-1]
    chips = mine.shape[0]
    chip = lax.axis_index("head") // 2
    for c in range(chips):
        both[c] = mine[c] + got[c].astype(jnp.float32)
    total[...] = both[chip]
    for hop, share in enumerate(shares, 1):
        share[...] = both[lax.rem(chip + hop, chips)].astype(share.dtype)


def finish_kernel(total, *rest):
    shares, residual, out = rest[:-2], rest[-2], rest[-1]
    x = total[...]
    for share in shares:
        x = x + share[...].astype(jnp.float32)
    for s in range(STEPS):
        rows = [x[r : r + 1] for r in range(s, x.shape[0], STEPS)]
        y = residual[s].astype(jnp.float32) + jnp.concatenate(rows, axis=0)
        out[s] = y.astype(out.dtype)


def copies_kernel(x, out):
    for r in range(out.shape[0]):
        out[r] = x[...]


def in_hbm(x):
    return pltpu.with_memory_space_constraint(x, pltpu.HBM)


def on_device(kernel, out_shape, in_spaces, limit, **more):
    return pl.pallas_call(
        kernel,
        out_shape=out_shape,
        in_specs=[pl.BlockSpec(memory_space=m) for m in in_spaces],
        compiler_params=pltpu.CompilerParams(vmem_limit_bytes=limit * MIB),
        **more,
    )


def block_table(seg_blocks, request_row, blocks):
    requests = seg_blocks.shape[0]
    order = jnp.arange(requests, dtype=jnp.int32)
    starts = jnp.sum(jnp.where(order[None, :] < order[:, None], seg_blocks[None, :], 0), axis=1)
    index = lax.axis_index("seq") * blocks + jnp.arange(blocks, dtype=jnp.int32)
    ends = starts + seg_blocks
    hit = (index[:, None] >= starts[None, :]) & (index[:, None] < ends[None, :])
    pick = lambda x: jnp.sum(jnp.where(hit, x[None, :], 0), axis=1)
    row = pick(request_row)
    base = pick(ends) * BLK - index * BLK
    live = jnp.any(hit, axis=1)
    before = hit & (index[:, None] > starts[None, :]) & (jnp.arange(blocks)[:, None] > 0)
    joined = jnp.any(before, axis=1)
    return jnp.stack([row, base, live.astype(jnp.int32), joined.astype(jnp.int32)])


def project_and_sum(rows, weight, residual, groups):
    chips = groups // 2
    size, columns = rows.shape[0] // groups, weight.shape[0]
    each = (chips, size, columns)
    mine, theirs = on_device(
        project_kernel,
        (jax.ShapeDtypeStruct(each, jnp.float32), jax.ShapeDtypeStruct(each, jnp.bfloat16)),
        [pltpu.VMEM] * 2,
        16,
    )(rows, weight)
    got = lax.ppermute(theirs, "head", [(i, i ^ 1) for i in range(groups)])
    share = jax.ShapeDtypeStruct((size, columns), jnp.bfloat16)
    total, *shares = on_device(
        pair_kernel,
        (jax.ShapeDtypeStruct((size, columns), jnp.float32), *[share] * (chips - 1)),
        [pltpu.VMEM] * 2,
        16,
        scratch_shapes=[pltpu.VMEM(each, jnp.float32)],
    )(mine, got)
    arrived = [
        lax.ppermute(x, "head", [(i, (i + 2 * hop) % groups) for i in range(groups)])
        for hop, x in enumerate(shares, 1)
    ]
    return on_device(
        finish_kernel,
        jax.ShapeDtypeStruct(residual.shape, residual.dtype),
        [pltpu.VMEM] * (chips + 1),
        16,
    )(total, *arrived, residual)


def body(
    queries,
    new_keys,
    new_values,
    cache_keys,
    cache_values,
    slopes,
    seg_blocks,
    request_row,
    out_weight,
    residual,
):
    heads = slopes.shape[0]
    width = queries.shape[2]
    hdim = width // heads
    peers = lax.axis_size("seq")
    groups = lax.axis_size("head")
    blocks = cache_keys.shape[0] // BLK
    vmem, smem, anywhere = pltpu.VMEM, pltpu.SMEM, pl.ANY
    own_query = queries.reshape(STEPS, width)

    copies = on_device(
        copies_kernel, jax.ShapeDtypeStruct((peers, STEPS, width), jnp.bfloat16), [vmem], 4
    )(own_query)
    everyone = lax.all_to_all(copies, "seq", 0, 0, tiled=True)

    table = block_table(seg_blocks, request_row, blocks)
    lanes = jnp.tile(jnp.pad(slopes, (0, GROUP - heads)), BLK // GROUP)[None]
    own_stats, own_acc = on_device(
        functools.partial(own_kernel, heads, hdim),
        (
            jax.ShapeDtypeStruct((STEPS, STATS), jnp.float32),
            jax.ShapeDtypeStruct((STEPS, width), jnp.float32),
        ),
        [vmem] * 4,
        4,
    )(own_query, new_keys.reshape(STEPS, width), new_values.reshape(STEPS, width), lanes)

    ready = blocks - 1
    turned = out_weight.shape[::-1]
    staged, weight = on_device(
        stage_kernel,
        (pltpu.VMEM((ready * BLK, width), jnp.bfloat16), pltpu.HBM(turned, jnp.bfloat16)),
        [pltpu.HBM] * 2,
        4,
        out_specs=[pl.BlockSpec(memory_space=pl.ANY)] * 2,
        scratch_shapes=[
            pltpu.VMEM(turned, jnp.bfloat16),
            pltpu.SemaphoreType.DMA((ready,)),
            pltpu.SemaphoreType.DMA((2,)),
        ],
        cost_estimate=pl.CostEstimate(
            flops=0, bytes_accessed=4 * ready * BLK * width, transcendentals=0
        ),
    )(in_hbm(cache_keys), in_hbm(out_weight.T))
    partials, weight = on_device(
        functools.partial(attend_kernel, blocks, hdim),
        (
            jax.ShapeDtypeStruct((peers, STEPS, width + STATS), jnp.bfloat16),
            pltpu.HBM(turned, jnp.bfloat16),
        ),
        [smem, vmem, vmem, pl.ANY, vmem] + [pltpu.HBM] * 3,
        32,
        out_specs=(pl.BlockSpec(memory_space=vmem), pl.BlockSpec(memory_space=pl.ANY)),
        input_output_aliases={7: 1},
        scratch_shapes=[
            pltpu.VMEM(((blocks - ready) * BLK, width), jnp.bfloat16),
            pltpu.VMEM(cache_values.shape, jnp.bfloat16),
            pltpu.SemaphoreType.DMA((2, blocks)),
        ],
    )(
        table,
        lanes,
        everyone,
        own_stats,
        staged,
        in_hbm(cache_keys),
        in_hbm(cache_values),
        weight,
    )
    arrived = lax.all_to_all(partials, "seq", 0, 0, tiled=True)

    attended = on_device(
        functools.partial(join_kernel, heads, hdim),
        jax.ShapeDtypeStruct((peers, STEPS, width), jnp.bfloat16),
        [vmem] * 3,
        16,
    )(arrived.reshape(peers * STEPS, width + STATS), own_stats, own_acc)
    rows = lax.all_to_all(attended, "seq", 0, 0, tiled=True).reshape(peers * STEPS, width)

    return project_and_sum(rows, weight, residual, groups)


def solution(mesh):
    in_specs = (
        P(None, "seq", "head"),
        P(None, "seq", "head"),
        P(None, "seq", "head"),
        P("seq", "head"),
        P("seq", "head"),
        P("head"),
        P(),
        P(),
        P("head", "seq"),
        P(None, "head", "seq"),
    )
    out_specs = P(None, "head", "seq")
    return jax.shard_map(body, mesh=mesh, in_specs=in_specs, out_specs=out_specs, check_vma=False)
```

```python
import functools
import math

import jax
import jax.numpy as jnp
from jax import lax
from jax.experimental import pallas as pl
from jax.experimental.pallas import tpu as pltpu
from jax.sharding import PartitionSpec as P

BLK = 128
NEG = -1e30
STEPS = 2
GROUP = 16
ROWS = 8
STATS = 128
MIB = 1024 * 1024


def iota(shape, dim):
    return lax.broadcasted_iota(jnp.int32, shape, dim)


def head_mask(width, hdim):
    return iota((GROUP, width), 1) // hdim == iota((GROUP, width), 0)


def by_step(x, mask):
    rows = [
        jnp.sum(jnp.where(mask, x[s * GROUP : (s + 1) * GROUP], 0.0), axis=0, keepdims=True)
        for s in range(STEPS)
    ]
    return jnp.concatenate(rows, axis=0)


def in_bf16_parts(x, parts):
    out = []
    for _ in range(parts):
        part = x.astype(jnp.bfloat16).astype(jnp.float32)
        out.append(part)
        x = x - part
    return out


def left(x, lanes):
    return pltpu.roll(x, x.shape[1] - lanes, 1) if lanes else x


def stage_kernel(keys, weight, out, weight_out, wbuf, sems, weight_sems):
    weight_in = pltpu.make_async_copy(weight, wbuf, weight_sems.at[0])
    weight_back = pltpu.make_async_copy(wbuf, weight_out, weight_sems.at[1])
    weight_in.start()
    copies = []
    for b in range(sems.shape[0]):
        rows = pl.ds(b * BLK, BLK)
        copies.append(pltpu.make_async_copy(keys.at[rows], out.at[rows], sems.at[b]))
    for copy in copies:
        copy.start()
    weight_in.wait()
    weight_back.start()
    for copy in (*copies, weight_back):
        copy.wait()


def attend_kernel(
    blocks,
    hdim,
    meta,
    slopes,
    query,
    own_stats,
    staged,
    keys,
    values,
    weight,
    out,
    weight_out,
    kbuf,
    vbuf,
    sems,
):
    width = keys.shape[1]
    per = STEPS * GROUP
    packs = BLK // per
    scale = 1.0 / math.sqrt(hdim)
    ready = staged.shape[0] // BLK
    key_copies = {}
    for b in range(ready, blocks):
        rows = pl.ds((b - ready) * BLK, BLK)
        copy = pltpu.make_async_copy(keys.at[pl.ds(b * BLK, BLK)], kbuf.at[rows], sems.at[0, b])
        key_copies[b] = copy
    value_copies = []
    for b in range(blocks):
        rows = pl.ds(b * BLK, BLK)
        value_copies.append(pltpu.make_async_copy(values.at[rows], vbuf.at[rows], sems.at[1, b]))
    for copy in (*key_copies.values(), *value_copies):
        copy.start()
    mask = head_mask(width, hdim)
    lane = iota((STEPS, STATS), 1)
    empty = jnp.concatenate(
        [jnp.zeros((STEPS, width), jnp.float32), jnp.where(lane < GROUP, NEG, 0.0)], axis=1
    ).astype(out.dtype)
    for r in range(out.shape[0]):
        out[r] = empty

    raw = []
    for g in range(blocks // packs):
        spread = []
        for b in range(g * packs, (g + 1) * packs):
            q = query[meta[0, b]].astype(jnp.float32)
            for s in range(STEPS):
                spread.append(jnp.where(mask, q[s : s + 1], 0.0).astype(jnp.bfloat16))
        spread = jnp.concatenate(spread, axis=0)
        first, last = g * packs, (g + 1) * packs
        split = min(max(first, ready), last)
        pieces = []
        if split > first:
            pieces.append(staged[first * BLK : split * BLK])
        if last > split:
            for b in range(split, last):
                key_copies[b].wait()
            pieces.append(kbuf[(split - ready) * BLK : (last - ready) * BLK])
        tiles = [
            lax.dot_general(
                piece, spread, (((1,), (1,)), ((), ())), preferred_element_type=jnp.float32
            )
            for piece in pieces
        ]
        raw.append(tiles[0] if len(tiles) == 1 else jnp.concatenate(tiles, axis=0))

    pack = iota((BLK, BLK), 1) // per
    when = (iota((BLK, BLK), 1) % per) // GROUP - iota((BLK, BLK), 0)
    slope = slopes[...]
    joined = [meta[3, b] == 1 for b in range(blocks)]
    scores = []
    tops = []
    for g in range(blocks // packs):
        for k in range(packs):
            b = g * packs + k
            tile = raw[g][k * BLK : (k + 1) * BLK]
            base = meta[1, b]
            x = tile if k == 0 else jnp.where(pack == k, tile, x)
            dist = when + base if k == 0 else jnp.where(pack == k, when + base, dist)
        x = x * scale - slope * dist.astype(jnp.float32)
        scores.append(x)
        top = jnp.max(x, axis=0, keepdims=True)
        tops += [left(top, k * per) for k in range(packs)]
    for b in range(1, blocks):
        tops[b] = jnp.where(joined[b], jnp.maximum(tops[b], tops[b - 1]), tops[b])
    for b in range(blocks - 2, -1, -1):
        tops[b] = jnp.where(joined[b + 1], tops[b + 1], tops[b])

    row = iota((BLK, BLK), 0)
    source = row // per * per + row % STEPS * GROUP + row % per // STEPS
    swap = (source == iota((BLK, BLK), 1)).astype(jnp.bfloat16)
    place = iota((1, BLK), 1) // per
    totals = []
    weights = []
    for g in range(blocks // packs):
        top = tops[g * packs]
        for k in range(1, packs):
            top = jnp.where(place == k, pltpu.roll(tops[g * packs + k], k * per, 1), top)
        probs = jnp.exp(scores[g] - top)
        total = jnp.sum(probs, axis=0, keepdims=True)
        totals += [left(total, k * per) for k in range(packs)]
        weights.append(
            lax.dot_general(
                swap,
                probs.astype(jnp.bfloat16),
                (((1,), (1,)), ((), ())),
                preferred_element_type=jnp.float32,
            )
        )
    for b in range(1, blocks):
        totals[b] = totals[b] + jnp.where(joined[b], totals[b - 1], 0.0)

    parts = in_bf16_parts(jnp.concatenate(tops, axis=0), 3)
    parts += in_bf16_parts(jnp.concatenate(totals, axis=0), 2)
    field = iota((blocks, STATS), 1) // GROUP
    stats = []
    for s in range(STEPS):
        row = jnp.zeros((blocks, STATS), jnp.float32)
        for k, part in enumerate(parts):
            row = jnp.where(field == k, left(part, (s - k) * GROUP % STATS), row)
        stats.append(row)

    rows = []
    acc = None
    for b in range(blocks):
        k = b % packs
        value_copies[b].wait()
        mine = []
        for h in range(0, width // hdim, ROWS // STEPS):
            lanes = slice(h * hdim, min(h + ROWS // STEPS, width // hdim) * hdim)
            some = jnp.dot(
                weights[b // packs][k * per + STEPS * h :][:ROWS].astype(jnp.bfloat16),
                vbuf[b * BLK : (b + 1) * BLK, lanes],
                preferred_element_type=jnp.float32,
            )
            for i in range(some.shape[1] // hdim):
                mine.append(some[STEPS * i : STEPS * (i + 1), i * hdim : (i + 1) * hdim])
        mine = jnp.concatenate(mine, axis=1)
        acc = mine if acc is None else mine + jnp.where(joined[b], acc, 0.0)
        tail = jnp.concatenate([x[b : b + 1] for x in stats], axis=0)
        row = jnp.concatenate([acc, tail], axis=1).astype(out.dtype)
        rows.append(jnp.where(meta[2, b] == 1, row, empty))
    for b in range(blocks):
        out[meta[0, b]] = rows[b]


def own_terms(heads, hdim, query, key, value, slopes):
    scale = 1.0 / math.sqrt(hdim)
    q = query[...].astype(jnp.float32)
    k = key[...].astype(jnp.float32)
    v = value[...].astype(jnp.float32)
    q0, q1 = q[0:1], q[1:2]
    k0, k1 = k[0:1], k[1:2]
    v0, v1 = v[0:1], v[1:2]
    lane = iota((1, STATS), 1)
    tops = [jnp.zeros((1, STATS), jnp.float32) for _ in range(STEPS)]
    sums = [jnp.zeros((1, STATS), jnp.float32) for _ in range(STEPS)]
    rows = [[], []]
    products = jnp.concatenate([q0 * k0, q1 * k0, q1 * k1], axis=0)
    for h in range(heads):
        at = slice(h * hdim, (h + 1) * hdim)
        dots = jnp.sum(products[:, at], axis=1, keepdims=True) * scale
        first = dots[0:1]
        cross = dots[1:2] - slopes[h]
        second = dots[2:3]
        upper = jnp.maximum(cross, second)
        e_cross = jnp.exp(cross - upper)
        e_second = jnp.exp(second - upper)
        tops[0] = jnp.where(lane == h, first, tops[0])
        tops[1] = jnp.where(lane == h, upper, tops[1])
        sums[0] = jnp.where(lane == h + GROUP, 1.0, sums[0])
        sums[1] = jnp.where(lane == h + GROUP, e_cross + e_second, sums[1])
        rows[0].append(v0[:, at])
        rows[1].append(e_cross * v0[:, at] + e_second * v1[:, at])
    stats = jnp.concatenate([tops[0] + sums[0], tops[1] + sums[1]], axis=0)
    return stats, jnp.concatenate([jnp.concatenate(r, axis=1) for r in rows], axis=0)


def block_table(blocks, seg_blocks, request_row):
    requests = seg_blocks.shape[0]
    index = lax.axis_index("seq") * blocks

    def skip(i, carry):
        request, end, total = carry
        total = total + seg_blocks[i]
        passed = total <= index
        return request + passed.astype(jnp.int32), jnp.where(passed, total, end), total

    zero = jnp.int32(0)
    request, end, _ = lax.fori_loop(0, requests, skip, (zero, zero, zero))
    last = requests - 1
    end = end + seg_blocks[jnp.minimum(request, last)]
    table = []
    for b in range(blocks):
        joined = jnp.bool_(False)
        if b:
            joined = index + b < end
            request = jnp.where(joined, request, request + 1)
            end = jnp.where(joined, end, end + seg_blocks[jnp.minimum(request, last)])
        live = request <= last
        row = request_row[jnp.minimum(request, last)]
        table.append((row, (end - index - b) * BLK, live, joined & live))
    return table


def own_kernel(
    blocks,
    heads,
    seg_blocks,
    request_row,
    slopes,
    query,
    key,
    value,
    table,
    lanes,
    stats,
    acc,
):
    for b, entry in enumerate(block_table(blocks, seg_blocks, request_row)):
        for i, x in enumerate(entry):
            table[i, b] = x.astype(jnp.int32)
    slope = jnp.zeros((1, BLK), jnp.float32)
    for h in range(heads):
        slope = jnp.where(iota((1, BLK), 1) % GROUP == h, slopes[h], slope)
    lanes[...] = slope
    stats[...], acc[...] = own_terms(heads, query.shape[1] // heads, query, key, value, slopes)


def join_kernel(heads, hdim, parts, own_stats, own_acc, out):
    width = heads * hdim
    count = parts.shape[0]
    stats = parts[:, width : width + STATS].astype(jnp.float32)
    top = (stats + left(stats, GROUP)) + left(stats, 2 * GROUP)
    total = left(stats, 3 * GROUP) + left(stats, 4 * GROUP)
    step = iota((count, STATS), 0) % STEPS
    lane = iota((count, STATS), 1)
    real = lane < heads
    top = jnp.where(real, top, NEG)
    total = jnp.where(real, total, 0.0)
    own = own_stats[...]
    own_real = iota(own.shape, 1) < heads
    own_top = jnp.where(own_real, own, 0.0)
    own_total = jnp.where(own_real, left(own, GROUP), 1.0)
    highest = [
        jnp.maximum(
            jnp.max(jnp.where(step == s, top, NEG), axis=0, keepdims=True), own_top[s : s + 1]
        )
        for s in range(STEPS)
    ]
    weight = jnp.exp(top - jnp.where(step == 0, highest[0], highest[1]))
    weight = jnp.where(real, weight, 0.0)
    own_weight = jnp.exp(own_top - jnp.concatenate(highest, axis=0))
    weighted = weight * total
    sums = [
        jnp.sum(jnp.where(step == s, weighted, 0.0), axis=0, keepdims=True) for s in range(STEPS)
    ]
    inverse = 1.0 / (jnp.concatenate(sums, axis=0) + own_weight * own_total)
    own_weight = own_weight * inverse
    weight = weight * jnp.where(step == 0, inverse[0:1], inverse[1:2])
    placed = jnp.where(step == 0, weight, 0.0) + pltpu.roll(
        jnp.where(step == 1, weight, 0.0), GROUP, 1
    )
    high, low = in_bf16_parts(placed, 2)
    both = high + pltpu.roll(low, STEPS * GROUP, 1)
    both = both.T[: 2 * STEPS * GROUP].astype(jnp.bfloat16)
    full = jnp.dot(both, parts[:, :width], preferred_element_type=jnp.float32)
    full = full[: STEPS * GROUP] + full[STEPS * GROUP :]
    acc = by_step(full, head_mask(width, hdim))
    mine = own_acc[...]
    mine = jnp.concatenate(
        [mine[:, h * hdim : (h + 1) * hdim] * own_weight[:, h : h + 1] for h in range(heads)],
        axis=1,
    )
    attended = (acc + mine).astype(out.dtype)
    for r in range(out.shape[0]):
        out[r] = attended


def project_kernel(rows, weight, mine, theirs):
    full = lax.dot_general(
        rows[...], weight[...], (((1,), (1,)), ((), ())), preferred_element_type=jnp.float32
    )
    first = lax.axis_index("head") % 2 == 0
    chips, size = mine.shape[0], mine.shape[1]
    for c in range(chips):
        a = full[2 * c * size : (2 * c + 1) * size]
        b = full[(2 * c + 1) * size : (2 * c + 2) * size]
        mine[c] = jnp.where(first, a, b)
        theirs[c] = jnp.where(first, b, a).astype(theirs.dtype)


def pair_kernel(mine, got, total, *rest):
    shares, both = rest[:-1], rest[-1]
    chips = mine.shape[0]
    chip = lax.axis_index("head") // 2
    for c in range(chips):
        both[c] = mine[c] + got[c].astype(jnp.float32)
    total[...] = both[chip]
    for hop, share in enumerate(shares, 1):
        share[...] = both[lax.rem(chip + hop, chips)].astype(share.dtype)


def finish_kernel(total, *rest):
    shares, residual, out = rest[:-2], rest[-2], rest[-1]
    x = total[...]
    for share in shares:
        x = x + share[...].astype(jnp.float32)
    for s in range(STEPS):
        rows = [x[r : r + 1] for r in range(s, x.shape[0], STEPS)]
        y = residual[s].astype(jnp.float32) + jnp.concatenate(rows, axis=0)
        out[s] = y.astype(out.dtype)


def copies_kernel(x, out):
    for r in range(out.shape[0]):
        out[r] = x[...]


def in_hbm(x):
    return pltpu.with_memory_space_constraint(x, pltpu.HBM)


def on_device(kernel, out_shape, in_spaces, limit, **more):
    return pl.pallas_call(
        kernel,
        out_shape=out_shape,
        in_specs=[pl.BlockSpec(memory_space=m) for m in in_spaces],
        compiler_params=pltpu.CompilerParams(vmem_limit_bytes=limit * MIB),
        **more,
    )


def project_and_sum(rows, weight, residual, groups):
    chips = groups // 2
    size, columns = rows.shape[0] // groups, weight.shape[0]
    each = (chips, size, columns)
    mine, theirs = on_device(
        project_kernel,
        (jax.ShapeDtypeStruct(each, jnp.float32), jax.ShapeDtypeStruct(each, jnp.bfloat16)),
        [pltpu.VMEM] * 2,
        16,
    )(rows, weight)
    got = lax.ppermute(theirs, "head", [(i, i ^ 1) for i in range(groups)])
    share = jax.ShapeDtypeStruct((size, columns), jnp.bfloat16)
    total, *shares = on_device(
        pair_kernel,
        (jax.ShapeDtypeStruct((size, columns), jnp.float32), *[share] * (chips - 1)),
        [pltpu.VMEM] * 2,
        16,
        scratch_shapes=[pltpu.VMEM(each, jnp.float32)],
    )(mine, got)
    arrived = [
        lax.ppermute(x, "head", [(i, (i + 2 * hop) % groups) for i in range(groups)])
        for hop, x in enumerate(shares, 1)
    ]
    return on_device(
        finish_kernel,
        jax.ShapeDtypeStruct(residual.shape, residual.dtype),
        [pltpu.VMEM] * (chips + 1),
        16,
    )(total, *arrived, residual)


def body(
    queries,
    new_keys,
    new_values,
    cache_keys,
    cache_values,
    slopes,
    seg_blocks,
    request_row,
    out_weight,
    residual,
):
    heads = slopes.shape[0]
    width = queries.shape[2]
    hdim = width // heads
    peers = lax.axis_size("seq")
    groups = lax.axis_size("head")
    blocks = cache_keys.shape[0] // BLK
    vmem, smem, anywhere = pltpu.VMEM, pltpu.SMEM, pl.ANY
    own_query = queries.reshape(STEPS, width)

    copies = on_device(
        copies_kernel, jax.ShapeDtypeStruct((peers, STEPS, width), jnp.bfloat16), [vmem], 4
    )(own_query)
    everyone = lax.all_to_all(copies, "seq", 0, 0, tiled=True)

    table, lanes, own_stats, own_acc = on_device(
        functools.partial(own_kernel, blocks, heads),
        (
            jax.ShapeDtypeStruct((4, blocks), jnp.int32),
            jax.ShapeDtypeStruct((1, BLK), jnp.float32),
            jax.ShapeDtypeStruct((STEPS, STATS), jnp.float32),
            jax.ShapeDtypeStruct((STEPS, width), jnp.float32),
        ),
        [smem] * 3 + [vmem] * 3,
        4,
        out_specs=[pl.BlockSpec(memory_space=m) for m in (smem, vmem, vmem, vmem)],
    )(
        in_hbm(seg_blocks),
        in_hbm(request_row),
        in_hbm(slopes),
        in_hbm(own_query),
        in_hbm(new_keys.reshape(STEPS, width)),
        in_hbm(new_values.reshape(STEPS, width)),
    )

    ready = blocks - 1
    turned = out_weight.shape[::-1]
    staged, weight = on_device(
        stage_kernel,
        (pltpu.VMEM((ready * BLK, width), jnp.bfloat16), pltpu.HBM(turned, jnp.bfloat16)),
        [pltpu.HBM] * 2,
        4,
        out_specs=[pl.BlockSpec(memory_space=pl.ANY)] * 2,
        scratch_shapes=[
            pltpu.VMEM(turned, jnp.bfloat16),
            pltpu.SemaphoreType.DMA((ready,)),
            pltpu.SemaphoreType.DMA((2,)),
        ],
        cost_estimate=pl.CostEstimate(
            flops=0, bytes_accessed=4 * ready * BLK * width, transcendentals=0
        ),
    )(in_hbm(cache_keys), in_hbm(out_weight.T))
    partials, weight = on_device(
        functools.partial(attend_kernel, blocks, hdim),
        (
            jax.ShapeDtypeStruct((peers, STEPS, width + STATS), jnp.bfloat16),
            pltpu.HBM(turned, jnp.bfloat16),
        ),
        [smem, vmem, vmem, pl.ANY, vmem] + [pltpu.HBM] * 3,
        32,
        out_specs=(pl.BlockSpec(memory_space=vmem), pl.BlockSpec(memory_space=pl.ANY)),
        input_output_aliases={7: 1},
        scratch_shapes=[
            pltpu.VMEM(((blocks - ready) * BLK, width), jnp.bfloat16),
            pltpu.VMEM(cache_values.shape, jnp.bfloat16),
            pltpu.SemaphoreType.DMA((2, blocks)),
        ],
    )(
        table,
        lanes,
        everyone,
        own_stats,
        staged,
        in_hbm(cache_keys),
        in_hbm(cache_values),
        weight,
    )
    arrived = lax.all_to_all(partials, "seq", 0, 0, tiled=True)

    attended = on_device(
        functools.partial(join_kernel, heads, hdim),
        jax.ShapeDtypeStruct((peers, STEPS, width), jnp.bfloat16),
        [vmem] * 3,
        16,
    )(arrived.reshape(peers * STEPS, width + STATS), own_stats, own_acc)
    rows = lax.all_to_all(attended, "seq", 0, 0, tiled=True).reshape(peers * STEPS, width)

    return project_and_sum(rows, weight, residual, groups)


def solution(mesh):
    in_specs = (
        P(None, "seq", "head"),
        P(None, "seq", "head"),
        P(None, "seq", "head"),
        P("seq", "head"),
        P("seq", "head"),
        P("head"),
        P(),
        P(),
        P("head", "seq"),
        P(None, "head", "seq"),
    )
    out_specs = P(None, "head", "seq")
    return jax.shard_map(body, mesh=mesh, in_specs=in_specs, out_specs=out_specs, check_vma=False)
```

```python
import functools
import math

import jax
import jax.numpy as jnp
from jax import lax
from jax.experimental import pallas as pl
from jax.experimental.pallas import tpu as pltpu
from jax.sharding import PartitionSpec as P

BLK = 128
NEG = -1e30
STEPS = 2
GROUP = 16
ROWS = 8
STATS = 128
MIB = 1024 * 1024


def iota(shape, dim):
    return lax.broadcasted_iota(jnp.int32, shape, dim)


def head_mask(width, hdim):
    return iota((GROUP, width), 1) // hdim == iota((GROUP, width), 0)


def by_step(x, mask):
    rows = [
        jnp.sum(jnp.where(mask, x[s * GROUP : (s + 1) * GROUP], 0.0), axis=0, keepdims=True)
        for s in range(STEPS)
    ]
    return jnp.concatenate(rows, axis=0)


def in_bf16_parts(x, parts):
    out = []
    for _ in range(parts):
        part = x.astype(jnp.bfloat16).astype(jnp.float32)
        out.append(part)
        x = x - part
    return out


def left(x, lanes):
    return pltpu.roll(x, x.shape[1] - lanes, 1) if lanes else x


def stage_kernel(keys, weight, out, weight_out, wbuf, sems, weight_sems):
    weight_in = pltpu.make_async_copy(weight, wbuf, weight_sems.at[0])
    weight_back = pltpu.make_async_copy(wbuf, weight_out, weight_sems.at[1])
    weight_in.start()
    copies = []
    for b in range(sems.shape[0]):
        rows = pl.ds(b * BLK, BLK)
        copies.append(pltpu.make_async_copy(keys.at[rows], out.at[rows], sems.at[b]))
    for copy in copies:
        copy.start()
    weight_in.wait()
    weight_back.start()
    for copy in (*copies, weight_back):
        copy.wait()


def attend_kernel(
    blocks,
    hdim,
    meta,
    slopes,
    query,
    own_stats,
    staged,
    keys,
    values,
    weight,
    out,
    weight_out,
    kbuf,
    vbuf,
    sems,
):
    width = keys.shape[1]
    per = STEPS * GROUP
    packs = BLK // per
    scale = 1.0 / math.sqrt(hdim)
    ready = staged.shape[0] // BLK
    key_copies = {}
    for b in range(ready, blocks):
        rows = pl.ds((b - ready) * BLK, BLK)
        copy = pltpu.make_async_copy(keys.at[pl.ds(b * BLK, BLK)], kbuf.at[rows], sems.at[0, b])
        key_copies[b] = copy
    value_copies = []
    for b in range(blocks):
        rows = pl.ds(b * BLK, BLK)
        value_copies.append(pltpu.make_async_copy(values.at[rows], vbuf.at[rows], sems.at[1, b]))
    for copy in (*key_copies.values(), *value_copies):
        copy.start()
    mask = head_mask(width, hdim)
    lane = iota((STEPS, STATS), 1)
    empty = jnp.concatenate(
        [jnp.zeros((STEPS, width), jnp.float32), jnp.where(lane < GROUP, NEG, 0.0)], axis=1
    ).astype(out.dtype)
    for r in range(out.shape[0]):
        out[r] = empty

    raw = []
    for g in range(blocks // packs):
        spread = []
        for b in range(g * packs, (g + 1) * packs):
            q = query[meta[0, b]].astype(jnp.float32)
            for s in range(STEPS):
                spread.append(jnp.where(mask, q[s : s + 1], 0.0).astype(jnp.bfloat16))
        spread = jnp.concatenate(spread, axis=0)
        first, last = g * packs, (g + 1) * packs
        split = min(max(first, ready), last)
        pieces = []
        if split > first:
            pieces.append(staged[first * BLK : split * BLK])
        if last > split:
            for b in range(split, last):
                key_copies[b].wait()
            pieces.append(kbuf[(split - ready) * BLK : (last - ready) * BLK])
        tiles = [
            lax.dot_general(
                piece, spread, (((1,), (1,)), ((), ())), preferred_element_type=jnp.float32
            )
            for piece in pieces
        ]
        raw.append(tiles[0] if len(tiles) == 1 else jnp.concatenate(tiles, axis=0))

    pack = iota((BLK, BLK), 1) // per
    when = (iota((BLK, BLK), 1) % per) // GROUP - iota((BLK, BLK), 0)
    slope = slopes[...]
    joined = [meta[3, b] == 1 for b in range(blocks)]
    scores = []
    tops = []
    for g in range(blocks // packs):
        for k in range(packs):
            b = g * packs + k
            tile = raw[g][k * BLK : (k + 1) * BLK]
            base = meta[1, b]
            x = tile if k == 0 else jnp.where(pack == k, tile, x)
            dist = when + base if k == 0 else jnp.where(pack == k, when + base, dist)
        x = x * scale - slope * dist.astype(jnp.float32)
        scores.append(x)
        top = jnp.max(x, axis=0, keepdims=True)
        tops += [left(top, k * per) for k in range(packs)]
    for b in range(1, blocks):
        tops[b] = jnp.where(joined[b], jnp.maximum(tops[b], tops[b - 1]), tops[b])
    for b in range(blocks - 2, -1, -1):
        tops[b] = jnp.where(joined[b + 1], tops[b + 1], tops[b])

    row = iota((BLK, BLK), 0)
    source = row // per * per + row % STEPS * GROUP + row % per // STEPS
    swap = (source == iota((BLK, BLK), 1)).astype(jnp.bfloat16)
    place = iota((1, BLK), 1) // per
    totals = []
    weights = []
    for g in range(blocks // packs):
        top = tops[g * packs]
        for k in range(1, packs):
            top = jnp.where(place == k, pltpu.roll(tops[g * packs + k], k * per, 1), top)
        probs = jnp.exp(scores[g] - top)
        total = jnp.sum(probs, axis=0, keepdims=True)
        totals += [left(total, k * per) for k in range(packs)]
        weights.append(
            lax.dot_general(
                swap,
                probs.astype(jnp.bfloat16),
                (((1,), (1,)), ((), ())),
                preferred_element_type=jnp.float32,
            )
        )
    for b in range(1, blocks):
        totals[b] = totals[b] + jnp.where(joined[b], totals[b - 1], 0.0)

    parts = in_bf16_parts(jnp.concatenate(tops, axis=0), 3)
    parts += in_bf16_parts(jnp.concatenate(totals, axis=0), 2)
    field = iota((blocks, STATS), 1) // GROUP
    stats = []
    for s in range(STEPS):
        row = jnp.zeros((blocks, STATS), jnp.float32)
        for k, part in enumerate(parts):
            row = jnp.where(field == k, left(part, (s - k) * GROUP % STATS), row)
        stats.append(row)

    rows = []
    acc = None
    for b in range(blocks):
        k = b % packs
        value_copies[b].wait()
        mine = []
        for h in range(0, width // hdim, ROWS // STEPS):
            lanes = slice(h * hdim, min(h + ROWS // STEPS, width // hdim) * hdim)
            some = jnp.dot(
                weights[b // packs][k * per + STEPS * h :][:ROWS].astype(jnp.bfloat16),
                vbuf[b * BLK : (b + 1) * BLK, lanes],
                preferred_element_type=jnp.float32,
            )
            for i in range(some.shape[1] // hdim):
                mine.append(some[STEPS * i : STEPS * (i + 1), i * hdim : (i + 1) * hdim])
        mine = jnp.concatenate(mine, axis=1)
        acc = mine if acc is None else mine + jnp.where(joined[b], acc, 0.0)
        tail = jnp.concatenate([x[b : b + 1] for x in stats], axis=0)
        row = jnp.concatenate([acc, tail], axis=1).astype(out.dtype)
        rows.append(jnp.where(meta[2, b] == 1, row, empty))
    for b in range(blocks):
        out[meta[0, b]] = rows[b]


def own_terms(heads, hdim, query, key, value, slopes):
    scale = 1.0 / math.sqrt(hdim)
    q = query[...].astype(jnp.float32)
    k = key[...].astype(jnp.float32)
    v = value[...].astype(jnp.float32)
    q0, q1 = q[0:1], q[1:2]
    k0, k1 = k[0:1], k[1:2]
    v0, v1 = v[0:1], v[1:2]
    lane = iota((1, STATS), 1)
    tops = [jnp.zeros((1, STATS), jnp.float32) for _ in range(STEPS)]
    sums = [jnp.zeros((1, STATS), jnp.float32) for _ in range(STEPS)]
    rows = [[], []]
    products = jnp.concatenate([q0 * k0, q1 * k0, q1 * k1], axis=0)
    for h in range(heads):
        at = slice(h * hdim, (h + 1) * hdim)
        dots = jnp.sum(products[:, at], axis=1, keepdims=True) * scale
        first = dots[0:1]
        cross = dots[1:2] - slopes[h]
        second = dots[2:3]
        upper = jnp.maximum(cross, second)
        e_cross = jnp.exp(cross - upper)
        e_second = jnp.exp(second - upper)
        tops[0] = jnp.where(lane == h, first, tops[0])
        tops[1] = jnp.where(lane == h, upper, tops[1])
        sums[0] = jnp.where(lane == h + GROUP, 1.0, sums[0])
        sums[1] = jnp.where(lane == h + GROUP, e_cross + e_second, sums[1])
        rows[0].append(v0[:, at])
        rows[1].append(e_cross * v0[:, at] + e_second * v1[:, at])
    stats = jnp.concatenate([tops[0] + sums[0], tops[1] + sums[1]], axis=0)
    return stats, jnp.concatenate([jnp.concatenate(r, axis=1) for r in rows], axis=0)


def block_table(blocks, seg_blocks, request_row):
    requests = seg_blocks.shape[0]
    index = lax.axis_index("seq") * blocks

    def skip(i, carry):
        request, end, total = carry
        total = total + seg_blocks[i]
        passed = total <= index
        return request + passed.astype(jnp.int32), jnp.where(passed, total, end), total

    zero = jnp.int32(0)
    request, end, _ = lax.fori_loop(0, requests, skip, (zero, zero, zero))
    last = requests - 1
    end = end + seg_blocks[jnp.minimum(request, last)]
    table = []
    for b in range(blocks):
        joined = jnp.bool_(False)
        if b:
            joined = index + b < end
            request = jnp.where(joined, request, request + 1)
            end = jnp.where(joined, end, end + seg_blocks[jnp.minimum(request, last)])
        live = request <= last
        row = request_row[jnp.minimum(request, last)]
        table.append((row, (end - index - b) * BLK, live, joined & live))
    return table


def own_kernel(
    blocks,
    heads,
    seg_blocks,
    request_row,
    slopes,
    query,
    key,
    value,
    table,
    lanes,
    stats,
    acc,
):
    for b, entry in enumerate(block_table(blocks, seg_blocks, request_row)):
        for i, x in enumerate(entry):
            table[i, b] = x.astype(jnp.int32)
    slope = jnp.zeros((1, BLK), jnp.float32)
    for h in range(heads):
        slope = jnp.where(iota((1, BLK), 1) % GROUP == h, slopes[h], slope)
    lanes[...] = slope
    stats[...], acc[...] = own_terms(heads, query.shape[1] // heads, query, key, value, slopes)


def join_kernel(heads, hdim, parts, own_stats, own_acc, out):
    width = heads * hdim
    count = parts.shape[0]
    stats = parts[:, width : width + STATS].astype(jnp.float32)
    top = (stats + left(stats, GROUP)) + left(stats, 2 * GROUP)
    total = left(stats, 3 * GROUP) + left(stats, 4 * GROUP)
    step = iota((count, STATS), 0) % STEPS
    lane = iota((count, STATS), 1)
    real = lane < heads
    top = jnp.where(real, top, NEG)
    total = jnp.where(real, total, 0.0)
    own = own_stats[...]
    own_real = iota(own.shape, 1) < heads
    own_top = jnp.where(own_real, own, 0.0)
    own_total = jnp.where(own_real, left(own, GROUP), 1.0)
    highest = [
        jnp.maximum(
            jnp.max(jnp.where(step == s, top, NEG), axis=0, keepdims=True), own_top[s : s + 1]
        )
        for s in range(STEPS)
    ]
    weight = jnp.exp(top - jnp.where(step == 0, highest[0], highest[1]))
    weight = jnp.where(real, weight, 0.0)
    own_weight = jnp.exp(own_top - jnp.concatenate(highest, axis=0))
    weighted = weight * total
    sums = [
        jnp.sum(jnp.where(step == s, weighted, 0.0), axis=0, keepdims=True) for s in range(STEPS)
    ]
    inverse = 1.0 / (jnp.concatenate(sums, axis=0) + own_weight * own_total)
    own_weight = own_weight * inverse
    weight = weight * jnp.where(step == 0, inverse[0:1], inverse[1:2])
    placed = jnp.where(step == 0, weight, 0.0) + pltpu.roll(
        jnp.where(step == 1, weight, 0.0), GROUP, 1
    )
    high, low = in_bf16_parts(placed, 2)
    both = high + pltpu.roll(low, STEPS * GROUP, 1)
    both = both.T[: 2 * STEPS * GROUP].astype(jnp.bfloat16)
    full = jnp.dot(both, parts[:, :width], preferred_element_type=jnp.float32)
    full = full[: STEPS * GROUP] + full[STEPS * GROUP :]
    acc = by_step(full, head_mask(width, hdim))
    mine = own_acc[...]
    mine = jnp.concatenate(
        [mine[:, h * hdim : (h + 1) * hdim] * own_weight[:, h : h + 1] for h in range(heads)],
        axis=1,
    )
    attended = (acc + mine).astype(out.dtype)
    for r in range(out.shape[0]):
        out[r] = attended


def project_kernel(rows, weight, mine, theirs):
    full = lax.dot_general(
        rows[...], weight[...], (((1,), (1,)), ((), ())), preferred_element_type=jnp.float32
    )
    first = lax.axis_index("head") % 2 == 0
    chips, size = mine.shape[0], mine.shape[1]
    for c in range(chips):
        a = full[2 * c * size : (2 * c + 1) * size]
        b = full[(2 * c + 1) * size : (2 * c + 2) * size]
        mine[c] = jnp.where(first, a, b)
        theirs[c] = jnp.where(first, b, a).astype(theirs.dtype)


def hops(chips):
    return sorted(range(1, chips), key=lambda hop: -min(hop, chips - hop))


def pair_kernel(mine, got, total, *rest):
    shares, both = rest[:-1], rest[-1]
    chips = mine.shape[0]
    chip = lax.axis_index("head") // 2
    for c in range(chips):
        both[c] = mine[c] + got[c].astype(jnp.float32)
    total[...] = both[chip]
    for hop, share in zip(hops(chips), shares):
        share[...] = both[lax.rem(chip + hop, chips)].astype(share.dtype)


def finish_kernel(total, *rest):
    shares, residual, out = rest[:-2], rest[-2], rest[-1]
    x = total[...]
    for share in shares:
        x = x + share[...].astype(jnp.float32)
    for s in range(STEPS):
        rows = [x[r : r + 1] for r in range(s, x.shape[0], STEPS)]
        y = residual[s].astype(jnp.float32) + jnp.concatenate(rows, axis=0)
        out[s] = y.astype(out.dtype)


def copies_kernel(x, out, buffer, sems):
    size = buffer.shape[0]
    for r in range(size):
        buffer[r] = x[...]
    copies = [
        pltpu.make_async_copy(buffer, out.at[pl.ds(i * size, size)], sems.at[i])
        for i in range(out.shape[0] // size)
    ]
    for copy in copies:
        copy.start()
    for copy in copies:
        copy.wait()


def in_hbm(x):
    return pltpu.with_memory_space_constraint(x, pltpu.HBM)


def on_device(kernel, out_shape, in_spaces, limit, **more):
    return pl.pallas_call(
        kernel,
        out_shape=out_shape,
        in_specs=[pl.BlockSpec(memory_space=m) for m in in_spaces],
        compiler_params=pltpu.CompilerParams(vmem_limit_bytes=limit * MIB),
        **more,
    )


def project_and_sum(rows, weight, residual, groups):
    chips = groups // 2
    size, columns = rows.shape[0] // groups, weight.shape[0]
    each = (chips, size, columns)
    mine, theirs = on_device(
        project_kernel,
        (jax.ShapeDtypeStruct(each, jnp.float32), jax.ShapeDtypeStruct(each, jnp.bfloat16)),
        [pltpu.VMEM] * 2,
        16,
    )(rows, weight)
    got = lax.ppermute(theirs, "head", [(i, i ^ 1) for i in range(groups)])
    share = jax.ShapeDtypeStruct((size, columns), jnp.bfloat16)
    total, *shares = on_device(
        pair_kernel,
        (jax.ShapeDtypeStruct((size, columns), jnp.float32), *[share] * (chips - 1)),
        [pltpu.VMEM] * 2,
        16,
        scratch_shapes=[pltpu.VMEM(each, jnp.float32)],
    )(mine, got)
    arrived = [
        lax.ppermute(x, "head", [(i, (i + 2 * hop) % groups) for i in range(groups)])
        for hop, x in zip(hops(chips), shares)
    ]
    return on_device(
        finish_kernel,
        jax.ShapeDtypeStruct(residual.shape, residual.dtype),
        [pltpu.VMEM] * (chips + 1),
        16,
    )(total, *arrived, residual)


def body(
    queries,
    new_keys,
    new_values,
    cache_keys,
    cache_values,
    slopes,
    seg_blocks,
    request_row,
    out_weight,
    residual,
):
    heads = slopes.shape[0]
    width = queries.shape[2]
    hdim = width // heads
    peers = lax.axis_size("seq")
    groups = lax.axis_size("head")
    blocks = cache_keys.shape[0] // BLK
    vmem, smem, anywhere = pltpu.VMEM, pltpu.SMEM, pl.ANY
    own_query = queries.reshape(STEPS, width)

    pieces = 8
    copies = on_device(
        copies_kernel,
        jax.ShapeDtypeStruct((peers, STEPS, width), jnp.bfloat16),
        [vmem],
        4,
        out_specs=pl.BlockSpec(memory_space=pl.ANY),
        scratch_shapes=[
            pltpu.VMEM((peers // pieces, STEPS, width), jnp.bfloat16),
            pltpu.SemaphoreType.DMA((pieces,)),
        ],
    )(own_query)
    everyone = lax.all_to_all(copies, "seq", 0, 0, tiled=True)

    table, lanes, own_stats, own_acc = on_device(
        functools.partial(own_kernel, blocks, heads),
        (
            jax.ShapeDtypeStruct((4, blocks), jnp.int32),
            jax.ShapeDtypeStruct((1, BLK), jnp.float32),
            jax.ShapeDtypeStruct((STEPS, STATS), jnp.float32),
            jax.ShapeDtypeStruct((STEPS, width), jnp.float32),
        ),
        [smem] * 3 + [vmem] * 3,
        4,
        out_specs=[pl.BlockSpec(memory_space=m) for m in (smem, vmem, vmem, vmem)],
    )(
        in_hbm(seg_blocks),
        in_hbm(request_row),
        in_hbm(slopes),
        in_hbm(own_query),
        in_hbm(new_keys.reshape(STEPS, width)),
        in_hbm(new_values.reshape(STEPS, width)),
    )

    ready = blocks - 1
    turned = out_weight.shape[::-1]
    staged, weight = on_device(
        stage_kernel,
        (pltpu.VMEM((ready * BLK, width), jnp.bfloat16), pltpu.HBM(turned, jnp.bfloat16)),
        [pltpu.HBM] * 2,
        4,
        out_specs=[pl.BlockSpec(memory_space=pl.ANY)] * 2,
        scratch_shapes=[
            pltpu.VMEM(turned, jnp.bfloat16),
            pltpu.SemaphoreType.DMA((ready,)),
            pltpu.SemaphoreType.DMA((2,)),
        ],
        cost_estimate=pl.CostEstimate(
            flops=0, bytes_accessed=4 * ready * BLK * width, transcendentals=0
        ),
    )(in_hbm(cache_keys), in_hbm(out_weight.T))
    partials, weight = on_device(
        functools.partial(attend_kernel, blocks, hdim),
        (
            jax.ShapeDtypeStruct((peers, STEPS, width + STATS), jnp.bfloat16),
            pltpu.HBM(turned, jnp.bfloat16),
        ),
        [smem, vmem, vmem, pl.ANY, vmem] + [pltpu.HBM] * 3,
        32,
        out_specs=(pl.BlockSpec(memory_space=vmem), pl.BlockSpec(memory_space=pl.ANY)),
        input_output_aliases={7: 1},
        scratch_shapes=[
            pltpu.VMEM(((blocks - ready) * BLK, width), jnp.bfloat16),
            pltpu.VMEM(cache_values.shape, jnp.bfloat16),
            pltpu.SemaphoreType.DMA((2, blocks)),
        ],
    )(
        table,
        lanes,
        everyone,
        own_stats,
        staged,
        in_hbm(cache_keys),
        in_hbm(cache_values),
        weight,
    )
    arrived = lax.all_to_all(partials, "seq", 0, 0, tiled=True)

    attended = on_device(
        functools.partial(join_kernel, heads, hdim),
        jax.ShapeDtypeStruct((peers, STEPS, width), jnp.bfloat16),
        [vmem] * 3,
        16,
    )(arrived.reshape(peers * STEPS, width + STATS), own_stats, own_acc)
    rows = lax.all_to_all(attended, "seq", 0, 0, tiled=True).reshape(peers * STEPS, width)

    return project_and_sum(rows, weight, residual, groups)


def solution(mesh):
    in_specs = (
        P(None, "seq", "head"),
        P(None, "seq", "head"),
        P(None, "seq", "head"),
        P("seq", "head"),
        P("seq", "head"),
        P("head"),
        P(),
        P(),
        P("head", "seq"),
        P(None, "head", "seq"),
    )
    out_specs = P(None, "head", "seq")
    return jax.shard_map(body, mesh=mesh, in_specs=in_specs, out_specs=out_specs, check_vma=False)
```

```python
import functools
import math

import jax
import jax.numpy as jnp
from jax import lax
from jax.experimental import pallas as pl
from jax.experimental.pallas import tpu as pltpu
from jax.sharding import PartitionSpec as P

BLK = 128
NEG = -1e30
STEPS = 2
GROUP = 16
ROWS = 8
STATS = 128
MIB = 1024 * 1024


def iota(shape, dim):
    return lax.broadcasted_iota(jnp.int32, shape, dim)


def head_mask(width, hdim):
    return iota((GROUP, width), 1) // hdim == iota((GROUP, width), 0)


def by_step(x, mask):
    rows = [
        jnp.sum(jnp.where(mask, x[s * GROUP : (s + 1) * GROUP], 0.0), axis=0, keepdims=True)
        for s in range(STEPS)
    ]
    return jnp.concatenate(rows, axis=0)


def in_bf16_parts(x, parts):
    out = []
    for _ in range(parts):
        part = x.astype(jnp.bfloat16).astype(jnp.float32)
        out.append(part)
        x = x - part
    return out


def left(x, lanes):
    return pltpu.roll(x, x.shape[1] - lanes, 1) if lanes else x


def stage_kernel(keys, weight, out, weight_out, wbuf, sems, weight_sems):
    weight_in = pltpu.make_async_copy(weight, wbuf, weight_sems.at[0])
    weight_back = pltpu.make_async_copy(wbuf, weight_out, weight_sems.at[1])
    weight_in.start()
    copies = []
    for b in range(sems.shape[0]):
        rows = pl.ds(b * BLK, BLK)
        copies.append(pltpu.make_async_copy(keys.at[rows], out.at[rows], sems.at[b]))
    for copy in copies:
        copy.start()
    weight_in.wait()
    weight_back.start()
    for copy in (*copies, weight_back):
        copy.wait()


def attend_kernel(
    blocks,
    hdim,
    meta,
    slopes,
    query,
    own_stats,
    staged,
    keys,
    values,
    weight,
    out,
    weight_out,
    kbuf,
    vbuf,
    sems,
):
    width = keys.shape[1]
    per = STEPS * GROUP
    packs = BLK // per
    scale = 1.0 / math.sqrt(hdim)
    ready = staged.shape[0] // BLK
    key_copies = {}
    for b in range(ready, blocks):
        rows = pl.ds((b - ready) * BLK, BLK)
        copy = pltpu.make_async_copy(keys.at[pl.ds(b * BLK, BLK)], kbuf.at[rows], sems.at[0, b])
        key_copies[b] = copy
    value_copies = []
    for b in range(blocks):
        rows = pl.ds(b * BLK, BLK)
        value_copies.append(pltpu.make_async_copy(values.at[rows], vbuf.at[rows], sems.at[1, b]))
    for copy in (*key_copies.values(), *value_copies):
        copy.start()
    mask = head_mask(width, hdim)
    lane = iota((STEPS, STATS), 1)
    empty = jnp.concatenate(
        [jnp.zeros((STEPS, width), jnp.float32), jnp.where(lane < GROUP, NEG, 0.0)], axis=1
    ).astype(out.dtype)
    for r in range(out.shape[0]):
        out[r] = empty

    raw = []
    for g in range(blocks // packs):
        spread = []
        for b in range(g * packs, (g + 1) * packs):
            q = query[meta[0, b]].astype(jnp.float32)
            for s in range(STEPS):
                spread.append(jnp.where(mask, q[s : s + 1], 0.0).astype(jnp.bfloat16))
        spread = jnp.concatenate(spread, axis=0)
        first, last = g * packs, (g + 1) * packs
        split = min(max(first, ready), last)
        pieces = []
        if split > first:
            pieces.append(staged[first * BLK : split * BLK])
        if last > split:
            for b in range(split, last):
                key_copies[b].wait()
            pieces.append(kbuf[(split - ready) * BLK : (last - ready) * BLK])
        tiles = [
            lax.dot_general(
                piece, spread, (((1,), (1,)), ((), ())), preferred_element_type=jnp.float32
            )
            for piece in pieces
        ]
        raw.append(tiles[0] if len(tiles) == 1 else jnp.concatenate(tiles, axis=0))

    pack = iota((BLK, BLK), 1) // per
    when = (iota((BLK, BLK), 1) % per) // GROUP - iota((BLK, BLK), 0)
    slope = slopes[...]
    joined = [meta[3, b] == 1 for b in range(blocks)]
    scores = []
    tops = []
    for g in range(blocks // packs):
        for k in range(packs):
            b = g * packs + k
            tile = raw[g][k * BLK : (k + 1) * BLK]
            base = meta[1, b]
            x = tile if k == 0 else jnp.where(pack == k, tile, x)
            dist = when + base if k == 0 else jnp.where(pack == k, when + base, dist)
        x = x * scale - slope * dist.astype(jnp.float32)
        scores.append(x)
        top = jnp.max(x, axis=0, keepdims=True)
        tops += [left(top, k * per) for k in range(packs)]
    for b in range(1, blocks):
        tops[b] = jnp.where(joined[b], jnp.maximum(tops[b], tops[b - 1]), tops[b])
    for b in range(blocks - 2, -1, -1):
        tops[b] = jnp.where(joined[b + 1], tops[b + 1], tops[b])

    row = iota((BLK, BLK), 0)
    source = row // per * per + row % STEPS * GROUP + row % per // STEPS
    swap = (source == iota((BLK, BLK), 1)).astype(jnp.bfloat16)
    place = iota((1, BLK), 1) // per
    totals = []
    weights = []
    for g in range(blocks // packs):
        top = tops[g * packs]
        for k in range(1, packs):
            top = jnp.where(place == k, pltpu.roll(tops[g * packs + k], k * per, 1), top)
        probs = jnp.exp(scores[g] - top)
        total = jnp.sum(probs, axis=0, keepdims=True)
        totals += [left(total, k * per) for k in range(packs)]
        weights.append(
            lax.dot_general(
                swap,
                probs.astype(jnp.bfloat16),
                (((1,), (1,)), ((), ())),
                preferred_element_type=jnp.float32,
            )
        )
    for b in range(1, blocks):
        totals[b] = totals[b] + jnp.where(joined[b], totals[b - 1], 0.0)

    parts = in_bf16_parts(jnp.concatenate(tops, axis=0), 3)
    parts += in_bf16_parts(jnp.concatenate(totals, axis=0), 2)
    field = iota((blocks, STATS), 1) // GROUP
    stats = []
    for s in range(STEPS):
        row = jnp.zeros((blocks, STATS), jnp.float32)
        for k, part in enumerate(parts):
            row = jnp.where(field == k, left(part, (s - k) * GROUP % STATS), row)
        stats.append(row)

    rows = []
    acc = None
    for b in range(blocks):
        k = b % packs
        value_copies[b].wait()
        mine = []
        for h in range(0, width // hdim, ROWS // STEPS):
            lanes = slice(h * hdim, min(h + ROWS // STEPS, width // hdim) * hdim)
            some = jnp.dot(
                weights[b // packs][k * per + STEPS * h :][:ROWS].astype(jnp.bfloat16),
                vbuf[b * BLK : (b + 1) * BLK, lanes],
                preferred_element_type=jnp.float32,
            )
            for i in range(some.shape[1] // hdim):
                mine.append(some[STEPS * i : STEPS * (i + 1), i * hdim : (i + 1) * hdim])
        mine = jnp.concatenate(mine, axis=1)
        acc = mine if acc is None else mine + jnp.where(joined[b], acc, 0.0)
        tail = jnp.concatenate([x[b : b + 1] for x in stats], axis=0)
        row = jnp.concatenate([acc, tail], axis=1).astype(out.dtype)
        rows.append(jnp.where(meta[2, b] == 1, row, empty))
    for b in range(blocks):
        out[meta[0, b]] = rows[b]


def own_terms(heads, hdim, query, key, value, slopes):
    scale = 1.0 / math.sqrt(hdim)
    q = query[...].astype(jnp.float32)
    k = key[...].astype(jnp.float32)
    v = value[...].astype(jnp.float32)
    q0, q1 = q[0:1], q[1:2]
    k0, k1 = k[0:1], k[1:2]
    v0, v1 = v[0:1], v[1:2]
    lane = iota((1, STATS), 1)
    tops = [jnp.zeros((1, STATS), jnp.float32) for _ in range(STEPS)]
    sums = [jnp.zeros((1, STATS), jnp.float32) for _ in range(STEPS)]
    rows = [[], []]
    products = jnp.concatenate([q0 * k0, q1 * k0, q1 * k1], axis=0)
    for h in range(heads):
        at = slice(h * hdim, (h + 1) * hdim)
        dots = jnp.sum(products[:, at], axis=1, keepdims=True) * scale
        first = dots[0:1]
        cross = dots[1:2] - slopes[h]
        second = dots[2:3]
        upper = jnp.maximum(cross, second)
        e_cross = jnp.exp(cross - upper)
        e_second = jnp.exp(second - upper)
        tops[0] = jnp.where(lane == h, first, tops[0])
        tops[1] = jnp.where(lane == h, upper, tops[1])
        sums[0] = jnp.where(lane == h + GROUP, 1.0, sums[0])
        sums[1] = jnp.where(lane == h + GROUP, e_cross + e_second, sums[1])
        rows[0].append(v0[:, at])
        rows[1].append(e_cross * v0[:, at] + e_second * v1[:, at])
    stats = jnp.concatenate([tops[0] + sums[0], tops[1] + sums[1]], axis=0)
    return stats, jnp.concatenate([jnp.concatenate(r, axis=1) for r in rows], axis=0)


def block_table(blocks, seg_blocks, request_row):
    requests = seg_blocks.shape[0]
    index = lax.axis_index("seq") * blocks

    def skip(i, carry):
        request, end, total = carry
        total = total + seg_blocks[i]
        passed = total <= index
        return request + passed.astype(jnp.int32), jnp.where(passed, total, end), total

    zero = jnp.int32(0)
    request, end, _ = lax.fori_loop(0, requests, skip, (zero, zero, zero))
    last = requests - 1
    end = end + seg_blocks[jnp.minimum(request, last)]
    table = []
    for b in range(blocks):
        joined = jnp.bool_(False)
        if b:
            joined = index + b < end
            request = jnp.where(joined, request, request + 1)
            end = jnp.where(joined, end, end + seg_blocks[jnp.minimum(request, last)])
        live = request <= last
        row = request_row[jnp.minimum(request, last)]
        table.append((row, (end - index - b) * BLK, live, joined & live))
    return table


def own_kernel(
    blocks,
    heads,
    seg_blocks,
    request_row,
    slopes,
    query,
    key,
    value,
    table,
    lanes,
    stats,
    acc,
):
    for b, entry in enumerate(block_table(blocks, seg_blocks, request_row)):
        for i, x in enumerate(entry):
            table[i, b] = x.astype(jnp.int32)
    slope = jnp.zeros((1, BLK), jnp.float32)
    for h in range(heads):
        slope = jnp.where(iota((1, BLK), 1) % GROUP == h, slopes[h], slope)
    lanes[...] = slope
    stats[...], acc[...] = own_terms(heads, query.shape[1] // heads, query, key, value, slopes)


def join_kernel(heads, hdim, parts, own_stats, own_acc, out):
    width = heads * hdim
    count = parts.shape[0]
    stats = parts[:, width : width + STATS].astype(jnp.float32)
    top = (stats + left(stats, GROUP)) + left(stats, 2 * GROUP)
    total = left(stats, 3 * GROUP) + left(stats, 4 * GROUP)
    step = iota((count, STATS), 0) % STEPS
    lane = iota((count, STATS), 1)
    real = lane < heads
    top = jnp.where(real, top, NEG)
    total = jnp.where(real, total, 0.0)
    own = own_stats[...]
    own_real = iota(own.shape, 1) < heads
    own_top = jnp.where(own_real, own, 0.0)
    own_total = jnp.where(own_real, left(own, GROUP), 1.0)
    highest = [
        jnp.maximum(
            jnp.max(jnp.where(step == s, top, NEG), axis=0, keepdims=True), own_top[s : s + 1]
        )
        for s in range(STEPS)
    ]
    weight = jnp.exp(top - jnp.where(step == 0, highest[0], highest[1]))
    weight = jnp.where(real, weight, 0.0)
    own_weight = jnp.exp(own_top - jnp.concatenate(highest, axis=0))
    weighted = weight * total
    sums = [
        jnp.sum(jnp.where(step == s, weighted, 0.0), axis=0, keepdims=True) for s in range(STEPS)
    ]
    inverse = 1.0 / (jnp.concatenate(sums, axis=0) + own_weight * own_total)
    own_weight = own_weight * inverse
    weight = weight * jnp.where(step == 0, inverse[0:1], inverse[1:2])
    placed = jnp.where(step == 0, weight, 0.0) + pltpu.roll(
        jnp.where(step == 1, weight, 0.0), GROUP, 1
    )
    high, low = in_bf16_parts(placed, 2)
    both = high + pltpu.roll(low, STEPS * GROUP, 1)
    both = both.T[: 2 * STEPS * GROUP].astype(jnp.bfloat16)
    full = jnp.dot(both, parts[:, :width], preferred_element_type=jnp.float32)
    full = full[: STEPS * GROUP] + full[STEPS * GROUP :]
    acc = by_step(full, head_mask(width, hdim))
    mine = own_acc[...]
    mine = jnp.concatenate(
        [mine[:, h * hdim : (h + 1) * hdim] * own_weight[:, h : h + 1] for h in range(heads)],
        axis=1,
    )
    attended = (acc + mine).astype(out.dtype)
    for r in range(out.shape[0]):
        out[r] = attended


def project_kernel(rows, weight, mine, theirs):
    full = lax.dot_general(
        rows[...], weight[...], (((1,), (1,)), ((), ())), preferred_element_type=jnp.float32
    )
    first = lax.axis_index("head") % 2 == 0
    chips, size = mine.shape[0], mine.shape[1]
    for c in range(chips):
        a = full[2 * c * size : (2 * c + 1) * size]
        b = full[(2 * c + 1) * size : (2 * c + 2) * size]
        mine[c] = jnp.where(first, a, b)
        theirs[c] = jnp.where(first, b, a).astype(theirs.dtype)


def pair_kernel(mine, got, keep, send, both):
    chip = lax.axis_index("head") // 2
    for c in range(mine.shape[0]):
        both[c] = mine[c] + got[c].astype(jnp.float32)
    for i, other in enumerate((0, 3)):
        keep[i] = both[chip ^ other]
        send[i] = both[chip ^ other ^ 1].astype(send.dtype)


def half_kernel(keep, got, total, send):
    total[...] = keep[0] + got[0].astype(jnp.float32)
    send[...] = (keep[1] + got[1].astype(jnp.float32)).astype(send.dtype)


def finish_kernel(total, got, residual, out):
    x = total[...] + got[...].astype(jnp.float32)
    for s in range(STEPS):
        rows = [x[r : r + 1] for r in range(s, x.shape[0], STEPS)]
        y = residual[s].astype(jnp.float32) + jnp.concatenate(rows, axis=0)
        out[s] = y.astype(out.dtype)


def copies_kernel(x, out):
    for r in range(out.shape[0]):
        out[r] = x[...]


def in_hbm(x):
    return pltpu.with_memory_space_constraint(x, pltpu.HBM)


def on_device(kernel, out_shape, in_spaces, limit, **more):
    return pl.pallas_call(
        kernel,
        out_shape=out_shape,
        in_specs=[pl.BlockSpec(memory_space=m) for m in in_spaces],
        compiler_params=pltpu.CompilerParams(vmem_limit_bytes=limit * MIB),
        **more,
    )


def project_and_sum(rows, weight, residual, groups):
    chips = groups // 2
    size, columns = rows.shape[0] // groups, weight.shape[0]
    each = (chips, size, columns)
    mine, theirs = on_device(
        project_kernel,
        (jax.ShapeDtypeStruct(each, jnp.float32), jax.ShapeDtypeStruct(each, jnp.bfloat16)),
        [pltpu.VMEM] * 2,
        16,
    )(rows, weight)
    got = lax.ppermute(theirs, "head", [(i, i ^ 1) for i in range(groups)])
    half = (2, size, columns)
    keep, send = on_device(
        pair_kernel,
        (jax.ShapeDtypeStruct(half, jnp.float32), jax.ShapeDtypeStruct(half, jnp.bfloat16)),
        [pltpu.VMEM] * 2,
        16,
        scratch_shapes=[pltpu.VMEM(each, jnp.float32)],
    )(mine, got)
    got = lax.ppermute(send, "head", [(i, i ^ 2) for i in range(groups)])
    total, send = on_device(
        half_kernel,
        (
            jax.ShapeDtypeStruct(half[1:], jnp.float32),
            jax.ShapeDtypeStruct(half[1:], jnp.bfloat16),
        ),
        [pltpu.VMEM] * 2,
        16,
    )(keep, got)
    got = lax.ppermute(send, "head", [(i, i ^ 6) for i in range(groups)])
    return on_device(
        finish_kernel,
        jax.ShapeDtypeStruct(residual.shape, residual.dtype),
        [pltpu.VMEM] * 3,
        16,
    )(total, got, residual)


def body(
    queries,
    new_keys,
    new_values,
    cache_keys,
    cache_values,
    slopes,
    seg_blocks,
    request_row,
    out_weight,
    residual,
):
    heads = slopes.shape[0]
    width = queries.shape[2]
    hdim = width // heads
    peers = lax.axis_size("seq")
    groups = lax.axis_size("head")
    blocks = cache_keys.shape[0] // BLK
    vmem, smem, anywhere = pltpu.VMEM, pltpu.SMEM, pl.ANY
    own_query = queries.reshape(STEPS, width)

    copies = on_device(
        copies_kernel, jax.ShapeDtypeStruct((peers, STEPS, width), jnp.bfloat16), [vmem], 4
    )(own_query)
    everyone = lax.all_to_all(copies, "seq", 0, 0, tiled=True)

    table, lanes, own_stats, own_acc = on_device(
        functools.partial(own_kernel, blocks, heads),
        (
            jax.ShapeDtypeStruct((4, blocks), jnp.int32),
            jax.ShapeDtypeStruct((1, BLK), jnp.float32),
            jax.ShapeDtypeStruct((STEPS, STATS), jnp.float32),
            jax.ShapeDtypeStruct((STEPS, width), jnp.float32),
        ),
        [smem] * 3 + [vmem] * 3,
        4,
        out_specs=[pl.BlockSpec(memory_space=m) for m in (smem, vmem, vmem, vmem)],
    )(
        in_hbm(seg_blocks),
        in_hbm(request_row),
        in_hbm(slopes),
        in_hbm(own_query),
        in_hbm(new_keys.reshape(STEPS, width)),
        in_hbm(new_values.reshape(STEPS, width)),
    )

    ready = blocks - 1
    turned = out_weight.shape[::-1]
    staged, weight = on_device(
        stage_kernel,
        (pltpu.VMEM((ready * BLK, width), jnp.bfloat16), pltpu.HBM(turned, jnp.bfloat16)),
        [pltpu.HBM] * 2,
        4,
        out_specs=[pl.BlockSpec(memory_space=pl.ANY)] * 2,
        scratch_shapes=[
            pltpu.VMEM(turned, jnp.bfloat16),
            pltpu.SemaphoreType.DMA((ready,)),
            pltpu.SemaphoreType.DMA((2,)),
        ],
        cost_estimate=pl.CostEstimate(
            flops=0, bytes_accessed=4 * ready * BLK * width, transcendentals=0
        ),
    )(in_hbm(cache_keys), in_hbm(out_weight.T))
    partials, weight = on_device(
        functools.partial(attend_kernel, blocks, hdim),
        (
            jax.ShapeDtypeStruct((peers, STEPS, width + STATS), jnp.bfloat16),
            pltpu.HBM(turned, jnp.bfloat16),
        ),
        [smem, vmem, vmem, pl.ANY, vmem] + [pltpu.HBM] * 3,
        32,
        out_specs=(pl.BlockSpec(memory_space=vmem), pl.BlockSpec(memory_space=pl.ANY)),
        input_output_aliases={7: 1},
        scratch_shapes=[
            pltpu.VMEM(((blocks - ready) * BLK, width), jnp.bfloat16),
            pltpu.VMEM(cache_values.shape, jnp.bfloat16),
            pltpu.SemaphoreType.DMA((2, blocks)),
        ],
    )(
        table,
        lanes,
        everyone,
        own_stats,
        staged,
        in_hbm(cache_keys),
        in_hbm(cache_values),
        weight,
    )
    arrived = lax.all_to_all(partials, "seq", 0, 0, tiled=True)

    attended = on_device(
        functools.partial(join_kernel, heads, hdim),
        jax.ShapeDtypeStruct((peers, STEPS, width), jnp.bfloat16),
        [vmem] * 3,
        16,
    )(arrived.reshape(peers * STEPS, width + STATS), own_stats, own_acc)
    rows = lax.all_to_all(attended, "seq", 0, 0, tiled=True).reshape(peers * STEPS, width)

    return project_and_sum(rows, weight, residual, groups)


def solution(mesh):
    in_specs = (
        P(None, "seq", "head"),
        P(None, "seq", "head"),
        P(None, "seq", "head"),
        P("seq", "head"),
        P("seq", "head"),
        P("head"),
        P(),
        P(),
        P("head", "seq"),
        P(None, "head", "seq"),
    )
    out_specs = P(None, "head", "seq")
    return jax.shard_map(body, mesh=mesh, in_specs=in_specs, out_specs=out_specs, check_vma=False)
```
